128 devices in a mesh: shard: 16 (over y_hi, x, core), context: 2 (over y_lo), tensor: 4 (over z).
Axes of the slice: x: 4, y: 4 (y_hi: 2, y_lo: 2; y = y_hi * 2 + y_lo), z: 4, core: 2. Of those that a mesh axis runs over, the one named last changes fastest.
Arguments:
- tokens: bfloat16 [32768, 1024], P(('shard', 'context')), may hold values from -6 to 6
- segment: int32 [32768], P(('shard', 'context')), may hold values from 0 to 64, as said below
- norm_gain: bfloat16 [1024], P('shard'), may hold values from 0.5 to 1.5
- w_z: bfloat16 [1024, 2048], P('shard', 'tensor'), may hold values from -0.1875 to 0.1875
- w_x: bfloat16 [1024, 2048], P('shard', 'tensor'), may hold values from -0.1875 to 0.1875
- w_dt: bfloat16 [1024, 32], P('shard', 'tensor'), may hold values from -0.1875 to 0.1875
- w_bc: bfloat16 [1024, 256], P('shard'), may hold values from -0.1875 to 0.1875
- conv_x: float32 [4, 2048], P(None, 'tensor'), may hold values from -3 to 3
- conv_xb: float32 [2048], P('tensor'), may hold values from -0.5 to 0.5
- conv_bc: float32 [4, 256], replicated, may hold values from -3 to 3
- conv_bcb: float32 [256], replicated, may hold values from -0.5 to 0.5
- dt_bias: float32 [32], P('tensor'), may hold values from -4 to -1
- a_log: float32 [32], P('tensor'), may hold values from -3.5 to 1
- d_skip: float32 [32], P('tensor'), may hold values from 0.3 to 1
- gate_gain: float32 [2048], P('tensor'), may hold values from 0.5 to 1.5
- w_out: bfloat16 [1024, 2048], P('shard', 'tensor'), may hold values from -0.125 to 0.125
- cotangent: bfloat16 [32768, 1024], P(('shard', 'context')), may hold values from -6 to 6
Outputs:
- output: bfloat16 [32768, 1024], P(('shard', 'context'))
- d_tokens: bfloat16 [32768, 1024], P(('shard', 'context'))
- g_norm_gain: float32 [1024], P('shard')
- g_w_z: float32 [1024, 2048], P('shard', 'tensor')
- g_w_x: float32 [1024, 2048], P('shard', 'tensor')
- g_w_dt: float32 [1024, 32], P('shard', 'tensor')
- g_w_bc: float32 [1024, 256], P('shard')
- g_conv_x: float32 [4, 2048], P(None, 'tensor')
- g_conv_xb: float32 [2048], P('tensor')
- g_conv_bc: float32 [4, 256], replicated
- g_conv_bcb: float32 [256], replicated
- g_dt_bias: float32 [32], P('tensor')
- g_a_log: float32 [32], P('tensor')
- g_d_skip: float32 [32], P('tensor')
- g_gate_gain: float32 [2048], P('tensor')
- g_w_out: float32 [1024, 2048], P('shard', 'tensor')
The draws below stay inside these ranges and needn't reach their ends.
Inputs may be any that keep to these rules, and one draw needn't show every extreme that they name: Along each packed row of 2048 tokens the segment numbers start at 0, never fall, and rise by at most 1 from one token to the next; each row ends with segment number 1024 // 16.
All inputs are finite; a program needn't handle non-finite values.
Results may differ from the reference program's by a relative error of at most 0.012.
The reference program's roundings to bfloat16 on the way count: a program that leaves them out, or rounds other values in their place, can miss the bound.
Values may be sent and summed in bfloat16 or wider, within the bound.
A program may use at most 192 MiB of HBM per device.

```python
from functools import partial
import jax
import jax.numpy as jnp
from jax import lax

D = 1024
NHEADS = 32
HEADDIM = 64
STATE = 128
CONV = 4
STRETCH = 256
TOK_DEV = 1024
INNER = 2048
LEN = 2048
TOKENS = 32768


def draw_segment(key, part):
    key = jax.random.fold_in(key, 11)
    row_count = TOKENS // LEN
    half_span = TOK_DEV // 2
    starts_per_row = TOK_DEV // 16
    allowed = jnp.concatenate([jnp.arange(1, half_span), jnp.arange(LEN - half_span, LEN)]).astype(jnp.int32)
    phase_key, row_base = jax.random.split(key)
    row_phase = jax.random.randint(phase_key, (), 0, 4).astype(jnp.int32)
    first_special = (4 - row_phase) % 4
    row_keys = jax.random.split(row_base, row_count)
    row_ids = jnp.arange(row_count, dtype=jnp.int32)
    inner_pos = jnp.arange(1, LEN - 1, dtype=jnp.int32)

    def one_row(one_key, row_id):
        spread_key, offset_key, other_key = jax.random.split(one_key, 3)
        crossing = jax.random.permutation(spread_key, allowed)[:starts_per_row]
        edge_offset = jnp.where(row_id == first_special, 0, jax.random.randint(offset_key, (), -3, 4)).astype(jnp.int32)
        forced_pos = (TOK_DEV + edge_offset).astype(jnp.int32)
        candidates = inner_pos + (inner_pos >= forced_pos).astype(jnp.int32)
        near_edge = jnp.concatenate([jax.random.permutation(other_key, candidates)[:starts_per_row - 1], forced_pos[None]])
        special_row = (row_id + row_phase) % 4 == 0
        return jnp.where(special_row, near_edge, crossing).astype(jnp.int32)
    start_picks = jax.vmap(one_row)(row_keys, row_ids)
    starts = jnp.zeros((row_count, LEN), jnp.int32).at[jnp.arange(row_count)[:, None], start_picks].set(1)
    starts = starts.at[:, 0].set(1)
    return (jnp.cumsum(starts, axis=1) - 1).astype(jnp.int32).reshape(TOKENS)


def block_scale(own_key, extent, cuts, low, high):
    gain = 1.0
    for position, shards_of in cuts:
        draws = jax.random.uniform(jax.random.fold_in(jax.random.fold_in(own_key, 6), position), (shards_of,), jnp.float32, low / len(cuts), high / len(cuts))
        gain = gain * jnp.repeat(jnp.exp(draws), extent[position] // shards_of).reshape((-1,) + (1,) * (len(extent) - 1 - position))
    return gain


def scatter_about(key, dims, spread, reach, shards=(), kind=jnp.bfloat16):
    level = block_scale(key, dims, shards, -0.22, 0.18) if shards else 1.0
    values = jax.random.normal(key, dims, jnp.float32) * spread * level
    return jnp.minimum(jnp.maximum(values, -reach), reach).astype(kind)


def setup_inputs(seed: int = 0) -> dict:
    arg_keys = jax.random.split(jax.random.key(seed), 18)
    tokens = scatter_about(arg_keys[0], (TOKENS, D), 1.0, 6.0, ((0, 32),))
    segment = draw_segment(jax.random.fold_in(arg_keys[17], 71), 0)
    norm_gain = jnp.clip(1.0 + 0.1 * jax.random.normal(arg_keys[2], (D,), jnp.float32), 0.5, 1.5).astype(jnp.bfloat16)
    w_z = scatter_about(arg_keys[3], (D, INNER), D ** -0.5, 0.1875, ((0, 16), (1, 4)))
    w_x = scatter_about(arg_keys[4], (D, INNER), D ** -0.5, 0.1875, ((0, 16), (1, 4)))
    w_dt = scatter_about(arg_keys[5], (D, NHEADS), D ** -0.5, 0.1875, ((0, 16), (1, 4)))
    w_bc = scatter_about(arg_keys[6], (D, 2 * STATE), D ** -0.5, 0.1875, ((0, 16),))
    conv_x = scatter_about(arg_keys[7], (CONV, INNER), CONV ** -0.5, 3.0, ((1, 4),), jnp.float32)
    conv_xb = jnp.clip(jax.random.uniform(arg_keys[8], (INNER,), jnp.float32, -0.5, 0.5) * block_scale(arg_keys[8], (INNER,), ((0, 4),), -0.4, 0.0), -0.5, 0.5)
    conv_bc = scatter_about(arg_keys[9], (CONV, 2 * STATE), CONV ** -0.5, 3.0, (), jnp.float32)
    conv_bcb = jnp.clip(jax.random.uniform(arg_keys[10], (2 * STATE,), jnp.float32, -0.5, 0.5), -0.5, 0.5)
    dt_bias = jnp.clip(-4.0 + 3.0 * jax.random.uniform(arg_keys[11], (NHEADS,), jnp.float32) ** block_scale(arg_keys[11], (NHEADS,), ((0, 4),), -0.2, 0.2), -4.0, -1.0)
    a_log = jnp.clip(-3.5 + 4.5 * jax.random.uniform(arg_keys[12], (NHEADS,), jnp.float32) ** block_scale(arg_keys[12], (NHEADS,), ((0, 4),), -0.2, 0.2), -3.5, 1.0)
    d_skip = jnp.clip(0.3 + 0.7 * jax.random.uniform(arg_keys[13], (NHEADS,), jnp.float32) ** block_scale(arg_keys[13], (NHEADS,), ((0, 4),), -0.2, 0.2), 0.3, 1.0)
    gate_gain = jnp.clip(1.0 + 0.1 * jax.random.normal(arg_keys[14], (INNER,), jnp.float32), 0.5, 1.5)
    w_out = scatter_about(arg_keys[15], (D, INNER), INNER ** -0.5, 0.125, ((0, 16), (1, 4)))
    cotangent = scatter_about(arg_keys[16], (TOKENS, D), 1.0, 6.0, ((0, 32),))
    return dict(tokens=tokens, segment=segment, norm_gain=norm_gain, w_z=w_z, w_x=w_x, w_dt=w_dt, w_bc=w_bc, conv_x=conv_x, conv_xb=conv_xb, conv_bc=conv_bc, conv_bcb=conv_bcb, dt_bias=dt_bias, a_log=a_log, d_skip=d_skip, gate_gain=gate_gain, w_out=w_out, cotangent=cotangent)


EPSILON = 1e-05
TOP_PRECISION = lax.Precision.HIGHEST

@jax.custom_vjp
def low(v):
    return lax.optimization_barrier(v.astype(jnp.bfloat16)).astype(jnp.float32)

@jax.custom_vjp
def low_back(v):
    return v

def low_keep(v):
    return (low(v), None)

def low_pass(kept, grad):
    return (grad,)

def back_keep(v):
    return (v, None)

def back_low(kept, grad):
    return (low(grad),)
low.defvjp(low_keep, low_pass)
low_back.defvjp(back_keep, back_low)

def block_step(a_neg, carried, block_in):
    state_now, last_seg = carried
    x_act, b_act, c_act, dt_val, seg_ids = block_in
    cum_decay = jnp.cumsum(dt_val * a_neg[None, :], axis=0)
    length = seg_ids.shape[0]
    causal = jnp.arange(length)[:, None] >= jnp.arange(length)[None, :]
    pair_mask = (causal & (seg_ids[:, None] == seg_ids[None, :]))[:, :, None]
    log_gap = jnp.where(pair_mask, cum_decay[:, None, :] - cum_decay[None, :, :], 0.0)
    pair_decay = jnp.where(pair_mask, jnp.exp(log_gap), 0.0)
    scores = jnp.dot(c_act, b_act.T, precision=TOP_PRECISION)
    weights = pair_decay * scores[:, :, None] * dt_val[None, :, :]
    mixed_out = jnp.einsum('ijh,jhp->ihp', weights, x_act, precision=TOP_PRECISION)
    enter_decay = jnp.where((seg_ids == last_seg)[:, None], jnp.exp(cum_decay), 0.0)
    mixed_out = mixed_out + enter_decay[:, :, None] * jnp.einsum('in,hpn->ihp', c_act, state_now, precision=TOP_PRECISION)
    tail_decay = jnp.where((seg_ids == seg_ids[-1])[:, None], jnp.exp(cum_decay[-1][None, :] - cum_decay), 0.0) * dt_val
    keep_decay = jnp.where(seg_ids[-1] == last_seg, jnp.exp(cum_decay[-1]), 0.0)
    fresh_state = jnp.einsum('jh,jhp,jn->hpn', tail_decay, x_act, b_act, precision=TOP_PRECISION)
    return ((keep_decay[:, None, None] * state_now + fresh_state, seg_ids[-1]), mixed_out)

def row_mixer(conv_w, conv_b, dt_bias, a_log, d_skip, row_data):
    x_bc, seg_ids, dt_raw = row_data
    length = seg_ids.shape[0]
    padded = jnp.concatenate([jnp.zeros((CONV - 1, x_bc.shape[1]), x_bc.dtype), x_bc], axis=0)
    seg_pad = jnp.concatenate([jnp.full((CONV - 1,), -1.0, seg_ids.dtype), seg_ids])
    pre_conv = jnp.broadcast_to(conv_b[None, :], x_bc.shape)
    for offset in range(CONV):
        same_seg = (seg_pad[offset:offset + length] == seg_ids)[:, None]
        pre_conv = pre_conv + conv_w[offset][None, :] * jnp.where(same_seg, padded[offset:offset + length], 0.0)
    activated = jax.nn.silu(pre_conv)
    x_act = activated[:, :INNER].reshape(length, NHEADS, HEADDIM)
    b_act = activated[:, INNER:INNER + STATE]
    c_act = activated[:, INNER + STATE:]
    dt_val = jax.nn.softplus(dt_raw + dt_bias[None, :])
    a_neg = -jnp.exp(a_log)
    block_count = length // STRETCH
    blocks = (x_act.reshape(block_count, STRETCH, NHEADS, HEADDIM), b_act.reshape(block_count, STRETCH, STATE), c_act.reshape(block_count, STRETCH, STATE), dt_val.reshape(block_count, STRETCH, NHEADS), seg_ids.reshape(block_count, STRETCH))
    start_carry = (jnp.zeros((NHEADS, HEADDIM, STATE), x_bc.dtype), jnp.full((), -1.0, seg_ids.dtype))
    final_state, mixed_out = lax.scan(partial(block_step, a_neg), start_carry, blocks)
    return mixed_out.reshape(length, INNER) + (d_skip[None, :, None] * x_act).reshape(length, INNER)

def layer(seg_float, tokens, norm_gain, w_z, w_x, w_dt, w_bc, conv_x, conv_xb, conv_bc, conv_bcb, dt_bias, a_log, d_skip, gate_gain, w_out):
    root_inv = lax.rsqrt(lax.optimization_barrier(jnp.mean(tokens * tokens, axis=1, keepdims=True)) + EPSILON)
    x_normed = low(tokens * root_inv * norm_gain[None, :])
    z_gate = low_back(jnp.dot(x_normed, w_z, precision=TOP_PRECISION, preferred_element_type=jnp.float32))
    x_part = jnp.dot(x_normed, w_x, precision=TOP_PRECISION, preferred_element_type=jnp.float32)
    bc_part = jnp.dot(x_normed, w_bc, precision=TOP_PRECISION, preferred_element_type=jnp.float32)
    x_bc = low(low_back(jnp.concatenate([x_part, bc_part], axis=1)))
    dt_raw = low_back(jnp.dot(x_normed, w_dt, precision=TOP_PRECISION, preferred_element_type=jnp.float32))
    conv_w = jnp.concatenate([conv_x, conv_bc], axis=1)
    conv_b = jnp.concatenate([conv_xb, conv_bcb])
    row_count = TOKENS // LEN
    mixer_fn = jax.checkpoint(partial(row_mixer, conv_w, conv_b, dt_bias, a_log, d_skip))
    y_mixed = lax.map(mixer_fn, (x_bc.reshape(row_count, LEN, INNER + 2 * STATE), seg_float.reshape(row_count, LEN), dt_raw.reshape(row_count, LEN, NHEADS))).reshape(TOKENS, INNER)
    gated = y_mixed * jax.nn.silu(z_gate)
    gate_root = lax.rsqrt(lax.optimization_barrier(jnp.mean(gated * gated, axis=1, keepdims=True)) + EPSILON)
    y_normed = low(gated * gate_root * gate_gain[None, :])
    branch = jnp.dot(y_normed, w_out.T, precision=TOP_PRECISION, preferred_element_type=jnp.float32)
    return tokens + branch

def reference(tokens, segment, norm_gain, w_z, w_x, w_dt, w_bc, conv_x, conv_xb, conv_bc, conv_bcb, dt_bias, a_log, d_skip, gate_gain, w_out, cotangent):
    as_float = [value.astype(jnp.float32) for value in (tokens, norm_gain, w_z, w_x, w_dt, w_bc, conv_x, conv_xb, conv_bc, conv_bcb, dt_bias, a_log, d_skip, gate_gain, w_out)]
    result, pullback = jax.vjp(partial(layer, segment.astype(jnp.float32)), *as_float)
    grads = pullback(cotangent.astype(jnp.float32))
    return (result.astype(jnp.bfloat16), grads[0].astype(jnp.bfloat16), grads[1], grads[2], grads[3], grads[4], grads[5], grads[6], grads[7], grads[8], grads[9], grads[10], grads[11], grads[12], grads[13], grads[14])
```

```python
from functools import partial

import jax
import jax.numpy as jnp
import numpy as np
from jax import lax
from jax.experimental import pallas as pl
from jax.experimental.pallas import tpu as pltpu
from jax.sharding import PartitionSpec as P

HEADDIM = 64
STATE = 128
CONV = 4
INNER = 2048


EPSILON = 1e-05


F32 = jnp.float32
BF = jnp.bfloat16
Q = 128
EDGE = 16
VMEM_LIMIT = 58 * 1024 * 1024


def mm(a, b):
    return lax.dot_general(a, b, (((1,), (0,)), ((), ())), preferred_element_type=F32)


def mm_nt(a, b):
    return lax.dot_general(a, b, (((1,), (1,)), ((), ())), preferred_element_type=F32)


def mm_tn(a, b):
    return lax.dot_general(a, b, (((0,), (0,)), ((), ())), preferred_element_type=F32)


def split2(v):
    hi = v.astype(BF)
    return hi, (v - hi.astype(F32)).astype(BF)


def mm2(a, b):
    hi, lo = split2(a)
    return mm(hi, b) + mm(lo, b)


def mm3_left(a, b):
    hi, lo = split2(b)
    lo2 = (b - hi.astype(F32) - lo.astype(F32)).astype(BF)
    return mm(a, hi) + (mm(a, lo) + mm(a, lo2))


def softplus(v):
    return jnp.maximum(v, 0.0) + jnp.log1p(jnp.exp(-jnp.abs(v)))


def sigmoid(v):
    return 1.0 / (1.0 + jnp.exp(-v))


def triangles():
    rows = lax.broadcasted_iota(jnp.int32, (Q, Q), 0)
    cols = lax.broadcasted_iota(jnp.int32, (Q, Q), 1)
    return rows >= cols, rows <= cols


def as_low(mask):
    return jnp.where(mask, 1.0, 0.0).astype(BF)


def halves(slab):
    lane = lax.broadcasted_iota(jnp.int32, slab.shape, 1)
    zero = jnp.zeros_like(slab)
    first = jnp.where(lane < HEADDIM, slab, zero)
    second = jnp.where(lane >= HEADDIM, slab, zero)
    return jnp.concatenate([first, second], axis=0)


def front_kernel(
    tok, etok, gain, w, colm, segr, cw, cb, dtb, alog, dsk, ex,
    xn_o, z_o, xbc_o, pre_o, dtr_o, y_o, er_o, c_o, st_o, xs,
):
    a_neg = -jnp.exp(alog[...])
    causal, _ = triangles()
    lower = as_low(causal)
    gain_row = gain[...].astype(F32)

    def normed(block):
        plain = block.astype(F32)
        root = lax.rsqrt(jnp.mean(plain * plain, axis=1, keepdims=True) + EPSILON)
        return (plain * root * gain_row).astype(BF)

    edge = mm(normed(etok[...]), w[:, 512:1280]).astype(BF)
    xbc_o[0:EDGE] = edge
    xs[0:EDGE] = edge.astype(F32)
    st_o[...] = jnp.zeros_like(st_o)
    expand = ex[...]
    dsk_e = mm2(dsk[...], expand)

    def body(b, run):
        r = pl.ds(pl.multiple_of(b * Q, Q), Q)
        rn = pl.ds(pl.multiple_of(b * Q + EDGE, EDGE), Q)
        xn = normed(tok[r])
        xn_o[r] = xn
        z_o[r] = mm(xn, w[:, 0:512])
        xb = mm(xn, w[:, 512:1280]).astype(BF)
        xbc_o[rn] = xb
        xs[rn] = xb.astype(F32)
        raw = mm(xn, w[:, 1280:1408])[:, 0:8]
        dtr_o[r] = raw
        marks = colm[r]
        acts = []
        for c in range(6):
            lanes = slice(c * 128, c * 128 + 128)
            slab = xs[pl.ds(pl.multiple_of(b * Q, Q), Q + EDGE), lanes]
            pre = cb[:, lanes] + cw[3:4, lanes] * slab[EDGE:]
            for d in range(1, 4):
                pre = pre + (cw[3 - d : 4 - d, lanes] * slab[EDGE - d : Q + EDGE - d]) * marks[:, d : d + 1]
            pre_o[r, lanes] = pre
            acts.append(pre * sigmoid(pre))
        b_low = acts[4].astype(BF)
        c_low = acts[5].astype(BF)
        c_o[r] = c_low
        dt = softplus(raw + dtb[...])
        cum = mm3_left(lower, dt * a_neg)
        er_o[r] = jnp.exp(run + cum) * marks[:, 4:5]
        cum_t = cum.T
        last = cum[Q - 1 : Q]
        enter = jnp.exp(cum) * marks[:, 5:6]
        tail = jnp.exp(last - cum) * marks[:, 6:7]
        dt_e = mm2(dt, expand)
        enter_e = mm2(enter, expand)
        tail_e = mm2(tail, expand)
        mask = causal & (marks[:, 0:1] == segr[pl.ds(b, 1), :])
        scores = jnp.where(mask, mm_nt(c_low, b_low), 0.0)
        state = st_o[...]
        inter = mm(c_low, state.astype(BF))
        pieces = []
        for p in range(4):
            lanes = slice(p * 128, p * 128 + 128)
            xdt = acts[p] * dt_e[:, lanes]
            pieces.append((xdt * tail_e[:, lanes]).astype(BF))
            ws = []
            for h in (2 * p, 2 * p + 1):
                decay = jnp.exp(jnp.minimum(cum[:, h : h + 1] - cum_t[h : h + 1, :], 0.0))
                ws.append((decay * scores).astype(BF))
            intra = mm(jnp.concatenate(ws, axis=1), halves(xdt.astype(BF)))
            y_o[r, lanes] = intra + enter_e[:, lanes] * inter[:, lanes] + dsk_e[:, lanes] * acts[p]
        fresh = mm_tn(b_low, jnp.concatenate(pieces, axis=1))
        st_o[...] = enter_e[Q - 1 : Q] * state + fresh
        return run + last

    lax.fori_loop(0, 8, body, jnp.zeros((1, 8), F32))


def back_kernel(
    dy, colm, segr, xbc, pre_r, dtr, st_in, g_in, cw, dtb, alog, dsk, ex, ext,
    dx_o, dbc_o, tail_o, ret_o, ddt_o, gcw_o, gcb_o, gh_o,
    states, acts, dpre, grad, heads,
):
    a_neg = -jnp.exp(alog[...])
    causal, anti = triangles()
    lower = as_low(causal)
    upper = as_low(anti)
    expand = ex[...]
    expand_t = ext[...]
    dsk_e = mm2(dsk[...], expand)

    def head_sum(v):
        return mm2(v, expand_t)

    states[0] = st_in[...]

    def forward(b, carry):
        r = pl.ds(pl.multiple_of(b * Q, Q), Q)
        marks = colm[r]
        dt = softplus(dtr[r] + dtb[...])
        cum = mm3_left(lower, dt * a_neg)
        last = cum[Q - 1 : Q]
        tail = jnp.exp(last - cum) * marks[:, 6:7] * dt
        keep_e = mm2(jnp.exp(last) * marks[Q - 1 : Q, 5:6], expand)
        tail_e = mm2(tail, expand)
        pieces = []
        for c in range(6):
            lanes = slice(c * 128, c * 128 + 128)
            pre = pre_r[r, lanes]
            act = pre * sigmoid(pre)
            acts[r, lanes] = act
            if c < 4:
                pieces.append((act * tail_e[:, lanes]).astype(BF))
            if c == 4:
                b_low = act.astype(BF)
        fresh = mm_tn(b_low, jnp.concatenate(pieces, axis=1))
        states[b + 1] = keep_e * states[b] + fresh
        return carry

    lax.fori_loop(0, 7, forward, 0)
    r7 = slice(7 * Q, 8 * Q)
    for c in range(6):
        lanes = slice(c * 128, c * 128 + 128)
        pre = pre_r[r7, lanes]
        acts[r7, lanes] = pre * sigmoid(pre)
    grad[...] = g_in[...]
    heads[...] = jnp.zeros_like(heads)
    dpre[0:8] = jnp.zeros((8, 768), F32)
    dpre[1032:1040] = jnp.zeros((8, 768), F32)

    def backward(i, carry):
        b = 7 - i
        r = pl.ds(pl.multiple_of(b * Q, Q), Q)
        rp = pl.ds(pl.multiple_of(b * Q + 8, 8), Q)
        marks = colm[r]
        raw = dtr[r] + dtb[...]
        dt = softplus(raw)
        cum = mm3_left(lower, dt * a_neg)
        cum_t = cum.T
        last = cum[Q - 1 : Q]
        enter = jnp.exp(cum) * marks[:, 5:6]
        tail = jnp.exp(last - cum) * marks[:, 6:7]
        dt_e = mm2(dt, expand)
        enter_e = mm2(enter, expand)
        tail_e = mm2(tail, expand)
        keep_e = enter_e[Q - 1 : Q]
        b_low = acts[r, 512:640].astype(BF)
        c_low = acts[r, 640:768].astype(BF)
        state = states[b]
        state_low = state.astype(BF)
        g_now = grad[...]
        g_low = g_now.astype(BF)
        inter = mm(c_low, state_low)
        back = mm(b_low, g_low)
        mask = causal & (marks[:, 0:1] == segr[pl.ds(b, 1), :])
        scores = jnp.where(mask, mm_nt(c_low, b_low), 0.0)
        kept = jnp.sum(state * g_now, axis=0, keepdims=True) * keep_e
        entered, tailed, e_terms, q_terms, x_terms, k_terms = [], [], [], [], [], []
        rows, cols = [], []
        d_scores = jnp.zeros((Q, Q), F32)
        for p in range(4):
            lanes = slice(p * 128, p * 128 + 128)
            x = acts[r, lanes]
            dys = dy[r, lanes]
            xdt = x * dt_e[:, lanes]
            xdt_low = xdt.astype(BF)
            ed = enter_e[:, lanes] * dys
            tx = tail_e[:, lanes] * xdt
            entered.append(ed.astype(BF))
            tailed.append(tx.astype(BF))
            dy_two = halves(dys.astype(BF))
            dw_two = mm_nt(dy_two, xdt_low)
            ws = []
            for k in range(2):
                h = 2 * p + k
                decay = jnp.exp(jnp.minimum(cum[:, h : h + 1] - cum_t[h : h + 1, :], 0.0))
                weight = decay * scores
                dw = dw_two[k * Q : k * Q + Q]
                d_scores = d_scores + decay * dw
                both = weight * dw
                rows.append(jnp.sum(both, axis=1, keepdims=True))
                cols.append(jnp.sum(both, axis=0, keepdims=True))
                ws.append(weight.astype(BF))
            dxdt = mm_tn(jnp.concatenate(ws, axis=0), dy_two) + tail_e[:, lanes] * back[:, lanes]
            e_terms.append(ed * inter[:, lanes] - tx * back[:, lanes])
            q_terms.append(jnp.sum(tx * back[:, lanes], axis=0, keepdims=True) + kept[:, lanes])
            x_terms.append(dxdt * x)
            k_terms.append(jnp.sum(dys * x, axis=0, keepdims=True))
            pre = pre_r[r, lanes]
            sig = sigmoid(pre)
            dpre[rp, lanes] = (dxdt * dt_e[:, lanes] + dsk_e[:, lanes] * dys) * (sig * (1.0 + pre * (1.0 - sig)))
        entered = jnp.concatenate(entered, axis=1)
        tailed = jnp.concatenate(tailed, axis=1)
        ds_low = jnp.where(mask, d_scores, 0.0).astype(BF)
        d_c = mm_nt(entered, state_low) + mm(ds_low, b_low)
        d_b = mm_nt(tailed, g_low) + mm_tn(ds_low, c_low)
        grad[...] = keep_e * g_now + mm_tn(c_low, entered)
        for c, value in ((4, d_b), (5, d_c)):
            lanes = slice(c * 128, c * 128 + 128)
            pre = pre_r[r, lanes]
            sig = sigmoid(pre)
            dpre[rp, lanes] = value * (sig * (1.0 + pre * (1.0 - sig)))
        d_cum = jnp.concatenate(rows, axis=1) - jnp.concatenate(cols, axis=0).T
        d_cum = d_cum + head_sum(jnp.concatenate(e_terms, axis=1))
        d_log = mm3_left(upper, d_cum) + head_sum(jnp.concatenate(q_terms, axis=1))
        d_dt = d_log * a_neg + head_sum(jnp.concatenate(x_terms, axis=1))
        d_raw = d_dt * sigmoid(raw)
        ddt_o[r] = d_raw
        heads[0:1] += jnp.sum(d_raw, axis=0, keepdims=True)
        heads[1:2] += jnp.sum(d_log * dt, axis=0, keepdims=True) * a_neg
        heads[2:3] += head_sum(jnp.concatenate(k_terms, axis=1))
        return carry

    lax.fori_loop(0, 8, backward, 0)
    gh_o[...] = heads[...]

    for c in range(6):
        lanes = slice(c * 128, c * 128 + 128)
        first = dpre[0:16, lanes]
        flags = jnp.concatenate([jnp.zeros((8, 8), F32), colm[0:8]], axis=0)
        total = jnp.zeros((8, 128), F32)
        for d in range(1, 4):
            total = total + cw[3 - d : 4 - d, lanes] * (first * flags[:, d : d + 1])[d : d + 8]
        ret_o[:, lanes] = total

        def conv(b, sums, lanes=lanes, c=c):
            r = pl.ds(pl.multiple_of(b * Q, Q), Q)
            slab = dpre[pl.ds(pl.multiple_of(b * Q + 8, 8), Q + 8), lanes]
            marks = colm[pl.ds(pl.multiple_of(b * Q, Q), Q + 8)]
            xin = xbc[pl.ds(pl.multiple_of(b * Q, Q), Q + EDGE), lanes].astype(F32)
            main = slab[0:Q]
            out = cw[3:4, lanes] * main
            new = [sums[0] + jnp.sum(main, axis=0, keepdims=True),
                   sums[1] + jnp.sum(main * xin[EDGE:], axis=0, keepdims=True)]
            for d in range(1, 4):
                masked = slab * marks[:, d : d + 1]
                out = out + cw[3 - d : 4 - d, lanes] * masked[d : d + Q]
                new.append(sums[d + 1] + jnp.sum(masked[0:Q] * xin[EDGE - d : Q + EDGE - d], axis=0, keepdims=True))
            if c < 4:
                dx_o[r, lanes] = out.astype(BF)
            else:
                dbc_o[r, slice(c * 128 - 512, c * 128 - 384)] = out

            @pl.when(b == 7)
            def _():
                tail_o[:, lanes] = out[Q - EDGE :]

            return tuple(new)

        zero = jnp.zeros((1, 128), F32)
        sums = lax.fori_loop(0, 8, conv, (zero,) * 5)
        gcb_o[:, lanes] = sums[0]
        for d in range(4):
            gcw_o[3 - d : 4 - d, lanes] = sums[d + 1]


def passed_along(value, axis, by):
    count = lax.axis_size(axis)
    pairs = [(i, i + by) for i in range(count) if 0 <= i + by < count]
    return lax.ppermute(value, axis, pairs)


def against(left, right):
    return lax.dot_general(
        left, right, (((1,), (1,)), ((), ())), preferred_element_type=jnp.float32
    )


def over_rows(left, right):
    return lax.dot_general(
        left, right, (((0,), (0,)), ((), ())), preferred_element_type=jnp.float32
    )


def silu_slope(value):
    sigma = jax.nn.sigmoid(value)
    return sigma * (1.0 + value * (1.0 - sigma))


def call(kernel, out_shapes, scratch, *args):
    return pl.pallas_call(
        kernel,
        out_shape=[jax.ShapeDtypeStruct(s, d) for s, d in out_shapes],
        in_specs=[pl.BlockSpec(memory_space=pltpu.VMEM)] * len(args),
        out_specs=[pl.BlockSpec(memory_space=pltpu.VMEM)] * len(out_shapes),
        scratch_shapes=[pltpu.VMEM(s, d) for s, d in scratch],
        compiler_params=pltpu.CompilerParams(vmem_limit_bytes=VMEM_LIMIT),
    )(*args)


def local(
    tokens,
    segment,
    norm_gain,
    w_z,
    w_x,
    w_dt,
    w_bc,
    conv_x,
    conv_xb,
    conv_bc,
    conv_bcb,
    dt_bias,
    a_log,
    d_skip,
    gate_gain,
    w_out,
    cotangent,
):
    gain_all, z_all, x_all, dt_all, bc_all, out_all = (
        lax.all_gather(norm_gain, "shard", axis=0, tiled=True),
        lax.all_gather(w_z, "shard", axis=0, tiled=True),
        lax.all_gather(w_x, "shard", axis=0, tiled=True),
        lax.all_gather(w_dt, "shard", axis=0, tiled=True),
        lax.all_gather(w_bc, "shard", axis=0, tiled=True),
        lax.all_gather(w_out, "shard", axis=0, tiled=True),
    )
    length = tokens.shape[0]
    head_count = dt_bias.shape[0]
    inner_width = head_count * HEADDIM
    bc_width = 2 * STATE
    pad_dt = jnp.pad(dt_all, ((0, 0), (0, 120)))
    w_in = jnp.concatenate([z_all, x_all, bc_all, pad_dt], axis=1)
    edge_tokens, edge_ids = passed_along((tokens[length - EDGE :], segment[length - EDGE :]), "context", 1)
    seg = segment
    ext_ids = jnp.concatenate([edge_ids[-3:], seg])
    start_seg = jnp.where(edge_ids[-1] == seg[0], seg[0], -1)
    blocks = seg.reshape(length // Q, Q)
    before = jnp.concatenate([start_seg[None], blocks[:-1, -1]])
    marks = [seg.astype(F32)]
    marks += [(ext_ids[3 - d : 3 - d + length] == seg).astype(F32) for d in (1, 2, 3)]
    marks += [(seg == start_seg).astype(F32)]
    marks += [(blocks == before[:, None]).astype(F32).reshape(-1)]
    marks += [(blocks == blocks[:, -1:]).astype(F32).reshape(-1)]
    marks += [jnp.zeros((length,), F32)]
    colm = jnp.pad(jnp.stack(marks, axis=1), ((0, 8), (0, 0)))
    segr = blocks.astype(F32)
    conv_w = jnp.concatenate([conv_x, conv_bc], axis=1)
    conv_b = jnp.concatenate([conv_xb, conv_bcb])[None]
    expand_np = np.kron(np.eye(8), np.ones((1, HEADDIM)))
    expand = jnp.asarray(expand_np, BF)
    expand_t = jnp.asarray(expand_np.T, BF)
    wide = (length, inner_width)
    x_normed, z_gate, xbc, pre, dt_raw, y_zero, enter_decay, c_act, state_local = call(
        front_kernel,
        [((length, 1024), BF), (wide, F32), ((length + EDGE, 768), BF), ((length, 768), F32), ((length, 8), F32),
         (wide, F32), ((length, 8), F32), ((length, STATE), BF), ((STATE, inner_width), F32)],
        [((length + EDGE, 768), F32)],
        tokens, edge_tokens, gain_all[None], w_in, colm, segr, conv_w, conv_b, dt_bias[None], a_log[None], d_skip[None], expand,
    )
    plain = tokens.astype(F32)
    root_inv = lax.rsqrt(jnp.mean(plain * plain, axis=1, keepdims=True) + EPSILON)
    gain_float = gain_all.astype(F32)
    state_in = passed_along(state_local, "context", 1)
    decay_e = jnp.repeat(enter_decay, HEADDIM, axis=1)
    y_mixed = y_zero + decay_e * jnp.dot(c_act, state_in.astype(BF), preferred_element_type=F32)
    gate_act = jax.nn.silu(z_gate)
    gated = y_mixed * gate_act
    d_y_normed = jnp.dot(cotangent, out_all, preferred_element_type=F32)
    d_scaled = d_y_normed * gate_gain[None, :]
    sums = lax.psum(jnp.stack([jnp.sum(gated * gated, axis=1), jnp.sum(d_scaled * gated, axis=1)]), "tensor")
    gate_root = lax.rsqrt(sums[0] / INNER + EPSILON)[:, None]
    y_normed = (gated * gate_root * gate_gain[None, :]).astype(BF)
    branch_part = against(y_normed, out_all).astype(BF)
    g_w_out = over_rows(cotangent, y_normed).astype(BF)
    g_gate_gain = jnp.sum(d_y_normed * gated * gate_root, axis=0)
    d_gated = gate_root * d_scaled - gated * gate_root**3 * (sums[1] / INNER)[:, None]
    d_y = d_gated * gate_act
    d_z = (d_gated * y_mixed * silu_slope(z_gate)).astype(BF)
    d_carry = over_rows(c_act, (d_y * decay_e).astype(BF)).astype(BF)
    d_state_out = passed_along(d_carry, "context", -1).astype(F32)
    d_x_first, d_bc_first, tail_rows, back_rows, d_dt_raw, g_conv_w, g_conv_b, g_heads = call(
        back_kernel,
        [(wide, BF), ((length, bc_width), F32), ((EDGE, 768), F32), ((8, 768), F32), ((length, 8), F32),
         ((CONV, 768), F32), ((1, 768), F32), ((8, 8), F32)],
        [((8, STATE, inner_width), F32), ((length, 768), F32), ((length + 16, 768), F32), ((STATE, inner_width), F32), ((8, 8), F32)],
        d_y, colm, segr, xbc, pre, dt_raw, state_in, d_state_out, conv_w, dt_bias[None], a_log[None], d_skip[None], expand, expand_t,
    )
    returned = passed_along(back_rows, "context", -1)
    tail_rows = tail_rows + jnp.pad(returned, ((EDGE - 8, 0), (0, 0)))
    d_x_low = lax.dynamic_update_slice(d_x_first, tail_rows[:, :inner_width].astype(BF), (length - EDGE, 0))
    d_bc = lax.dynamic_update_slice(d_bc_first, tail_rows[:, inner_width:], (length - EDGE, 0))
    d_dt_low = d_dt_raw.astype(BF)
    part_in = (against(d_z, z_all) + against(d_x_low, x_all) + against(d_dt_low, dt_all)).astype(BF)
    g_w_z = over_rows(x_normed, d_z).astype(BF)
    g_w_x = over_rows(x_normed, d_x_low).astype(BF)
    g_w_dt = over_rows(x_normed, d_dt_low).astype(BF)
    in_sum, bc_sum, branch, conv_bc_sum, conv_bcb_sum = lax.psum(
        (part_in, d_bc.astype(BF), branch_part, g_conv_w[:, inner_width:], g_conv_b[:, inner_width:]), "tensor"
    )
    output = (plain + branch).astype(BF)
    d_bc_low = bc_sum.astype(BF)
    d_x_normed = in_sum + against(d_bc_low, bc_all)
    stat_rows = plain * root_inv
    g_norm_gain = jnp.sum(d_x_normed * stat_rows, axis=0)
    d_plain = d_x_normed * gain_float[None, :]
    d_tokens = (
        cotangent.astype(F32)
        + root_inv * d_plain
        - plain * root_inv**3 * jnp.mean(d_plain * plain, axis=1, keepdims=True)
    ).astype(BF)
    g_w_bc = over_rows(x_normed, d_bc_low).astype(BF)
    whole = jnp.concatenate([g_w_z, g_w_x, g_w_out, g_w_bc, g_w_dt], axis=1)
    owned = lax.psum(lax.psum_scatter(whole, "shard", scatter_dimension=0, tiled=True), "context").astype(F32)
    small, gn = lax.psum((jnp.concatenate([g_conv_w[:, :inner_width].reshape(-1), g_conv_b[0, :inner_width], conv_bc_sum.reshape(-1),
        conv_bcb_sum[0], g_heads[0], g_heads[1], g_heads[2], g_gate_gain]), g_norm_gain), ("shard", "context"))
    own_norm = lax.dynamic_slice(gn, (lax.axis_index("shard") * 64,), (64,))
    cuts = np.cumsum([2048, 512, 1024, 256, 8, 8, 8])
    pieces = jnp.split(small, cuts)
    return (
        output,
        d_tokens,
        own_norm,
        owned[:, 0:512],
        owned[:, 512:1024],
        owned[:, 1792:1800],
        owned[:, 1536:1792],
        pieces[0].reshape(CONV, inner_width),
        pieces[1],
        pieces[2].reshape(CONV, bc_width),
        pieces[3],
        pieces[4],
        pieces[5],
        pieces[6],
        pieces[7],
        owned[:, 1024:1536],
    )


def solution(mesh):
    in_specs = (
        P(("shard", "context"), None),
        P(("shard", "context")),
        P("shard"),
        P("shard", "tensor"),
        P("shard", "tensor"),
        P("shard", "tensor"),
        P("shard", None),
        P(None, "tensor"),
        P("tensor"),
        P(),
        P(),
        P("tensor"),
        P("tensor"),
        P("tensor"),
        P("tensor"),
        P("shard", "tensor"),
        P(("shard", "context"), None),
    )
    out_specs = (
        P(("shard", "context"), None),
        P(("shard", "context"), None),
        P("shard"),
        P("shard", "tensor"),
        P("shard", "tensor"),
        P("shard", "tensor"),
        P("shard", None),
        P(None, "tensor"),
        P("tensor"),
        P(),
        P(),
        P("tensor"),
        P("tensor"),
        P("tensor"),
        P("tensor"),
        P("shard", "tensor"),
    )
    return jax.shard_map(local, mesh=mesh, in_specs=in_specs, out_specs=out_specs, check_vma=False)
```

```python
from functools import partial

import jax
import jax.numpy as jnp
import numpy as np
from jax import lax
from jax.experimental import pallas as pl
from jax.experimental.pallas import tpu as pltpu
from jax.sharding import PartitionSpec as P

HEADDIM = 64
STATE = 128
CONV = 4
INNER = 2048


EPSILON = 1e-05


F32 = jnp.float32
BF = jnp.bfloat16
Q = 128
EDGE = 16
VMEM_LIMIT = 58 * 1024 * 1024


def mm(a, b):
    return lax.dot_general(a, b, (((1,), (0,)), ((), ())), preferred_element_type=F32)


def mm_nt(a, b):
    return lax.dot_general(a, b, (((1,), (1,)), ((), ())), preferred_element_type=F32)


def mm_tn(a, b):
    return lax.dot_general(a, b, (((0,), (0,)), ((), ())), preferred_element_type=F32)


def split2(v):
    hi = v.astype(BF)
    return hi, (v - hi.astype(F32)).astype(BF)


def mm2(a, b):
    hi, lo = split2(a)
    return mm(hi, b) + mm(lo, b)


def mm3_left(a, b):
    hi, lo = split2(b)
    lo2 = (b - hi.astype(F32) - lo.astype(F32)).astype(BF)
    return mm(a, hi) + (mm(a, lo) + mm(a, lo2))


def softplus(v):
    return jnp.maximum(v, 0.0) + jnp.log1p(jnp.exp(-jnp.abs(v)))


def sigmoid(v):
    return 1.0 / (1.0 + jnp.exp(-v))


def triangles():
    rows = lax.broadcasted_iota(jnp.int32, (Q, Q), 0)
    cols = lax.broadcasted_iota(jnp.int32, (Q, Q), 1)
    return rows >= cols, rows <= cols


def as_low(mask):
    return jnp.where(mask, 1.0, 0.0).astype(BF)


def halves(slab):
    lane = lax.broadcasted_iota(jnp.int32, slab.shape, 1)
    zero = jnp.zeros_like(slab)
    first = jnp.where(lane < HEADDIM, slab, zero)
    second = jnp.where(lane >= HEADDIM, slab, zero)
    return jnp.concatenate([first, second], axis=0)


def front_kernel(
    tok, etok, w, colm, segr, cw, cb, dtb, alog, dsk, ex,
    xn_o, z_o, xbc_o, pre_o, dtr_o, y_o, er_o, c_o, st_o, gain_o, xs,
):
    a_neg = -jnp.exp(alog[...])
    causal, _ = triangles()
    lower = as_low(causal)
    gain_row = w[:, 1280:1408].astype(F32).T[8:9]
    gain_o[...] = gain_row

    def normed(block):
        plain = block.astype(F32)
        root = lax.rsqrt(jnp.mean(plain * plain, axis=1, keepdims=True) + EPSILON)
        return (plain * root * gain_row).astype(BF)

    edge = mm(normed(etok[...]), w[:, 512:1280]).astype(BF)
    xbc_o[0:EDGE] = edge
    xs[0:EDGE] = edge.astype(F32)
    st_o[...] = jnp.zeros_like(st_o)
    expand = ex[...]
    dsk_e = mm2(dsk[...], expand)

    def body(b, run):
        r = pl.ds(pl.multiple_of(b * Q, Q), Q)
        rn = pl.ds(pl.multiple_of(b * Q + EDGE, EDGE), Q)
        xn = normed(tok[r])
        xn_o[r] = xn
        z_o[r] = mm(xn, w[:, 0:512])
        xb = mm(xn, w[:, 512:1280]).astype(BF)
        xbc_o[rn] = xb
        xs[rn] = xb.astype(F32)
        raw = mm(xn, w[:, 1280:1408])[:, 0:8]
        dtr_o[r] = raw
        marks = colm[r]
        acts = []
        for c in range(6):
            lanes = slice(c * 128, c * 128 + 128)
            slab = xs[pl.ds(pl.multiple_of(b * Q, Q), Q + EDGE), lanes]
            pre = cb[:, lanes] + cw[3:4, lanes] * slab[EDGE:]
            for d in range(1, 4):
                pre = pre + (cw[3 - d : 4 - d, lanes] * slab[EDGE - d : Q + EDGE - d]) * marks[:, d : d + 1]
            pre_o[r, lanes] = pre
            acts.append(pre * sigmoid(pre))
        b_low = acts[4].astype(BF)
        c_low = acts[5].astype(BF)
        c_o[r] = c_low
        dt = softplus(raw + dtb[...])
        cum = mm3_left(lower, dt * a_neg)
        er_o[r] = jnp.exp(run + cum) * marks[:, 4:5]
        cum_t = cum.T
        last = cum[Q - 1 : Q]
        enter = jnp.exp(cum) * marks[:, 5:6]
        tail = jnp.exp(last - cum) * marks[:, 6:7]
        dt_e = mm2(dt, expand)
        enter_e = mm2(enter, expand)
        tail_e = mm2(tail, expand)
        mask = causal & (marks[:, 0:1] == segr[pl.ds(b, 1), :])
        scores = jnp.where(mask, mm_nt(c_low, b_low), 0.0)
        state = st_o[...]
        inter = mm(c_low, state.astype(BF))
        pieces = []
        for p in range(4):
            lanes = slice(p * 128, p * 128 + 128)
            xdt = acts[p] * dt_e[:, lanes]
            pieces.append((xdt * tail_e[:, lanes]).astype(BF))
            ws = []
            for h in (2 * p, 2 * p + 1):
                decay = jnp.exp(jnp.minimum(cum[:, h : h + 1] - cum_t[h : h + 1, :], 0.0))
                ws.append((decay * scores).astype(BF))
            intra = mm(jnp.concatenate(ws, axis=1), halves(xdt.astype(BF)))
            y_o[r, lanes] = intra + enter_e[:, lanes] * inter[:, lanes] + dsk_e[:, lanes] * acts[p]
        fresh = mm_tn(b_low, jnp.concatenate(pieces, axis=1))
        st_o[...] = enter_e[Q - 1 : Q] * state + fresh
        return run + last

    lax.fori_loop(0, 8, body, jnp.zeros((1, 8), F32))


def back_kernel(
    dy, colm, segr, xbc, pre_r, dtr, st_in, g_in, cw, dtb, alog, dsk, ex, ext,
    dx_o, dbc_o, tail_o, ret_o, ddt_o, small_o,
    states, acts, dpre, grad, heads,
):
    a_neg = -jnp.exp(alog[...])
    causal, anti = triangles()
    lower = as_low(causal)
    upper = as_low(anti)
    expand = ex[...]
    expand_t = ext[...]
    dsk_e = mm2(dsk[...], expand)

    def head_sum(v):
        return mm2(v, expand_t)

    states[0] = st_in[...]

    def forward(b, carry):
        r = pl.ds(pl.multiple_of(b * Q, Q), Q)
        marks = colm[r]
        dt = softplus(dtr[r] + dtb[...])
        cum = mm3_left(lower, dt * a_neg)
        last = cum[Q - 1 : Q]
        tail = jnp.exp(last - cum) * marks[:, 6:7] * dt
        keep_e = mm2(jnp.exp(last) * marks[Q - 1 : Q, 5:6], expand)
        tail_e = mm2(tail, expand)
        pieces = []
        for c in range(6):
            lanes = slice(c * 128, c * 128 + 128)
            pre = pre_r[r, lanes]
            act = pre * sigmoid(pre)
            acts[r, lanes] = act
            if c < 4:
                pieces.append((act * tail_e[:, lanes]).astype(BF))
            if c == 4:
                b_low = act.astype(BF)
        fresh = mm_tn(b_low, jnp.concatenate(pieces, axis=1))
        states[b + 1] = keep_e * states[b] + fresh
        return carry

    lax.fori_loop(0, 7, forward, 0)
    r7 = slice(7 * Q, 8 * Q)
    for c in range(6):
        lanes = slice(c * 128, c * 128 + 128)
        pre = pre_r[r7, lanes]
        acts[r7, lanes] = pre * sigmoid(pre)
    grad[...] = g_in[...]
    heads[...] = jnp.zeros_like(heads)
    dpre[0:8] = jnp.zeros((8, 768), F32)
    dpre[1032:1040] = jnp.zeros((8, 768), F32)

    def backward(i, carry):
        b = 7 - i
        r = pl.ds(pl.multiple_of(b * Q, Q), Q)
        rp = pl.ds(pl.multiple_of(b * Q + 8, 8), Q)
        marks = colm[r]
        raw = dtr[r] + dtb[...]
        dt = softplus(raw)
        cum = mm3_left(lower, dt * a_neg)
        cum_t = cum.T
        last = cum[Q - 1 : Q]
        enter = jnp.exp(cum) * marks[:, 5:6]
        tail = jnp.exp(last - cum) * marks[:, 6:7]
        dt_e = mm2(dt, expand)
        enter_e = mm2(enter, expand)
        tail_e = mm2(tail, expand)
        keep_e = enter_e[Q - 1 : Q]
        b_low = acts[r, 512:640].astype(BF)
        c_low = acts[r, 640:768].astype(BF)
        state = states[b]
        state_low = state.astype(BF)
        g_now = grad[...]
        g_low = g_now.astype(BF)
        inter = mm(c_low, state_low)
        back = mm(b_low, g_low)
        mask = causal & (marks[:, 0:1] == segr[pl.ds(b, 1), :])
        scores = jnp.where(mask, mm_nt(c_low, b_low), 0.0)
        kept = jnp.sum(state * g_now, axis=0, keepdims=True) * keep_e
        entered, tailed, e_terms, q_terms, x_terms, k_terms = [], [], [], [], [], []
        rows, cols = [], []
        d_scores = jnp.zeros((Q, Q), F32)
        for p in range(4):
            lanes = slice(p * 128, p * 128 + 128)
            x = acts[r, lanes]
            dys = dy[r, lanes]
            xdt = x * dt_e[:, lanes]
            xdt_low = xdt.astype(BF)
            ed = enter_e[:, lanes] * dys
            tx = tail_e[:, lanes] * xdt
            entered.append(ed.astype(BF))
            tailed.append(tx.astype(BF))
            dy_two = halves(dys.astype(BF))
            dw_two = mm_nt(dy_two, xdt_low)
            ws = []
            for k in range(2):
                h = 2 * p + k
                decay = jnp.exp(jnp.minimum(cum[:, h : h + 1] - cum_t[h : h + 1, :], 0.0))
                weight = decay * scores
                dw = dw_two[k * Q : k * Q + Q]
                d_scores = d_scores + decay * dw
                both = weight * dw
                rows.append(jnp.sum(both, axis=1, keepdims=True))
                cols.append(jnp.sum(both, axis=0, keepdims=True))
                ws.append(weight.astype(BF))
            dxdt = mm_tn(jnp.concatenate(ws, axis=0), dy_two) + tail_e[:, lanes] * back[:, lanes]
            e_terms.append(ed * inter[:, lanes] - tx * back[:, lanes])
            q_terms.append(jnp.sum(tx * back[:, lanes], axis=0, keepdims=True) + kept[:, lanes])
            x_terms.append(dxdt * x)
            k_terms.append(jnp.sum(dys * x, axis=0, keepdims=True))
            pre = pre_r[r, lanes]
            sig = sigmoid(pre)
            dpre[rp, lanes] = (dxdt * dt_e[:, lanes] + dsk_e[:, lanes] * dys) * (sig * (1.0 + pre * (1.0 - sig)))
        entered = jnp.concatenate(entered, axis=1)
        tailed = jnp.concatenate(tailed, axis=1)
        ds_low = jnp.where(mask, d_scores, 0.0).astype(BF)
        d_c = mm_nt(entered, state_low) + mm(ds_low, b_low)
        d_b = mm_nt(tailed, g_low) + mm_tn(ds_low, c_low)
        grad[...] = keep_e * g_now + mm_tn(c_low, entered)
        for c, value in ((4, d_b), (5, d_c)):
            lanes = slice(c * 128, c * 128 + 128)
            pre = pre_r[r, lanes]
            sig = sigmoid(pre)
            dpre[rp, lanes] = value * (sig * (1.0 + pre * (1.0 - sig)))
        d_cum = jnp.concatenate(rows, axis=1) - jnp.concatenate(cols, axis=0).T
        d_cum = d_cum + head_sum(jnp.concatenate(e_terms, axis=1))
        d_log = mm3_left(upper, d_cum) + head_sum(jnp.concatenate(q_terms, axis=1))
        d_dt = d_log * a_neg + head_sum(jnp.concatenate(x_terms, axis=1))
        d_raw = d_dt * sigmoid(raw)
        ddt_o[r] = d_raw
        heads[0:1] += jnp.sum(d_raw, axis=0, keepdims=True)
        heads[1:2] += jnp.sum(d_log * dt, axis=0, keepdims=True) * a_neg
        heads[2:3] += head_sum(jnp.concatenate(k_terms, axis=1))
        return carry

    lax.fori_loop(0, 8, backward, 0)
    small_o[...] = jnp.zeros_like(small_o)
    small_o[24:32, 0:8] = heads[...]

    for c in range(6):
        lanes = slice(c * 128, c * 128 + 128)
        first = dpre[0:16, lanes]
        flags = jnp.concatenate([jnp.zeros((8, 8), F32), colm[0:8]], axis=0)
        total = jnp.zeros((8, 128), F32)
        for d in range(1, 4):
            total = total + cw[3 - d : 4 - d, lanes] * (first * flags[:, d : d + 1])[d : d + 8]
        ret_o[:, lanes] = total

        def conv(b, sums, lanes=lanes, c=c):
            r = pl.ds(pl.multiple_of(b * Q, Q), Q)
            slab = dpre[pl.ds(pl.multiple_of(b * Q + 8, 8), Q + 8), lanes]
            marks = colm[pl.ds(pl.multiple_of(b * Q, Q), Q + 8)]
            xin = xbc[pl.ds(pl.multiple_of(b * Q, Q), Q + EDGE), lanes].astype(F32)
            main = slab[0:Q]
            out = cw[3:4, lanes] * main
            new = [sums[0] + jnp.sum(main, axis=0, keepdims=True),
                   sums[1] + jnp.sum(main * xin[EDGE:], axis=0, keepdims=True)]
            for d in range(1, 4):
                masked = slab * marks[:, d : d + 1]
                out = out + cw[3 - d : 4 - d, lanes] * masked[d : d + Q]
                new.append(sums[d + 1] + jnp.sum(masked[0:Q] * xin[EDGE - d : Q + EDGE - d], axis=0, keepdims=True))
            if c < 4:
                dx_o[r, lanes] = out.astype(BF)
            else:
                dbc_o[r, slice(c * 128 - 512, c * 128 - 384)] = out

            @pl.when(b == 7)
            def _():
                tail_o[:, lanes] = out[Q - EDGE :]

            return tuple(new)

        zero = jnp.zeros((1, 128), F32)
        sums = lax.fori_loop(0, 8, conv, (zero,) * 5)
        at = 16 + c if c < 4 else 36 + c
        small_o[at : at + 1] = sums[0]
        for d in range(4):
            at = (3 - d) * 4 + c if c < 4 else 28 + (3 - d) * 2 + c
            small_o[at : at + 1] = sums[d + 1]


MESH = pl.DeviceIdType.MESH


class Links:
    def __init__(self, send, recv):
        self.send, self.recv, self.count, self.started = send, recv, 0, []

    def copy(self, src, dst, device):
        made = pltpu.make_async_remote_copy(
            src_ref=src,
            dst_ref=dst,
            send_sem=self.send.at[self.count],
            recv_sem=self.recv.at[self.count],
            device_id=device,
            device_id_type=MESH,
        )
        self.count += 1
        self.started.append(made)
        made.start()
        return made

    def finish(self):
        for made in self.started:
            made.wait_send()


def arrival(like, dst, links_recv, device):
    return pltpu.make_async_remote_copy(
        src_ref=dst, dst_ref=dst, send_sem=links_recv, recv_sem=links_recv, device_id=device, device_id_type=MESH
    )


def greet(devices):
    barrier = pltpu.get_barrier_semaphore()
    for device in devices:
        pl.semaphore_signal(barrier, inc=1, device_id=device, device_id_type=MESH)
    pl.semaphore_wait(barrier, len(devices))


def places():
    shard, context, tensor = (lax.axis_index(name) for name in ("shard", "context", "tensor"))
    core, chip = lax.rem(shard, 2), lax.div(shard, 2)

    def at(shard_to=None, context_to=None, tensor_to=None):
        return (
            shard if shard_to is None else shard_to,
            context if context_to is None else context_to,
            tensor if tensor_to is None else tensor_to,
        )

    chips = [None] + [lax.rem(chip + k, 8) for k in range(1, 8)]
    sibling = at(shard_to=chip * 2 + (1 - core))
    others = [None] + [at(shard_to=c * 2 + core) for c in chips[1:]]
    partner = at(context_to=1 - context)
    ranks = [None] + [lax.rem(tensor + k, 4) for k in range(1, 4)]
    group = [None] + [at(tensor_to=t) for t in ranks[1:]]
    return shard, context, tensor, core, chip, chips, sibling, others, partner, ranks, group


def gather_kernel(wz, wx, wbc, wdt, norm, wo, etok, eseg, all_o, etok_o, eseg_o, mine, etok_b, send, recv):
    shard, context, tensor, core, chip, chips, sibling, others, partner, ranks, group = places()
    mine[:, 0:512] = wz[...]
    mine[:, 512:1024] = wx[...]
    mine[:, 1024:1280] = wbc[...]
    mine[:, 1280:1408] = jnp.zeros((64, 128), BF)
    mine[:, 1280:1288] = wdt[...]
    mine[:, 1288:1289] = norm[...]
    mine[:, 1408:1920] = wo[...]
    greet([sibling, partner] + others[1:])
    links = Links(send, recv)
    tokens_in = links.copy(etok, etok_b, partner)
    seg_in = links.copy(eseg, eseg_o, partner)
    first = [None]
    for k in range(1, 8):
        first.append(links.copy(mine, all_o.at[shard], others[k]))
    base = links.count
    links.copy(mine, all_o.at[shard], sibling)
    all_o[shard] = mine[...]
    for k in (1, 7, 2, 6, 3, 5, 4):
        source = lax.rem(chip + 8 - k, 8) * 2 + core
        slot = all_o.at[source]
        arrival(mine, slot, recv.at[1 + k], others[k]).wait_recv()
        links.copy(slot, slot, sibling)
    for n, k in enumerate((0, 1, 7, 2, 6, 3, 5, 4)):
        source = lax.rem(chip + 8 - k, 8) * 2 + (1 - core)
        arrival(mine, all_o.at[source], recv.at[base + n], sibling).wait_recv()
    tokens_in.wait_recv()
    seg_in.wait_recv()
    links.finish()
    etok_o[...] = jnp.where(context > 0, etok_b[...].astype(F32), 0.0).astype(BF)


def tail_kernel(
    part, branch, dbc, gz, gx, go, gd, small, gate, gain, tok, cot, xn, w,
    out_o, dtok_o, oz, ox, oo, odt, obc, onorm, small_o,
    rp, rbc, rb, sz, sx, so, sd, chunk, rg, cs, cr,
    g2, s2, chunk2, rg2, c2s, c2r, t2,
    sm, sm_s, sm_c, sm_x, sm_r, sm_t,
    tok_r, cot_r, xn_r, wbc, send, recv, local_sem,
):
    shard, context, tensor, core, chip, chips, sibling, others, partner, ranks, group = places()
    own = pl.ds(pl.multiple_of(tensor * 256, 256), 256)
    fetch = [
        pltpu.make_async_copy(tok.at[own], tok_r, local_sem.at[0]),
        pltpu.make_async_copy(cot.at[own], cot_r, local_sem.at[1]),
        pltpu.make_async_copy(xn.at[own], xn_r, local_sem.at[2]),
        pltpu.make_async_copy(w.at[:, pl.ds(1024, 256)], wbc, local_sem.at[3]),
    ]
    for copy in fetch:
        copy.start()
    greet([sibling, partner] + others[1:] + group[1:])
    links = Links(send, recv)
    sm[...] = small[...]
    sm[20:24] = gate[...]
    rows = [None] + [pl.ds(pl.multiple_of(t * 256, 256), 256) for t in ranks[1:]]
    dbc_in = [links.copy(dbc.at[rows[k]], rbc.at[k - 1], group[k]) for k in range(1, 4)]
    part_in = [links.copy(part.at[rows[k]], rp.at[k - 1], group[k]) for k in range(1, 4)]
    sib_in = [
        links.copy(sm, sm_s, sibling),
        links.copy(gz.at[:, 1 - core], sz, sibling),
        links.copy(gx.at[:, 1 - core], sx, sibling),
        links.copy(go.at[:, 1 - core], so, sibling),
        links.copy(gd.at[:, 1 - core], sd, sibling),
    ]
    branch_in = [links.copy(branch.at[rows[k]], rb.at[k - 1], group[k]) for k in range(1, 4)]
    for copy in sib_in:
        copy.wait_recv()
    sm_c[chip] = sm[...] + sm_s[...]
    small_in = [links.copy(sm_c.at[chip], sm_c.at[chip], others[k]) for k in range(1, 8)]
    small_base = links.count - 8

    def merge(c, carry):
        for mine, theirs, at in ((gz, sz, 0), (gx, sx, 512), (go, so, 1024)):
            chunk[c, :, at : at + 512] = (mine[c, core].astype(F32) + theirs[c].astype(F32)).astype(BF)
        chunk[c, :, 1536:1664] = (gd[c, core].astype(F32) + sd[c].astype(F32)).astype(BF)
        return carry

    lax.fori_loop(0, 8, merge, 0)
    grads_in = [links.copy(chunk.at[chips[k]], rg.at[k - 1], others[k]) for k in range(1, 8)]

    for copy in fetch:
        copy.wait()
    for copy in dbc_in + part_in:
        copy.wait_recv()
    ones = jnp.full((64, 128), 1.0, BF)

    def slice_rows(i):
        r = pl.ds(pl.multiple_of(i * 64, 64), 64)
        rt = pl.ds(pl.multiple_of(tensor * 256 + i * 64, 64), 64)
        return r, rt

    def inner(i, carry):
        r, rt = slice_rows(i)
        d_bc = dbc[rt].astype(F32) + rbc[0, r].astype(F32) + rbc[1, r].astype(F32) + rbc[2, r].astype(F32)
        d_bc_low = d_bc.astype(BF)
        total = part[rt].astype(F32) + rp[0, r].astype(F32) + rp[1, r].astype(F32) + rp[2, r].astype(F32)
        total = total + mm_nt(d_bc_low, wbc[...])
        plain = tok_r[r].astype(F32)
        root = lax.rsqrt(jnp.mean(plain * plain, axis=1, keepdims=True) + EPSILON)
        stat = plain * root
        d_plain = total * gain[...]
        mean = jnp.mean(d_plain * plain, axis=1, keepdims=True)
        dtok_o[rt] = (cot_r[r].astype(F32) + root * d_plain - stat * (root * root) * mean).astype(BF)
        g_bc, g_norm = carry
        g_bc = g_bc + mm_tn(xn_r[r], d_bc_low)
        g_norm = g_norm + mm_tn((total * stat).astype(BF), ones)
        return g_bc, g_norm

    g_bc, g_norm = lax.fori_loop(0, 4, inner, (jnp.zeros((1024, 256), F32), jnp.zeros((1024, 128), F32)))
    g2[:, :, :, 0:256] = g_bc.astype(BF).reshape(8, 2, 64, 256)
    g2[:, :, :, 256:384] = g_norm.astype(BF).reshape(8, 2, 64, 128)
    sib2_in = links.copy(g2.at[:, 1 - core], s2, sibling)
    mine_rows = dtok_o.at[own]
    dtok_base = links.count
    for k in range(1, 4):
        links.copy(mine_rows, mine_rows, group[k])
    sib2_in.wait_recv()
    for c in range(8):
        chunk2[c] = (g2[c, core].astype(F32) + s2[c].astype(F32)).astype(BF)
    grads2_in = [links.copy(chunk2.at[chips[k]], rg2.at[k - 1], others[k]) for k in range(1, 8)]

    for copy in branch_in:
        copy.wait_recv()

    def finish_out(i, carry):
        r, rt = slice_rows(i)
        total = branch[rt].astype(F32) + rb[0, r].astype(F32) + rb[1, r].astype(F32) + rb[2, r].astype(F32)
        out_o[rt] = (tok_r[r].astype(F32) + total).astype(BF)
        return carry

    lax.fori_loop(0, 4, finish_out, 0)
    out_rows = out_o.at[own]
    out_base = links.count
    for k in range(1, 4):
        links.copy(out_rows, out_rows, group[k])

    for k in range(1, 8):
        source = lax.rem(chip + 8 - k, 8)
        arrival(None, sm_c.at[source], recv.at[small_base + k], others[k]).wait_recv()
    total = sm_c[0]
    for c in range(1, 8):
        total = total + sm_c[c]
    sm_x[...] = total
    small_ctx = links.copy(sm_x, sm_r, partner)
    for copy in grads_in:
        copy.wait_recv()
    for at in range(0, 1664, 128):
        lanes = slice(at, at + 128)
        acc = chunk[chip, :, lanes].astype(F32)
        for k in range(7):
            acc = acc + rg[k, :, lanes].astype(F32)
        cs[:, lanes] = acc.astype(BF)
    grads_ctx = links.copy(cs, cr, partner)
    for copy in grads2_in:
        copy.wait_recv()
    for at in range(0, 384, 128):
        lanes = slice(at, at + 128)
        acc = chunk2[chip, :, lanes].astype(F32)
        for k in range(7):
            acc = acc + rg2[k, :, lanes].astype(F32)
        c2s[:, lanes] = acc
    grads2_ctx = links.copy(c2s, c2r, partner)
    small_ctx.wait_recv()
    sums = sm_x[...] + sm_r[...]
    small_o[0:32] = sums[0:32]
    sm_t[tensor] = sums[32:48]
    small_t = links.count
    for k in range(1, 4):
        links.copy(sm_t.at[tensor], sm_t.at[tensor], group[k])
    grads2_ctx.wait_recv()
    t2[tensor] = c2s[...] + c2r[...]
    grads2_t = links.count
    for k in range(1, 4):
        links.copy(t2.at[tensor], t2.at[tensor], group[k])
    grads_ctx.wait_recv()
    oz[...] = cs[:, 0:512].astype(F32) + cr[:, 0:512].astype(F32)
    ox[...] = cs[:, 512:1024].astype(F32) + cr[:, 512:1024].astype(F32)
    oo[...] = cs[:, 1024:1536].astype(F32) + cr[:, 1024:1536].astype(F32)
    odt[...] = cs[:, 1536:1664].astype(F32) + cr[:, 1536:1664].astype(F32)
    for k in range(1, 4):
        source = lax.rem(tensor + 4 - k, 4)
        arrival(None, sm_t.at[source], recv.at[small_t + k - 1], group[k]).wait_recv()
        arrival(None, t2.at[source], recv.at[grads2_t + k - 1], group[k]).wait_recv()
    small_o[32:48] = (sm_t[0] + sm_t[1]) + (sm_t[2] + sm_t[3])
    both = (t2[0] + t2[1]) + (t2[2] + t2[3])
    obc[...] = both[:, 0:256]
    onorm[...] = both[:, 256:384]
    for k in range(1, 4):
        source = pl.ds(pl.multiple_of(lax.rem(tensor + 4 - k, 4) * 256, 256), 256)
        arrival(None, dtok_o.at[source], recv.at[dtok_base + k - 1], group[k]).wait_recv()
        arrival(None, out_o.at[source], recv.at[out_base + k - 1], group[k]).wait_recv()
    links.finish()


def passed_along(value, axis, by):
    count = lax.axis_size(axis)
    pairs = [(i, i + by) for i in range(count) if 0 <= i + by < count]
    return lax.ppermute(value, axis, pairs)


def against(left, right):
    return lax.dot_general(
        left, right, (((1,), (1,)), ((), ())), preferred_element_type=jnp.float32
    )


def over_rows(left, right):
    return lax.dot_general(
        left, right, (((0,), (0,)), ((), ())), preferred_element_type=jnp.float32
    )


def silu_slope(value):
    sigma = jax.nn.sigmoid(value)
    return sigma * (1.0 + value * (1.0 - sigma))


def call(kernel, out_shapes, scratch, *args, specs=None, collective_id=None):
    return pl.pallas_call(
        kernel,
        out_shape=[jax.ShapeDtypeStruct(s, d) for s, d in out_shapes],
        in_specs=[pl.BlockSpec(memory_space=pl.ANY if n in (specs or ()) else pltpu.VMEM) for n in range(len(args))],
        out_specs=[pl.BlockSpec(memory_space=pltpu.VMEM)] * len(out_shapes),
        scratch_shapes=[pltpu.SemaphoreType.DMA(s) if d is None else pltpu.VMEM(s, d) for s, d in scratch],
        compiler_params=pltpu.CompilerParams(vmem_limit_bytes=VMEM_LIMIT, collective_id=collective_id, has_side_effects=collective_id is not None
        ),
    )(*args)


def local(
    tokens,
    segment,
    norm_gain,
    w_z,
    w_x,
    w_dt,
    w_bc,
    conv_x,
    conv_xb,
    conv_bc,
    conv_bcb,
    dt_bias,
    a_log,
    d_skip,
    gate_gain,
    w_out,
    cotangent,
):
    length = tokens.shape[0]
    head_count = dt_bias.shape[0]
    inner_width = head_count * HEADDIM
    bc_width = 2 * STATE
    seg = segment
    w_all, edge_tokens, edge_segs = call(
        gather_kernel,
        [((16, 64, 1920), BF), ((EDGE, 1024), BF), ((8, 128), jnp.int32)],
        [((64, 1920), BF), ((EDGE, 1024), BF), ((24,), None), ((24,), None)],
        w_z, w_x, w_bc, w_dt, norm_gain[:, None], w_out, tokens[length - EDGE :], seg.reshape(8, 128),
        collective_id=1,
    )
    w_all = w_all.reshape(1024, 1920)
    out_all = w_all[:, 1408:]
    edge_ids = jnp.where(lax.axis_index("context") > 0, edge_segs[7, 112:], 0)
    ext_ids = jnp.concatenate([edge_ids[-3:], seg])
    start_seg = jnp.where(edge_ids[-1] == seg[0], seg[0], -1)
    blocks = seg.reshape(length // Q, Q)
    before = jnp.concatenate([start_seg[None], blocks[:-1, -1]])
    marks = [seg.astype(F32)]
    marks += [(ext_ids[3 - d : 3 - d + length] == seg).astype(F32) for d in (1, 2, 3)]
    marks += [(seg == start_seg).astype(F32)]
    marks += [(blocks == before[:, None]).astype(F32).reshape(-1)]
    marks += [(blocks == blocks[:, -1:]).astype(F32).reshape(-1)]
    marks += [jnp.zeros((length,), F32)]
    colm = jnp.pad(jnp.stack(marks, axis=1), ((0, 8), (0, 0)))
    segr = blocks.astype(F32)
    conv_w = jnp.concatenate([conv_x, conv_bc], axis=1)
    conv_b = jnp.concatenate([conv_xb, conv_bcb])[None]
    expand_np = np.kron(np.eye(8), np.ones((1, HEADDIM)))
    expand = jnp.asarray(expand_np, BF)
    expand_t = jnp.asarray(expand_np.T, BF)
    wide = (length, inner_width)
    x_normed, z_gate, xbc, pre, dt_raw, y_zero, enter_decay, c_act, state_local, gain_row = call(
        front_kernel,
        [((length, 1024), BF), (wide, F32), ((length + EDGE, 768), BF), ((length, 768), F32), ((length, 8), F32),
         (wide, F32), ((length, 8), F32), ((length, STATE), BF), ((STATE, inner_width), F32), ((1, 1024), F32)],
        [((length + EDGE, 768), F32)],
        tokens, edge_tokens, w_all, colm, segr, conv_w, conv_b, dt_bias[None], a_log[None], d_skip[None], expand,
    )
    state_in = passed_along(state_local, "context", 1)
    decay_e = jnp.repeat(enter_decay, HEADDIM, axis=1)
    y_mixed = y_zero + decay_e * jnp.dot(c_act, state_in.astype(BF), preferred_element_type=F32)
    gate_act = jax.nn.silu(z_gate)
    gated = y_mixed * gate_act
    d_y_normed = jnp.dot(cotangent, out_all, preferred_element_type=F32)
    d_scaled = d_y_normed * gate_gain[None, :]
    sums = lax.psum(jnp.stack([jnp.sum(gated * gated, axis=1), jnp.sum(d_scaled * gated, axis=1)]), "tensor")
    gate_root = lax.rsqrt(sums[0] / INNER + EPSILON)[:, None]
    y_normed = (gated * gate_root * gate_gain[None, :]).astype(BF)
    branch_part = against(y_normed, out_all).astype(BF)
    g_w_out = over_rows(cotangent, y_normed).astype(BF)
    g_gate_gain = jnp.sum(d_y_normed * gated * gate_root, axis=0)
    d_gated = gate_root * d_scaled - gated * gate_root**3 * (sums[1] / INNER)[:, None]
    d_y = d_gated * gate_act
    d_z = (d_gated * y_mixed * silu_slope(z_gate)).astype(BF)
    d_carry = over_rows(c_act, (d_y * decay_e).astype(BF)).astype(BF)
    d_state_out = passed_along(d_carry, "context", -1).astype(F32)
    d_x_first, d_bc_first, tail_rows, back_rows, d_dt_raw, small = call(
        back_kernel,
        [(wide, BF), ((length, bc_width), F32), ((EDGE, 768), F32), ((8, 768), F32), ((length, 8), F32),
         ((48, 128), F32)],
        [((8, STATE, inner_width), F32), ((length, 768), F32), ((length + 16, 768), F32), ((STATE, inner_width), F32), ((8, 8), F32)],
        d_y, colm, segr, xbc, pre, dt_raw, state_in, d_state_out, conv_w, dt_bias[None], a_log[None], d_skip[None], expand, expand_t,
    )
    returned = passed_along(back_rows, "context", -1)
    tail_rows = tail_rows + jnp.pad(returned, ((EDGE - 8, 0), (0, 0)))
    d_x_low = lax.dynamic_update_slice(d_x_first, tail_rows[:, :inner_width].astype(BF), (length - EDGE, 0))
    d_bc = lax.dynamic_update_slice(d_bc_first, tail_rows[:, inner_width:], (length - EDGE, 0))
    d_bc = d_bc.astype(BF)
    d_dt_low = jnp.pad(d_dt_raw.astype(BF), ((0, 0), (0, 120)))
    gates = jnp.concatenate([d_z, d_x_low], axis=1)
    part_in = (against(gates, w_all[:, :1024]) + against(d_dt_low, w_all[:, 1280:1408])).astype(BF)
    g_w_z = over_rows(x_normed, d_z).astype(BF)
    g_w_x = over_rows(x_normed, d_x_low).astype(BF)
    g_w_dt = over_rows(x_normed, d_dt_low).astype(BF)
    grid = (8, 2, 64)
    output, d_tokens, o_z, o_x, o_out, o_dt, o_bc, o_norm, total = call(
        tail_kernel,
        [((length, 1024), BF), ((length, 1024), BF), ((64, 512), F32), ((64, 512), F32), ((64, 512), F32), ((64, 128), F32),
         ((64, 256), F32), ((64, 128), F32), ((48, 128), F32)],
        [((3, 256, 1024), BF), ((3, 256, 256), BF), ((3, 256, 1024), BF),
         ((8, 64, 512), BF), ((8, 64, 512), BF), ((8, 64, 512), BF), ((8, 64, 128), BF), ((8, 64, 1664), BF), ((7, 64, 1664), BF),
         ((64, 1664), BF), ((64, 1664), BF),
         ((8, 2, 64, 384), BF), ((8, 64, 384), BF), ((8, 64, 384), BF), ((7, 64, 384), BF),
         ((64, 384), F32), ((64, 384), F32), ((4, 64, 384), F32),
         ((48, 128), F32), ((48, 128), F32), ((8, 48, 128), F32), ((48, 128), F32), ((48, 128), F32), ((4, 16, 128), F32),
         ((256, 1024), BF), ((256, 1024), BF), ((256, 1024), BF), ((1024, 256), BF),
         ((64,), None), ((64,), None), ((4,), None)],
        part_in, branch_part, d_bc, g_w_z.reshape(grid + (512,)), g_w_x.reshape(grid + (512,)), g_w_out.reshape(grid + (512,)),
        g_w_dt.reshape(grid + (128,)), small, g_gate_gain.reshape(4, 128), gain_row, tokens, cotangent, x_normed, w_all,
        specs=(10, 11, 12, 13), collective_id=2,
    )
    return (
        output,
        d_tokens,
        o_norm[:, 0],
        o_z,
        o_x,
        o_dt[:, 0:8],
        o_bc,
        total[0:16].reshape(CONV, inner_width),
        total[16:20].reshape(inner_width),
        total[32:40].reshape(CONV, bc_width),
        total[40:42].reshape(bc_width),
        total[24, 0:8],
        total[25, 0:8],
        total[26, 0:8],
        total[20:24].reshape(inner_width),
        o_out,
    )


def solution(mesh):
    in_specs = (
        P(("shard", "context"), None),
        P(("shard", "context")),
        P("shard"),
        P("shard", "tensor"),
        P("shard", "tensor"),
        P("shard", "tensor"),
        P("shard", None),
        P(None, "tensor"),
        P("tensor"),
        P(),
        P(),
        P("tensor"),
        P("tensor"),
        P("tensor"),
        P("tensor"),
        P("shard", "tensor"),
        P(("shard", "context"), None),
    )
    out_specs = (
        P(("shard", "context"), None),
        P(("shard", "context"), None),
        P("shard"),
        P("shard", "tensor"),
        P("shard", "tensor"),
        P("shard", "tensor"),
        P("shard", None),
        P(None, "tensor"),
        P("tensor"),
        P(),
        P(),
        P("tensor"),
        P("tensor"),
        P("tensor"),
        P("tensor"),
        P("shard", "tensor"),
    )
    return jax.shard_map(local, mesh=mesh, in_specs=in_specs, out_specs=out_specs, check_vma=False)
```

```python
from functools import partial

import jax
import jax.numpy as jnp
import numpy as np
from jax import lax
from jax.experimental import pallas as pl
from jax.experimental.pallas import tpu as pltpu
from jax.sharding import PartitionSpec as P

HEADDIM = 64
STATE = 128
CONV = 4
INNER = 2048


EPSILON = 1e-05


F32 = jnp.float32
BF = jnp.bfloat16
Q = 128
EDGE = 16
VMEM_LIMIT = 58 * 1024 * 1024


def mm(a, b):
    return lax.dot_general(a, b, (((1,), (0,)), ((), ())), preferred_element_type=F32)


def mm_nt(a, b):
    return lax.dot_general(a, b, (((1,), (1,)), ((), ())), preferred_element_type=F32)


def mm_tn(a, b):
    return lax.dot_general(a, b, (((0,), (0,)), ((), ())), preferred_element_type=F32)


def split2(v):
    hi = v.astype(BF)
    return hi, (v - hi.astype(F32)).astype(BF)


def mm2(a, b):
    hi, lo = split2(a)
    return mm(hi, b) + mm(lo, b)


def mm3_left(a, b):
    hi, lo = split2(b)
    lo2 = (b - hi.astype(F32) - lo.astype(F32)).astype(BF)
    return mm(a, hi) + (mm(a, lo) + mm(a, lo2))


def softplus(v):
    return jnp.maximum(v, 0.0) + jnp.log1p(jnp.exp(-jnp.abs(v)))


def sigmoid(v):
    return 1.0 / (1.0 + jnp.exp(-v))


def triangles():
    rows = lax.broadcasted_iota(jnp.int32, (Q, Q), 0)
    cols = lax.broadcasted_iota(jnp.int32, (Q, Q), 1)
    return rows >= cols, rows <= cols


def as_low(mask):
    return jnp.where(mask, 1.0, 0.0).astype(BF)


def halves(slab):
    lane = lax.broadcasted_iota(jnp.int32, slab.shape, 1)
    zero = jnp.zeros_like(slab)
    first = jnp.where(lane < HEADDIM, slab, zero)
    second = jnp.where(lane >= HEADDIM, slab, zero)
    return jnp.concatenate([first, second], axis=0)


def front_kernel(
    tok, etok, w, colm, segr, cw, cb, dtb, alog, dsk, ex,
    xn_o, z_o, xbc_o, pre_o, dtr_o, y_o, er_o, c_o, st_o, gain_o, xs,
):
    a_neg = -jnp.exp(alog[...])
    causal, _ = triangles()
    lower = as_low(causal)
    gain_row = w[:, 1280:1408].astype(F32).T[8:9]
    gain_o[...] = gain_row

    def normed(block):
        plain = block.astype(F32)
        root = lax.rsqrt(jnp.mean(plain * plain, axis=1, keepdims=True) + EPSILON)
        return (plain * root * gain_row).astype(BF)

    edge = mm(normed(etok[...]), w[:, 512:1280]).astype(BF)
    xbc_o[0:EDGE] = edge
    xs[0:EDGE] = edge.astype(F32)
    st_o[...] = jnp.zeros_like(st_o)
    expand = ex[...]
    dsk_e = mm2(dsk[...], expand)

    def body(b, run):
        r = pl.ds(pl.multiple_of(b * Q, Q), Q)
        rn = pl.ds(pl.multiple_of(b * Q + EDGE, EDGE), Q)
        xn = normed(tok[r])
        xn_o[r] = xn
        z_o[r] = mm(xn, w[:, 0:512])
        xb = mm(xn, w[:, 512:1280]).astype(BF)
        xbc_o[rn] = xb
        xs[rn] = xb.astype(F32)
        raw = mm(xn, w[:, 1280:1408])[:, 0:8]
        dtr_o[r] = raw
        marks = colm[r]
        acts = []
        for c in range(6):
            lanes = slice(c * 128, c * 128 + 128)
            slab = xs[pl.ds(pl.multiple_of(b * Q, Q), Q + EDGE), lanes]
            pre = cb[:, lanes] + cw[3:4, lanes] * slab[EDGE:]
            for d in range(1, 4):
                pre = pre + (cw[3 - d : 4 - d, lanes] * slab[EDGE - d : Q + EDGE - d]) * marks[:, d : d + 1]
            pre_o[r, lanes] = pre
            acts.append(pre * sigmoid(pre))
        b_low = acts[4].astype(BF)
        c_low = acts[5].astype(BF)
        c_o[r] = c_low
        dt = softplus(raw + dtb[...])
        cum = mm3_left(lower, dt * a_neg)
        er_o[r] = jnp.exp(run + cum) * marks[:, 4:5]
        cum_t = cum.T
        last = cum[Q - 1 : Q]
        enter = jnp.exp(cum) * marks[:, 5:6]
        tail = jnp.exp(last - cum) * marks[:, 6:7]
        dt_e = mm2(dt, expand)
        enter_e = mm2(enter, expand)
        tail_e = mm2(tail, expand)
        mask = causal & (marks[:, 0:1] == segr[pl.ds(b, 1), :])
        scores = jnp.where(mask, mm_nt(c_low, b_low), 0.0)
        state = st_o[...]
        inter = mm(c_low, state.astype(BF))
        pieces = []
        for p in range(4):
            lanes = slice(p * 128, p * 128 + 128)
            xdt = acts[p] * dt_e[:, lanes]
            pieces.append((xdt * tail_e[:, lanes]).astype(BF))
            ws = []
            for h in (2 * p, 2 * p + 1):
                decay = jnp.exp(jnp.minimum(cum[:, h : h + 1] - cum_t[h : h + 1, :], 0.0))
                ws.append((decay * scores).astype(BF))
            intra = mm(jnp.concatenate(ws, axis=1), halves(xdt.astype(BF)))
            y_o[r, lanes] = intra + enter_e[:, lanes] * inter[:, lanes] + dsk_e[:, lanes] * acts[p]
        fresh = mm_tn(b_low, jnp.concatenate(pieces, axis=1))
        st_o[...] = enter_e[Q - 1 : Q] * state + fresh
        return run + last

    lax.fori_loop(0, 8, body, jnp.zeros((1, 8), F32))


def back_kernel(
    dy, colm, segr, xbc, pre_r, dtr, st_in, g_send, cw, dtb, alog, dsk, ex, ext, branch, tok,
    dx_o, dbc_o, ddt_o, small_o, out_o,
    states, acts, dpre, grad, heads, g_in, tail_r, ret_s, ret_r, near, relay, from_d, from_u, tok_r, send, recv, local_sem,
):
    shard, context, tensor, core, chip, chips, sibling, others, partner, ranks, group = places()
    own = pl.ds(pl.multiple_of(tensor * 256, 256), 256)
    fetch = pltpu.make_async_copy(tok.at[own], tok_r, local_sem.at[0])
    fetch.start()
    greet([partner, group[1], group[3]])
    links = Links(send, recv)
    carry_in = links.copy(g_send, g_in, partner)
    ring = Ring(links, tensor, group)
    ring.reduce_first(branch, near, from_d, from_u)
    a_neg = -jnp.exp(alog[...])
    causal, anti = triangles()
    lower = as_low(causal)
    upper = as_low(anti)
    expand = ex[...]
    expand_t = ext[...]
    dsk_e = mm2(dsk[...], expand)

    def head_sum(v):
        return mm2(v, expand_t)

    states[0] = st_in[...]

    def forward(b, carry):
        r = pl.ds(pl.multiple_of(b * Q, Q), Q)
        marks = colm[r]
        dt = softplus(dtr[r] + dtb[...])
        cum = mm3_left(lower, dt * a_neg)
        last = cum[Q - 1 : Q]
        tail = jnp.exp(last - cum) * marks[:, 6:7] * dt
        keep_e = mm2(jnp.exp(last) * marks[Q - 1 : Q, 5:6], expand)
        tail_e = mm2(tail, expand)
        pieces = []
        for c in range(6):
            lanes = slice(c * 128, c * 128 + 128)
            pre = pre_r[r, lanes]
            act = pre * sigmoid(pre)
            acts[r, lanes] = act
            if c < 4:
                pieces.append((act * tail_e[:, lanes]).astype(BF))
            if c == 4:
                b_low = act.astype(BF)
        fresh = mm_tn(b_low, jnp.concatenate(pieces, axis=1))
        states[b + 1] = keep_e * states[b] + fresh
        return carry

    lax.fori_loop(0, 7, forward, 0)
    r7 = slice(7 * Q, 8 * Q)
    for c in range(6):
        lanes = slice(c * 128, c * 128 + 128)
        pre = pre_r[r7, lanes]
        acts[r7, lanes] = pre * sigmoid(pre)
    carry_in.wait_recv()
    grad[...] = jnp.where(context == 0, g_in[...].astype(F32), 0.0)
    heads[...] = jnp.zeros_like(heads)
    dpre[0:8] = jnp.zeros((8, 768), F32)
    dpre[1032:1040] = jnp.zeros((8, 768), F32)

    def backward(i, carry):
        b = 7 - i
        r = pl.ds(pl.multiple_of(b * Q, Q), Q)
        rp = pl.ds(pl.multiple_of(b * Q + 8, 8), Q)
        marks = colm[r]
        raw = dtr[r] + dtb[...]
        dt = softplus(raw)
        cum = mm3_left(lower, dt * a_neg)
        cum_t = cum.T
        last = cum[Q - 1 : Q]
        enter = jnp.exp(cum) * marks[:, 5:6]
        tail = jnp.exp(last - cum) * marks[:, 6:7]
        dt_e = mm2(dt, expand)
        enter_e = mm2(enter, expand)
        tail_e = mm2(tail, expand)
        keep_e = enter_e[Q - 1 : Q]
        b_low = acts[r, 512:640].astype(BF)
        c_low = acts[r, 640:768].astype(BF)
        state = states[b]
        state_low = state.astype(BF)
        g_now = grad[...]
        g_low = g_now.astype(BF)
        inter = mm(c_low, state_low)
        back = mm(b_low, g_low)
        mask = causal & (marks[:, 0:1] == segr[pl.ds(b, 1), :])
        scores = jnp.where(mask, mm_nt(c_low, b_low), 0.0)
        kept = jnp.sum(state * g_now, axis=0, keepdims=True) * keep_e
        entered, tailed, e_terms, q_terms, x_terms, k_terms = [], [], [], [], [], []
        rows, cols = [], []
        d_scores = jnp.zeros((Q, Q), F32)
        for p in range(4):
            lanes = slice(p * 128, p * 128 + 128)
            x = acts[r, lanes]
            dys = dy[r, lanes]
            xdt = x * dt_e[:, lanes]
            xdt_low = xdt.astype(BF)
            ed = enter_e[:, lanes] * dys
            tx = tail_e[:, lanes] * xdt
            entered.append(ed.astype(BF))
            tailed.append(tx.astype(BF))
            dy_two = halves(dys.astype(BF))
            dw_two = mm_nt(dy_two, xdt_low)
            ws = []
            for k in range(2):
                h = 2 * p + k
                decay = jnp.exp(jnp.minimum(cum[:, h : h + 1] - cum_t[h : h + 1, :], 0.0))
                weight = decay * scores
                dw = dw_two[k * Q : k * Q + Q]
                d_scores = d_scores + decay * dw
                both = weight * dw
                rows.append(jnp.sum(both, axis=1, keepdims=True))
                cols.append(jnp.sum(both, axis=0, keepdims=True))
                ws.append(weight.astype(BF))
            dxdt = mm_tn(jnp.concatenate(ws, axis=0), dy_two) + tail_e[:, lanes] * back[:, lanes]
            e_terms.append(ed * inter[:, lanes] - tx * back[:, lanes])
            q_terms.append(jnp.sum(tx * back[:, lanes], axis=0, keepdims=True) + kept[:, lanes])
            x_terms.append(dxdt * x)
            k_terms.append(jnp.sum(dys * x, axis=0, keepdims=True))
            pre = pre_r[r, lanes]
            sig = sigmoid(pre)
            dpre[rp, lanes] = (dxdt * dt_e[:, lanes] + dsk_e[:, lanes] * dys) * (sig * (1.0 + pre * (1.0 - sig)))
        entered = jnp.concatenate(entered, axis=1)
        tailed = jnp.concatenate(tailed, axis=1)
        ds_low = jnp.where(mask, d_scores, 0.0).astype(BF)
        d_c = mm_nt(entered, state_low) + mm(ds_low, b_low)
        d_b = mm_nt(tailed, g_low) + mm_tn(ds_low, c_low)
        grad[...] = keep_e * g_now + mm_tn(c_low, entered)
        for c, value in ((4, d_b), (5, d_c)):
            lanes = slice(c * 128, c * 128 + 128)
            pre = pre_r[r, lanes]
            sig = sigmoid(pre)
            dpre[rp, lanes] = value * (sig * (1.0 + pre * (1.0 - sig)))
        d_cum = jnp.concatenate(rows, axis=1) - jnp.concatenate(cols, axis=0).T
        d_cum = d_cum + head_sum(jnp.concatenate(e_terms, axis=1))
        d_log = mm3_left(upper, d_cum) + head_sum(jnp.concatenate(q_terms, axis=1))
        d_dt = d_log * a_neg + head_sum(jnp.concatenate(x_terms, axis=1))
        d_raw = d_dt * sigmoid(raw)
        ddt_o[r] = d_raw
        heads[0:1] += jnp.sum(d_raw, axis=0, keepdims=True)
        heads[1:2] += jnp.sum(d_log * dt, axis=0, keepdims=True) * a_neg
        heads[2:3] += head_sum(jnp.concatenate(k_terms, axis=1))
        return carry

    lax.fori_loop(0, 1, backward, 0)
    ring.reduce_second(branch, near, relay, from_d, from_u)
    lax.fori_loop(1, 4, backward, 0)
    fetch.wait()
    ring.reduce_wait()

    def finish_out(i, carry):
        r = pl.ds(pl.multiple_of(i * 64, 64), 64)
        rt = pl.ds(pl.multiple_of(tensor * 256 + i * 64, 64), 64)
        total = branch[rt].astype(F32) + from_d[r].astype(F32) + from_u[r].astype(F32)
        out_o[rt] = (tok_r[r].astype(F32) + total).astype(BF)
        return carry

    lax.fori_loop(0, 4, finish_out, 0)
    ring.gather_first(out_o)
    lax.fori_loop(4, 8, backward, 0)
    small_o[...] = jnp.zeros_like(small_o)
    small_o[24:32, 0:8] = heads[...]

    for c in range(6):
        lanes = slice(c * 128, c * 128 + 128)
        first = dpre[0:16, lanes]
        flags = jnp.concatenate([jnp.zeros((8, 8), F32), colm[0:8]], axis=0)
        total = jnp.zeros((8, 128), F32)
        for d in range(1, 4):
            total = total + cw[3 - d : 4 - d, lanes] * (first * flags[:, d : d + 1])[d : d + 8]
        ret_s[:, lanes] = total
    ret_in = links.copy(ret_s, ret_r, partner)
    ring.gather_second(out_o)
    for c in range(6):
        lanes = slice(c * 128, c * 128 + 128)

        def conv(b, sums, lanes=lanes, c=c):
            r = pl.ds(pl.multiple_of(b * Q, Q), Q)
            slab = dpre[pl.ds(pl.multiple_of(b * Q + 8, 8), Q + 8), lanes]
            marks = colm[pl.ds(pl.multiple_of(b * Q, Q), Q + 8)]
            xin = xbc[pl.ds(pl.multiple_of(b * Q, Q), Q + EDGE), lanes].astype(F32)
            main = slab[0:Q]
            out = cw[3:4, lanes] * main
            new = [sums[0] + jnp.sum(main, axis=0, keepdims=True),
                   sums[1] + jnp.sum(main * xin[EDGE:], axis=0, keepdims=True)]
            for d in range(1, 4):
                masked = slab * marks[:, d : d + 1]
                out = out + cw[3 - d : 4 - d, lanes] * masked[d : d + Q]
                new.append(sums[d + 1] + jnp.sum(masked[0:Q] * xin[EDGE - d : Q + EDGE - d], axis=0, keepdims=True))
            if c < 4:
                dx_o[r, lanes] = out.astype(BF)
            else:
                dbc_o[r, slice(c * 128 - 512, c * 128 - 384)] = out.astype(BF)

            @pl.when(b == 7)
            def _():
                tail_r[:, lanes] = out[Q - EDGE :]

            return tuple(new)

        zero = jnp.zeros((1, 128), F32)
        sums = lax.fori_loop(0, 8, conv, (zero,) * 5)
        at = 16 + c if c < 4 else 36 + c
        small_o[at : at + 1] = sums[0]
        for d in range(4):
            at = (3 - d) * 4 + c if c < 4 else 28 + (3 - d) * 2 + c
            small_o[at : at + 1] = sums[d + 1]
    ret_in.wait_recv()
    returned = jnp.where(context == 0, ret_r[...], 0.0)
    last = tail_r[...] + jnp.concatenate([jnp.zeros((EDGE - 8, 768), F32), returned], axis=0)
    dx_o[1024 - EDGE : 1024] = last[:, 0:512].astype(BF)
    dbc_o[1024 - EDGE : 1024] = last[:, 512:768].astype(BF)
    ring.gather_wait(out_o)
    links.finish()


MESH = pl.DeviceIdType.MESH


class Links:
    def __init__(self, send, recv):
        self.send, self.recv, self.count, self.started = send, recv, 0, []

    def copy(self, src, dst, device):
        made = pltpu.make_async_remote_copy(
            src_ref=src,
            dst_ref=dst,
            send_sem=self.send.at[self.count],
            recv_sem=self.recv.at[self.count],
            device_id=device,
            device_id_type=MESH,
        )
        self.count += 1
        self.started.append(made)
        made.start()
        return made

    def finish(self):
        for made in self.started:
            made.wait_send()


def arrival(like, dst, links_recv, device):
    return pltpu.make_async_remote_copy(
        src_ref=dst, dst_ref=dst, send_sem=links_recv, recv_sem=links_recv, device_id=device, device_id_type=MESH
    )


def greet(devices):
    barrier = pltpu.get_barrier_semaphore()
    for device in devices:
        pl.semaphore_signal(barrier, inc=1, device_id=device, device_id_type=MESH)
    pl.semaphore_wait(barrier, len(devices))


def places():
    shard, context, tensor = (lax.axis_index(name) for name in ("shard", "context", "tensor"))
    core, chip = lax.rem(shard, 2), lax.div(shard, 2)

    def at(shard_to=None, context_to=None, tensor_to=None):
        return (
            shard if shard_to is None else shard_to,
            context if context_to is None else context_to,
            tensor if tensor_to is None else tensor_to,
        )

    chips = [None] + [lax.rem(chip + k, 8) for k in range(1, 8)]
    sibling = at(shard_to=chip * 2 + (1 - core))
    others = [None] + [at(shard_to=c * 2 + core) for c in chips[1:]]
    partner = at(context_to=1 - context)
    ranks = [None] + [lax.rem(tensor + k, 4) for k in range(1, 4)]
    group = [None] + [at(tensor_to=t) for t in ranks[1:]]
    return shard, context, tensor, core, chip, chips, sibling, others, partner, ranks, group


class Ring:
    def __init__(self, links, tensor, group):
        self.links, self.tensor = links, tensor
        self.up, self.down = group[1], group[3]
        self.t_up, self.t_down, self.t_far = (lax.rem(tensor + k, 4) for k in (1, 3, 2))

    def half(self, rank, which):
        return pl.ds(pl.multiple_of(rank * 256 + which * 128, 128), 128)

    def whole(self, rank):
        return pl.ds(pl.multiple_of(rank * 256, 256), 256)

    def reduce_first(self, src, near, from_down, from_up):
        copy = self.links.copy
        self.first = (
            copy(src.at[self.half(self.t_far, 0)], near.at[0], self.up),
            copy(src.at[self.half(self.t_far, 1)], near.at[1], self.down),
        )
        self.alone = (
            copy(src.at[self.half(self.t_up, 1)], from_down.at[pl.ds(128, 128)], self.up),
            copy(src.at[self.half(self.t_down, 0)], from_up.at[pl.ds(0, 128)], self.down),
        )

    def reduce_second(self, src, near, relay, from_down, from_up):
        copy = self.links.copy
        self.first[0].wait_recv()
        relay[0] = (near[0].astype(F32) + src[self.half(self.t_up, 0)].astype(F32)).astype(BF)
        up = copy(relay.at[0], from_down.at[pl.ds(0, 128)], self.up)
        self.first[1].wait_recv()
        relay[1] = (near[1].astype(F32) + src[self.half(self.t_down, 1)].astype(F32)).astype(BF)
        down = copy(relay.at[1], from_up.at[pl.ds(128, 128)], self.down)
        self.summed = (up, down)

    def reduce_wait(self):
        for made in self.alone + self.summed:
            made.wait_recv()

    def gather_first(self, ref):
        mine = ref.at[self.whole(self.tensor)]
        self.base = self.links.count
        self.links.copy(mine, mine, self.up)
        self.links.copy(mine, mine, self.down)

    def landed(self, slot, which, device):
        arrival(None, slot, self.links.recv.at[self.base + which], device).wait_recv()

    def gather_second(self, ref):
        self.landed(ref.at[self.whole(self.t_down)], 0, self.down)
        self.base2 = self.links.count
        up = ref.at[self.half(self.t_down, 0)]
        self.links.copy(up, up, self.up)
        self.landed(ref.at[self.whole(self.t_up)], 1, self.up)
        down = ref.at[self.half(self.t_up, 1)]
        self.links.copy(down, down, self.down)

    def gather_wait(self, ref):
        offset = self.base2 - self.base
        self.landed(ref.at[self.half(self.t_far, 0)], offset, self.down)
        self.landed(ref.at[self.half(self.t_far, 1)], offset + 1, self.up)


def gather_kernel(wz, wx, wbc, wdt, norm, wo, etok, eseg, all_o, etok_o, eseg_o, mine, etok_b, send, recv):
    shard, context, tensor, core, chip, chips, sibling, others, partner, ranks, group = places()
    mine[:, 0:512] = wz[...]
    mine[:, 512:1024] = wx[...]
    mine[:, 1024:1280] = wbc[...]
    mine[:, 1280:1408] = jnp.zeros((64, 128), BF)
    mine[:, 1280:1288] = wdt[...]
    mine[:, 1288:1289] = norm[...]
    mine[:, 1408:1920] = wo[...]
    greet([sibling, partner] + others[1:])
    links = Links(send, recv)
    tokens_in = links.copy(etok, etok_b, partner)
    seg_in = links.copy(eseg, eseg_o, partner)
    first = [None]
    for k in range(1, 8):
        first.append(links.copy(mine, all_o.at[shard], others[k]))
    base = links.count
    links.copy(mine, all_o.at[shard], sibling)
    all_o[shard] = mine[...]
    for k in (1, 7, 2, 6, 3, 5, 4):
        source = lax.rem(chip + 8 - k, 8) * 2 + core
        slot = all_o.at[source]
        arrival(mine, slot, recv.at[1 + k], others[k]).wait_recv()
        links.copy(slot, slot, sibling)
    for n, k in enumerate((0, 1, 7, 2, 6, 3, 5, 4)):
        source = lax.rem(chip + 8 - k, 8) * 2 + (1 - core)
        arrival(mine, all_o.at[source], recv.at[base + n], sibling).wait_recv()
    tokens_in.wait_recv()
    seg_in.wait_recv()
    links.finish()
    etok_o[...] = jnp.where(context > 0, etok_b[...].astype(F32), 0.0).astype(BF)


def tail_kernel(
    part, dbc, gz, gx, go, gd, small, gate, gain, tok, cot, xn, w,
    dtok_o, oz, ox, oo, odt, obc, onorm, conv_o, convb_o, bc_o, bcb_o, gate_o, heads_o,
    near, relay, from_d, from_u, near2, relay2, from_d2, from_u2, sz, sx, so, sd, chunk, rg, cs, cr,
    g2, s2, chunk2, rg2, c2s, c2r, t2,
    sm, sm_s, sm_c, sm_x, sm_r, sm_t,
    tok_r, cot_r, xn_r, wbc, send, recv, local_sem,
):
    shard, context, tensor, core, chip, chips, sibling, others, partner, ranks, group = places()
    own = pl.ds(pl.multiple_of(tensor * 256, 256), 256)
    fetch = [
        pltpu.make_async_copy(tok.at[own], tok_r, local_sem.at[0]),
        pltpu.make_async_copy(cot.at[own], cot_r, local_sem.at[1]),
        pltpu.make_async_copy(xn.at[own], xn_r, local_sem.at[2]),
        pltpu.make_async_copy(w.at[:, pl.ds(1024, 256)], wbc, local_sem.at[3]),
    ]
    for copy in fetch:
        copy.start()
    greet([sibling, partner] + others[1:] + group[1:])
    links = Links(send, recv)
    sm[...] = small[...]
    sm[20:24] = gate[...]
    wide, thin = Ring(links, tensor, group), Ring(links, tensor, group)
    thin.reduce_first(dbc, near2, from_d2, from_u2)
    wide.reduce_first(part, near, from_d, from_u)
    sib_in = [
        links.copy(sm, sm_s, sibling),
        links.copy(gz.at[:, 1 - core], sz, sibling),
        links.copy(gx.at[:, 1 - core], sx, sibling),
        links.copy(go.at[:, 1 - core], so, sibling),
        links.copy(gd.at[:, 1 - core], sd, sibling),
    ]
    thin.reduce_second(dbc, near2, relay2, from_d2, from_u2)
    for copy in sib_in:
        copy.wait_recv()
    sm_c[chip] = sm[...] + sm_s[...]
    small_in = [links.copy(sm_c.at[chip], sm_c.at[chip], others[k]) for k in range(1, 8)]
    small_base = links.count - 8

    def merge(c, carry):
        for mine, theirs, at in ((gz, sz, 0), (gx, sx, 512), (go, so, 1024)):
            chunk[c, :, at : at + 512] = (mine[c, core].astype(F32) + theirs[c].astype(F32)).astype(BF)
        chunk[c, :, 1536:1664] = (gd[c, core].astype(F32) + sd[c].astype(F32)).astype(BF)
        return carry

    lax.fori_loop(0, 8, merge, 0)
    wide.reduce_second(part, near, relay, from_d, from_u)
    grads_in = [links.copy(chunk.at[chips[k]], rg.at[k - 1], others[k]) for k in range(1, 8)]

    for copy in fetch:
        copy.wait()
    thin.reduce_wait()
    wide.reduce_wait()
    ones = jnp.full((64, 128), 1.0, BF)

    def slice_rows(i):
        r = pl.ds(pl.multiple_of(i * 64, 64), 64)
        rt = pl.ds(pl.multiple_of(tensor * 256 + i * 64, 64), 64)
        return r, rt

    def inner(i, carry):
        r, rt = slice_rows(i)
        d_bc = dbc[rt].astype(F32) + from_d2[r].astype(F32) + from_u2[r].astype(F32)
        d_bc_low = d_bc.astype(BF)
        total = part[rt].astype(F32) + from_d[r].astype(F32) + from_u[r].astype(F32)
        total = total + mm_nt(d_bc_low, wbc[...])
        plain = tok_r[r].astype(F32)
        root = lax.rsqrt(jnp.mean(plain * plain, axis=1, keepdims=True) + EPSILON)
        stat = plain * root
        d_plain = total * gain[...]
        mean = jnp.mean(d_plain * plain, axis=1, keepdims=True)
        dtok_o[rt] = (cot_r[r].astype(F32) + root * d_plain - stat * (root * root) * mean).astype(BF)
        g_bc, g_norm = carry
        g_bc = g_bc + mm_tn(xn_r[r], d_bc_low)
        g_norm = g_norm + mm_tn((total * stat).astype(BF), ones)
        return g_bc, g_norm

    g_bc, g_norm = lax.fori_loop(0, 4, inner, (jnp.zeros((1024, 256), F32), jnp.zeros((1024, 128), F32)))
    g2[:, :, :, 0:256] = g_bc.astype(BF).reshape(8, 2, 64, 256)
    g2[:, :, :, 256:384] = g_norm.astype(BF).reshape(8, 2, 64, 128)
    sib2_in = links.copy(g2.at[:, 1 - core], s2, sibling)
    wide.gather_first(dtok_o)
    sib2_in.wait_recv()
    for c in range(8):
        chunk2[c] = (g2[c, core].astype(F32) + s2[c].astype(F32)).astype(BF)
    grads2_in = [links.copy(chunk2.at[chips[k]], rg2.at[k - 1], others[k]) for k in range(1, 8)]

    for k in range(1, 8):
        source = lax.rem(chip + 8 - k, 8)
        arrival(None, sm_c.at[source], recv.at[small_base + k], others[k]).wait_recv()
    total = sm_c[0]
    for c in range(1, 8):
        total = total + sm_c[c]
    sm_x[...] = total
    small_ctx = links.copy(sm_x, sm_r, partner)
    for copy in grads_in:
        copy.wait_recv()
    for at in range(0, 1664, 128):
        lanes = slice(at, at + 128)
        acc = chunk[chip, :, lanes].astype(F32)
        for k in range(7):
            acc = acc + rg[k, :, lanes].astype(F32)
        cs[:, lanes] = acc.astype(BF)
    grads_ctx = links.copy(cs, cr, partner)
    wide.gather_second(dtok_o)
    for copy in grads2_in:
        copy.wait_recv()
    for at in range(0, 384, 128):
        lanes = slice(at, at + 128)
        acc = chunk2[chip, :, lanes].astype(F32)
        for k in range(7):
            acc = acc + rg2[k, :, lanes].astype(F32)
        c2s[:, lanes] = acc
    grads2_ctx = links.copy(c2s, c2r, partner)
    small_ctx.wait_recv()
    sums = sm_x[...] + sm_r[...]
    for k in range(4):
        for p in range(4):
            conv_o[k : k + 1, p * 128 : p * 128 + 128] = sums[k * 4 + p : k * 4 + p + 1]
    for p in range(4):
        convb_o[:, p * 128 : p * 128 + 128] = sums[16 + p : 17 + p]
        gate_o[:, p * 128 : p * 128 + 128] = sums[20 + p : 21 + p]
    heads_o[...] = sums[24:32]
    sm_t[tensor] = sums[32:48]
    small_t = links.count
    for k in range(1, 4):
        links.copy(sm_t.at[tensor], sm_t.at[tensor], group[k])
    grads2_ctx.wait_recv()
    t2[tensor] = c2s[...] + c2r[...]
    grads2_t = links.count
    for k in range(1, 4):
        links.copy(t2.at[tensor], t2.at[tensor], group[k])
    grads_ctx.wait_recv()
    oz[...] = cs[:, 0:512].astype(F32) + cr[:, 0:512].astype(F32)
    ox[...] = cs[:, 512:1024].astype(F32) + cr[:, 512:1024].astype(F32)
    oo[...] = cs[:, 1024:1536].astype(F32) + cr[:, 1024:1536].astype(F32)
    odt[...] = cs[:, 1536:1664].astype(F32) + cr[:, 1536:1664].astype(F32)
    for k in range(1, 4):
        source = lax.rem(tensor + 4 - k, 4)
        arrival(None, sm_t.at[source], recv.at[small_t + k - 1], group[k]).wait_recv()
        arrival(None, t2.at[source], recv.at[grads2_t + k - 1], group[k]).wait_recv()
    sums = (sm_t[0] + sm_t[1]) + (sm_t[2] + sm_t[3])
    for k in range(4):
        for p in range(2):
            bc_o[k : k + 1, p * 128 : p * 128 + 128] = sums[k * 2 + p : k * 2 + p + 1]
    for p in range(2):
        bcb_o[:, p * 128 : p * 128 + 128] = sums[8 + p : 9 + p]
    both = (t2[0] + t2[1]) + (t2[2] + t2[3])
    obc[...] = both[:, 0:256]
    onorm[...] = both[:, 256:384]
    wide.gather_wait(dtok_o)
    links.finish()


def passed_along(value, axis, by):
    count = lax.axis_size(axis)
    pairs = [(i, i + by) for i in range(count) if 0 <= i + by < count]
    return lax.ppermute(value, axis, pairs)


def against(left, right):
    return lax.dot_general(
        left, right, (((1,), (1,)), ((), ())), preferred_element_type=jnp.float32
    )


def over_rows(left, right):
    return lax.dot_general(
        left, right, (((0,), (0,)), ((), ())), preferred_element_type=jnp.float32
    )


def silu_slope(value):
    sigma = jax.nn.sigmoid(value)
    return sigma * (1.0 + value * (1.0 - sigma))


def call(kernel, out_shapes, scratch, *args, specs=None, collective_id=None):
    return pl.pallas_call(
        kernel,
        out_shape=[jax.ShapeDtypeStruct(s, d) for s, d in out_shapes],
        in_specs=[pl.BlockSpec(memory_space=pl.ANY if n in (specs or ()) else pltpu.VMEM) for n in range(len(args))],
        out_specs=[pl.BlockSpec(memory_space=pltpu.VMEM)] * len(out_shapes),
        scratch_shapes=[pltpu.SemaphoreType.DMA(s) if d is None else pltpu.VMEM(s, d) for s, d in scratch],
        compiler_params=pltpu.CompilerParams(vmem_limit_bytes=VMEM_LIMIT, collective_id=collective_id, has_side_effects=collective_id is not None
        ),
    )(*args)


def local(
    tokens,
    segment,
    norm_gain,
    w_z,
    w_x,
    w_dt,
    w_bc,
    conv_x,
    conv_xb,
    conv_bc,
    conv_bcb,
    dt_bias,
    a_log,
    d_skip,
    gate_gain,
    w_out,
    cotangent,
):
    length = tokens.shape[0]
    head_count = dt_bias.shape[0]
    inner_width = head_count * HEADDIM
    bc_width = 2 * STATE
    seg = segment
    w_all, edge_tokens, edge_segs = call(
        gather_kernel,
        [((16, 64, 1920), BF), ((EDGE, 1024), BF), ((8, 128), jnp.int32)],
        [((64, 1920), BF), ((EDGE, 1024), BF), ((24,), None), ((24,), None)],
        w_z, w_x, w_bc, w_dt, norm_gain[:, None], w_out, tokens[length - EDGE :], seg.reshape(8, 128),
        collective_id=1,
    )
    w_all = w_all.reshape(1024, 1920)
    out_all = w_all[:, 1408:]
    edge_ids = jnp.where(lax.axis_index("context") > 0, edge_segs[7, 112:], 0)
    ext_ids = jnp.concatenate([edge_ids[-3:], seg])
    start_seg = jnp.where(edge_ids[-1] == seg[0], seg[0], -1)
    blocks = seg.reshape(length // Q, Q)
    before = jnp.concatenate([start_seg[None], blocks[:-1, -1]])
    marks = [seg.astype(F32)]
    marks += [(ext_ids[3 - d : 3 - d + length] == seg).astype(F32) for d in (1, 2, 3)]
    marks += [(seg == start_seg).astype(F32)]
    marks += [(blocks == before[:, None]).astype(F32).reshape(-1)]
    marks += [(blocks == blocks[:, -1:]).astype(F32).reshape(-1)]
    marks += [jnp.zeros((length,), F32)]
    colm = jnp.pad(jnp.stack(marks, axis=1), ((0, 8), (0, 0)))
    segr = blocks.astype(F32)
    conv_w = jnp.concatenate([conv_x, conv_bc], axis=1)
    conv_b = jnp.concatenate([conv_xb, conv_bcb])[None]
    expand_np = np.kron(np.eye(8), np.ones((1, HEADDIM)))
    expand = jnp.asarray(expand_np, BF)
    expand_t = jnp.asarray(expand_np.T, BF)
    wide = (length, inner_width)
    x_normed, z_gate, xbc, pre, dt_raw, y_zero, enter_decay, c_act, state_local, gain_row = call(
        front_kernel,
        [((length, 1024), BF), (wide, F32), ((length + EDGE, 768), BF), ((length, 768), F32), ((length, 8), F32),
         (wide, F32), ((length, 8), F32), ((length, STATE), BF), ((STATE, inner_width), F32), ((1, 1024), F32)],
        [((length + EDGE, 768), F32)],
        tokens, edge_tokens, w_all, colm, segr, conv_w, conv_b, dt_bias[None], a_log[None], d_skip[None], expand,
    )
    state_in = passed_along(state_local, "context", 1)
    decay_e = jnp.repeat(enter_decay, HEADDIM, axis=1)
    y_mixed = y_zero + decay_e * jnp.dot(c_act, state_in.astype(BF), preferred_element_type=F32)
    gate_act = jax.nn.silu(z_gate)
    gated = y_mixed * gate_act
    d_y_normed = jnp.dot(cotangent, out_all, preferred_element_type=F32)
    d_scaled = d_y_normed * gate_gain[None, :]
    sums = lax.psum(jnp.stack([jnp.sum(gated * gated, axis=1), jnp.sum(d_scaled * gated, axis=1)]), "tensor")
    gate_root = lax.rsqrt(sums[0] / INNER + EPSILON)[:, None]
    y_normed = (gated * gate_root * gate_gain[None, :]).astype(BF)
    branch_part = against(y_normed, out_all).astype(BF)
    g_w_out = over_rows(cotangent, y_normed).astype(BF)
    g_gate_gain = jnp.sum(d_y_normed * gated * gate_root, axis=0)
    d_gated = gate_root * d_scaled - gated * gate_root**3 * (sums[1] / INNER)[:, None]
    d_y = d_gated * gate_act
    d_z = (d_gated * y_mixed * silu_slope(z_gate)).astype(BF)
    d_carry = over_rows(c_act, (d_y * decay_e).astype(BF)).astype(BF)
    d_x_low, d_bc, d_dt_raw, small, output = call(
        back_kernel,
        [(wide, BF), ((length, bc_width), BF), ((length, 8), F32), ((48, 128), F32), ((length, 1024), BF)],
        [((8, STATE, inner_width), F32), ((length, 768), F32), ((length + 16, 768), F32), ((STATE, inner_width), F32), ((8, 8), F32),
         ((STATE, inner_width), BF), ((EDGE, 768), F32), ((8, 768), F32), ((8, 768), F32),
         ((2, 128, 1024), BF), ((2, 128, 1024), BF), ((256, 1024), BF), ((256, 1024), BF), ((256, 1024), BF),
         ((16,), None), ((16,), None), ((1,), None)],
        d_y, colm, segr, xbc, pre, dt_raw, state_in, d_carry, conv_w, dt_bias[None], a_log[None], d_skip[None], expand, expand_t,
        branch_part, tokens,
        specs=(15,), collective_id=3,
    )
    d_dt_low = jnp.pad(d_dt_raw.astype(BF), ((0, 0), (0, 120)))
    gates = jnp.concatenate([d_z, d_x_low], axis=1)
    part_in = (against(gates, w_all[:, :1024]) + against(d_dt_low, w_all[:, 1280:1408])).astype(BF)
    g_w_z = over_rows(x_normed, d_z).astype(BF)
    g_w_x = over_rows(x_normed, d_x_low).astype(BF)
    g_w_dt = over_rows(x_normed, d_dt_low).astype(BF)
    grid = (8, 2, 64)
    d_tokens, o_z, o_x, o_out, o_dt, o_bc, o_norm, conv_o, convb_o, cbc_o, cbcb_o, gate_o, heads_o = call(
        tail_kernel,
        [((length, 1024), BF), ((64, 512), F32), ((64, 512), F32), ((64, 512), F32), ((64, 128), F32),
         ((64, 256), F32), ((64, 128), F32), ((4, 512), F32), ((1, 512), F32), ((4, 256), F32), ((1, 256), F32), ((1, 512), F32), ((8, 128), F32)],
        [((2, 128, 1024), BF), ((2, 128, 1024), BF), ((256, 1024), BF), ((256, 1024), BF),
         ((2, 128, 256), BF), ((2, 128, 256), BF), ((256, 256), BF), ((256, 256), BF),
         ((8, 64, 512), BF), ((8, 64, 512), BF), ((8, 64, 512), BF), ((8, 64, 128), BF), ((8, 64, 1664), BF), ((7, 64, 1664), BF),
         ((64, 1664), BF), ((64, 1664), BF),
         ((8, 2, 64, 384), BF), ((8, 64, 384), BF), ((8, 64, 384), BF), ((7, 64, 384), BF),
         ((64, 384), F32), ((64, 384), F32), ((4, 64, 384), F32),
         ((48, 128), F32), ((48, 128), F32), ((8, 48, 128), F32), ((48, 128), F32), ((48, 128), F32), ((4, 16, 128), F32),
         ((256, 1024), BF), ((256, 1024), BF), ((256, 1024), BF), ((1024, 256), BF),
         ((64,), None), ((64,), None), ((4,), None)],
        part_in, d_bc, g_w_z.reshape(grid + (512,)), g_w_x.reshape(grid + (512,)), g_w_out.reshape(grid + (512,)),
        g_w_dt.reshape(grid + (128,)), small, g_gate_gain.reshape(4, 128), gain_row, tokens, cotangent, x_normed, w_all,
        specs=(9, 10, 11, 12), collective_id=2,
    )
    return (
        output,
        d_tokens,
        o_norm[:, 0],
        o_z,
        o_x,
        o_dt[:, 0:8],
        o_bc,
        conv_o,
        convb_o[0],
        cbc_o,
        cbcb_o[0],
        heads_o[0, 0:8],
        heads_o[1, 0:8],
        heads_o[2, 0:8],
        gate_o[0],
        o_out,
    )


def solution(mesh):
    in_specs = (
        P(("shard", "context"), None),
        P(("shard", "context")),
        P("shard"),
        P("shard", "tensor"),
        P("shard", "tensor"),
        P("shard", "tensor"),
        P("shard", None),
        P(None, "tensor"),
        P("tensor"),
        P(),
        P(),
        P("tensor"),
        P("tensor"),
        P("tensor"),
        P("tensor"),
        P("shard", "tensor"),
        P(("shard", "context"), None),
    )
    out_specs = (
        P(("shard", "context"), None),
        P(("shard", "context"), None),
        P("shard"),
        P("shard", "tensor"),
        P("shard", "tensor"),
        P("shard", "tensor"),
        P("shard", None),
        P(None, "tensor"),
        P("tensor"),
        P(),
        P(),
        P("tensor"),
        P("tensor"),
        P("tensor"),
        P("tensor"),
        P("shard", "tensor"),
    )
    return jax.shard_map(local, mesh=mesh, in_specs=in_specs, out_specs=out_specs, check_vma=False)
```

```python
from functools import partial

import jax
import jax.numpy as jnp
import numpy as np
from jax import lax
from jax.experimental import pallas as pl
from jax.experimental.pallas import tpu as pltpu
from jax.sharding import PartitionSpec as P

HEADDIM = 64
STATE = 128
CONV = 4
INNER = 2048


EPSILON = 1e-05


F32 = jnp.float32
BF = jnp.bfloat16
Q = 128
EDGE = 16
VMEM_LIMIT = 58 * 1024 * 1024


def mm(a, b):
    return lax.dot_general(a, b, (((1,), (0,)), ((), ())), preferred_element_type=F32)


def mm_nt(a, b):
    return lax.dot_general(a, b, (((1,), (1,)), ((), ())), preferred_element_type=F32)


def mm_tn(a, b):
    return lax.dot_general(a, b, (((0,), (0,)), ((), ())), preferred_element_type=F32)


def split2(v):
    hi = v.astype(BF)
    return hi, (v - hi.astype(F32)).astype(BF)


def mm2(a, b):
    hi, lo = split2(a)
    return mm(hi, b) + mm(lo, b)


def mm3_left(a, b):
    hi, lo = split2(b)
    lo2 = (b - hi.astype(F32) - lo.astype(F32)).astype(BF)
    return mm(a, hi) + (mm(a, lo) + mm(a, lo2))


def softplus(v):
    return jnp.maximum(v, 0.0) + jnp.log1p(jnp.exp(-jnp.abs(v)))


def sigmoid(v):
    return 1.0 / (1.0 + jnp.exp(-v))


def triangles():
    rows = lax.broadcasted_iota(jnp.int32, (Q, Q), 0)
    cols = lax.broadcasted_iota(jnp.int32, (Q, Q), 1)
    return rows >= cols, rows <= cols


def as_low(mask):
    return jnp.where(mask, 1.0, 0.0).astype(BF)


def halves(slab):
    lane = lax.broadcasted_iota(jnp.int32, slab.shape, 1)
    zero = jnp.zeros_like(slab)
    first = jnp.where(lane < HEADDIM, slab, zero)
    second = jnp.where(lane >= HEADDIM, slab, zero)
    return jnp.concatenate([first, second], axis=0)


def back_kernel(
    dy, colm, segr, xbc, pre_r, dtr, st_in, g_send, cw, dtb, alog, dsk, ex, ext, branch, tok,
    dx_o, dbc_o, ddt_o, small_o, out_o,
    states, acts, dpre, grad, heads, g_in, tail_r, ret_s, ret_r, near, relay, from_d, from_u, tok_r, send, recv, local_sem,
):
    shard, context, tensor, core, chip, chips, sibling, others, partner, ranks, group = places()
    own = pl.ds(pl.multiple_of(tensor * 256, 256), 256)
    fetch = pltpu.make_async_copy(tok.at[own], tok_r, local_sem.at[0])
    fetch.start()
    greet([partner, group[1], group[3]])
    links = Links(send, recv)
    carry_in = links.copy(g_send, g_in, partner)
    ring = Ring(links, tensor, group)
    ring.reduce_first(branch, near, from_d, from_u)
    a_neg = -jnp.exp(alog[...])
    causal, anti = triangles()
    lower = as_low(causal)
    upper = as_low(anti)
    expand = ex[...]
    expand_t = ext[...]
    dsk_e = mm2(dsk[...], expand)

    def head_sum(v):
        return mm2(v, expand_t)

    states[0] = st_in[...]

    def forward(b, carry):
        r = pl.ds(pl.multiple_of(b * Q, Q), Q)
        marks = colm[r]
        dt = softplus(dtr[r] + dtb[...])
        cum = mm3_left(lower, dt * a_neg)
        last = cum[Q - 1 : Q]
        tail = jnp.exp(last - cum) * marks[:, 6:7] * dt
        keep_e = mm2(jnp.exp(last) * marks[Q - 1 : Q, 5:6], expand)
        tail_e = mm2(tail, expand)
        pieces = []
        for c in range(6):
            lanes = slice(c * 128, c * 128 + 128)
            pre = pre_r[r, lanes]
            act = pre * sigmoid(pre)
            acts[r, lanes] = act
            if c < 4:
                pieces.append((act * tail_e[:, lanes]).astype(BF))
            if c == 4:
                b_low = act.astype(BF)
        fresh = mm_tn(b_low, jnp.concatenate(pieces, axis=1))
        states[b + 1] = keep_e * states[b] + fresh
        return carry

    lax.fori_loop(0, 7, forward, 0)
    r7 = slice(7 * Q, 8 * Q)
    for c in range(6):
        lanes = slice(c * 128, c * 128 + 128)
        pre = pre_r[r7, lanes]
        acts[r7, lanes] = pre * sigmoid(pre)
    carry_in.wait_recv()
    grad[...] = jnp.where(context == 0, g_in[...].astype(F32), 0.0)
    heads[...] = jnp.zeros_like(heads)
    dpre[0:8] = jnp.zeros((8, 768), F32)
    dpre[1032:1040] = jnp.zeros((8, 768), F32)

    def backward(i, carry):
        b = 7 - i
        r = pl.ds(pl.multiple_of(b * Q, Q), Q)
        rp = pl.ds(pl.multiple_of(b * Q + 8, 8), Q)
        marks = colm[r]
        raw = dtr[r] + dtb[...]
        dt = softplus(raw)
        cum = mm3_left(lower, dt * a_neg)
        cum_t = cum.T
        last = cum[Q - 1 : Q]
        enter = jnp.exp(cum) * marks[:, 5:6]
        tail = jnp.exp(last - cum) * marks[:, 6:7]
        dt_e = mm2(dt, expand)
        enter_e = mm2(enter, expand)
        tail_e = mm2(tail, expand)
        keep_e = enter_e[Q - 1 : Q]
        b_low = acts[r, 512:640].astype(BF)
        c_low = acts[r, 640:768].astype(BF)
        state = states[b]
        state_low = state.astype(BF)
        g_now = grad[...]
        g_low = g_now.astype(BF)
        inter = mm(c_low, state_low)
        back = mm(b_low, g_low)
        mask = causal & (marks[:, 0:1] == segr[pl.ds(b, 1), :])
        scores = jnp.where(mask, mm_nt(c_low, b_low), 0.0)
        kept = jnp.sum(state * g_now, axis=0, keepdims=True) * keep_e
        entered, tailed, e_terms, q_terms, x_terms, k_terms = [], [], [], [], [], []
        rows, cols = [], []
        d_scores = jnp.zeros((Q, Q), F32)
        for p in range(4):
            lanes = slice(p * 128, p * 128 + 128)
            x = acts[r, lanes]
            dys = dy[r, lanes]
            xdt = x * dt_e[:, lanes]
            xdt_low = xdt.astype(BF)
            ed = enter_e[:, lanes] * dys
            tx = tail_e[:, lanes] * xdt
            entered.append(ed.astype(BF))
            tailed.append(tx.astype(BF))
            dy_two = halves(dys.astype(BF))
            dw_two = mm_nt(dy_two, xdt_low)
            ws = []
            for k in range(2):
                h = 2 * p + k
                decay = jnp.exp(jnp.minimum(cum[:, h : h + 1] - cum_t[h : h + 1, :], 0.0))
                weight = decay * scores
                dw = dw_two[k * Q : k * Q + Q]
                d_scores = d_scores + decay * dw
                both = weight * dw
                rows.append(jnp.sum(both, axis=1, keepdims=True))
                cols.append(jnp.sum(both, axis=0, keepdims=True))
                ws.append(weight.astype(BF))
            dxdt = mm_tn(jnp.concatenate(ws, axis=0), dy_two) + tail_e[:, lanes] * back[:, lanes]
            e_terms.append(ed * inter[:, lanes] - tx * back[:, lanes])
            q_terms.append(jnp.sum(tx * back[:, lanes], axis=0, keepdims=True) + kept[:, lanes])
            x_terms.append(dxdt * x)
            k_terms.append(jnp.sum(dys * x, axis=0, keepdims=True))
            pre = pre_r[r, lanes]
            sig = sigmoid(pre)
            dpre[rp, lanes] = (dxdt * dt_e[:, lanes] + dsk_e[:, lanes] * dys) * (sig * (1.0 + pre * (1.0 - sig)))
        entered = jnp.concatenate(entered, axis=1)
        tailed = jnp.concatenate(tailed, axis=1)
        ds_low = jnp.where(mask, d_scores, 0.0).astype(BF)
        d_c = mm_nt(entered, state_low) + mm(ds_low, b_low)
        d_b = mm_nt(tailed, g_low) + mm_tn(ds_low, c_low)
        grad[...] = keep_e * g_now + mm_tn(c_low, entered)
        for c, value in ((4, d_b), (5, d_c)):
            lanes = slice(c * 128, c * 128 + 128)
            pre = pre_r[r, lanes]
            sig = sigmoid(pre)
            dpre[rp, lanes] = value * (sig * (1.0 + pre * (1.0 - sig)))
        d_cum = jnp.concatenate(rows, axis=1) - jnp.concatenate(cols, axis=0).T
        d_cum = d_cum + head_sum(jnp.concatenate(e_terms, axis=1))
        d_log = mm3_left(upper, d_cum) + head_sum(jnp.concatenate(q_terms, axis=1))
        d_dt = d_log * a_neg + head_sum(jnp.concatenate(x_terms, axis=1))
        d_raw = d_dt * sigmoid(raw)
        ddt_o[r] = d_raw
        heads[0:1] += jnp.sum(d_raw, axis=0, keepdims=True)
        heads[1:2] += jnp.sum(d_log * dt, axis=0, keepdims=True) * a_neg
        heads[2:3] += head_sum(jnp.concatenate(k_terms, axis=1))
        return carry

    lax.fori_loop(0, 1, backward, 0)
    ring.reduce_second(branch, near, relay, from_d, from_u)
    lax.fori_loop(1, 4, backward, 0)
    fetch.wait()
    ring.reduce_wait()

    def finish_out(i, carry):
        r = pl.ds(pl.multiple_of(i * 64, 64), 64)
        rt = pl.ds(pl.multiple_of(tensor * 256 + i * 64, 64), 64)
        total = branch[rt].astype(F32) + from_d[r].astype(F32) + from_u[r].astype(F32)
        out_o[rt] = (tok_r[r].astype(F32) + total).astype(BF)
        return carry

    lax.fori_loop(0, 4, finish_out, 0)
    ring.gather_first(out_o)
    lax.fori_loop(4, 8, backward, 0)
    small_o[...] = jnp.zeros_like(small_o)
    small_o[24:32, 0:8] = heads[...]

    for c in range(6):
        lanes = slice(c * 128, c * 128 + 128)
        first = dpre[0:16, lanes]
        flags = jnp.concatenate([jnp.zeros((8, 8), F32), colm[0:8]], axis=0)
        total = jnp.zeros((8, 128), F32)
        for d in range(1, 4):
            total = total + cw[3 - d : 4 - d, lanes] * (first * flags[:, d : d + 1])[d : d + 8]
        ret_s[:, lanes] = total
    ret_in = links.copy(ret_s, ret_r, partner)
    ring.gather_second(out_o)
    for c in range(6):
        lanes = slice(c * 128, c * 128 + 128)

        def conv(b, sums, lanes=lanes, c=c):
            r = pl.ds(pl.multiple_of(b * Q, Q), Q)
            slab = dpre[pl.ds(pl.multiple_of(b * Q + 8, 8), Q + 8), lanes]
            marks = colm[pl.ds(pl.multiple_of(b * Q, Q), Q + 8)]
            xin = xbc[pl.ds(pl.multiple_of(b * Q, Q), Q + EDGE), lanes].astype(F32)
            main = slab[0:Q]
            out = cw[3:4, lanes] * main
            new = [sums[0] + jnp.sum(main, axis=0, keepdims=True),
                   sums[1] + jnp.sum(main * xin[EDGE:], axis=0, keepdims=True)]
            for d in range(1, 4):
                masked = slab * marks[:, d : d + 1]
                out = out + cw[3 - d : 4 - d, lanes] * masked[d : d + Q]
                new.append(sums[d + 1] + jnp.sum(masked[0:Q] * xin[EDGE - d : Q + EDGE - d], axis=0, keepdims=True))
            if c < 4:
                dx_o[r, lanes] = out.astype(BF)
            else:
                dbc_o[r, slice(c * 128 - 512, c * 128 - 384)] = out.astype(BF)

            @pl.when(b == 7)
            def _():
                tail_r[:, lanes] = out[Q - EDGE :]

            return tuple(new)

        zero = jnp.zeros((1, 128), F32)
        sums = lax.fori_loop(0, 8, conv, (zero,) * 5)
        at = 16 + c if c < 4 else 36 + c
        small_o[at : at + 1] = sums[0]
        for d in range(4):
            at = (3 - d) * 4 + c if c < 4 else 28 + (3 - d) * 2 + c
            small_o[at : at + 1] = sums[d + 1]
    ret_in.wait_recv()
    returned = jnp.where(context == 0, ret_r[...], 0.0)
    last = tail_r[...] + jnp.concatenate([jnp.zeros((EDGE - 8, 768), F32), returned], axis=0)
    dx_o[1024 - EDGE : 1024] = last[:, 0:512].astype(BF)
    dbc_o[1024 - EDGE : 1024] = last[:, 512:768].astype(BF)
    ring.gather_wait(out_o)
    links.finish()


MESH = pl.DeviceIdType.MESH


class Links:
    def __init__(self, send, recv):
        self.send, self.recv, self.count, self.started = send, recv, 0, []

    def copy(self, src, dst, device):
        made = pltpu.make_async_remote_copy(
            src_ref=src,
            dst_ref=dst,
            send_sem=self.send.at[self.count],
            recv_sem=self.recv.at[self.count],
            device_id=device,
            device_id_type=MESH,
        )
        self.count += 1
        self.started.append(made)
        made.start()
        return made

    def finish(self):
        for made in self.started:
            made.wait_send()


def arrival(like, dst, links_recv, device):
    return pltpu.make_async_remote_copy(
        src_ref=dst, dst_ref=dst, send_sem=links_recv, recv_sem=links_recv, device_id=device, device_id_type=MESH
    )


def greet(devices):
    barrier = pltpu.get_barrier_semaphore()
    for device in devices:
        pl.semaphore_signal(barrier, inc=1, device_id=device, device_id_type=MESH)
    pl.semaphore_wait(barrier, len(devices))


def places():
    shard, context, tensor = (lax.axis_index(name) for name in ("shard", "context", "tensor"))
    core, chip = lax.rem(shard, 2), lax.div(shard, 2)

    def at(shard_to=None, context_to=None, tensor_to=None):
        return (
            shard if shard_to is None else shard_to,
            context if context_to is None else context_to,
            tensor if tensor_to is None else tensor_to,
        )

    chips = [None] + [lax.rem(chip + k, 8) for k in range(1, 8)]
    sibling = at(shard_to=chip * 2 + (1 - core))
    others = [None] + [at(shard_to=c * 2 + core) for c in chips[1:]]
    partner = at(context_to=1 - context)
    ranks = [None] + [lax.rem(tensor + k, 4) for k in range(1, 4)]
    group = [None] + [at(tensor_to=t) for t in ranks[1:]]
    return shard, context, tensor, core, chip, chips, sibling, others, partner, ranks, group


class Ring:
    def __init__(self, links, tensor, group):
        self.links, self.tensor = links, tensor
        self.up, self.down = group[1], group[3]
        self.t_up, self.t_down, self.t_far = (lax.rem(tensor + k, 4) for k in (1, 3, 2))

    def half(self, rank, which):
        return pl.ds(pl.multiple_of(rank * 256 + which * 128, 128), 128)

    def whole(self, rank):
        return pl.ds(pl.multiple_of(rank * 256, 256), 256)

    def reduce_first(self, src, near, from_down, from_up):
        copy = self.links.copy
        self.first = (
            copy(src.at[self.half(self.t_far, 0)], near.at[0], self.up),
            copy(src.at[self.half(self.t_far, 1)], near.at[1], self.down),
        )
        self.alone = (
            copy(src.at[self.half(self.t_up, 1)], from_down.at[pl.ds(128, 128)], self.up),
            copy(src.at[self.half(self.t_down, 0)], from_up.at[pl.ds(0, 128)], self.down),
        )

    def reduce_second(self, src, near, relay, from_down, from_up):
        copy = self.links.copy
        self.first[0].wait_recv()
        relay[0] = (near[0].astype(F32) + src[self.half(self.t_up, 0)].astype(F32)).astype(BF)
        up = copy(relay.at[0], from_down.at[pl.ds(0, 128)], self.up)
        self.first[1].wait_recv()
        relay[1] = (near[1].astype(F32) + src[self.half(self.t_down, 1)].astype(F32)).astype(BF)
        down = copy(relay.at[1], from_up.at[pl.ds(128, 128)], self.down)
        self.summed = (up, down)

    def reduce_wait(self):
        for made in self.alone + self.summed:
            made.wait_recv()

    def gather_first(self, ref):
        mine = ref.at[self.whole(self.tensor)]
        self.base = self.links.count
        self.links.copy(mine, mine, self.up)
        self.links.copy(mine, mine, self.down)

    def landed(self, slot, which, device):
        arrival(None, slot, self.links.recv.at[self.base + which], device).wait_recv()

    def gather_second(self, ref):
        self.landed(ref.at[self.whole(self.t_down)], 0, self.down)
        self.base2 = self.links.count
        up = ref.at[self.half(self.t_down, 0)]
        self.links.copy(up, up, self.up)
        self.landed(ref.at[self.whole(self.t_up)], 1, self.up)
        down = ref.at[self.half(self.t_up, 1)]
        self.links.copy(down, down, self.down)

    def gather_wait(self, ref):
        offset = self.base2 - self.base
        self.landed(ref.at[self.half(self.t_far, 0)], offset, self.down)
        self.landed(ref.at[self.half(self.t_far, 1)], offset + 1, self.up)


def forward_kernel(
    wz, wx, wbc, wdt, norm, wo, etok, tok, cot, seg, cwx, cwb, cbx, cbb, dtb, alog, dsk, gg, ex, ext,
    in_o, zo_o, xn_o, xbc_o, pre_o, dtr_o, colm_o, gain_o, st_o, dy_o, dz_o, yn_o, branch_o, carry_o, gate_o,
    mine1, mine2, etok_b, eseg, xs, st, st_low, st_in, y_s, er_s, c_s, z_s, dn_s, row_s, row_r, send, recv,
):
    shard, context, tensor, core, chip, chips, sibling, others, partner, ranks, group = places()
    mine1[:, 0:512] = wx[...]
    mine1[:, 512:768] = wbc[...]
    mine1[:, 768:896] = jnp.zeros((64, 128), BF)
    mine1[:, 768:776] = wdt[...]
    mine1[:, 776:777] = norm[...]
    mine2[:, 0:512] = wz[...]
    mine2[:, 512:1024] = wo[...]
    greet([sibling, partner] + others[1:] + group[1:])
    links = Links(send, recv)

    def slot(ref, owner):
        return ref.at[pl.ds(pl.multiple_of(owner * 64, 64), 64)]

    seg_in = links.copy(seg, eseg, partner)
    first = links.count - 1
    for k in range(1, 8):
        links.copy(mine1, slot(in_o, shard), others[k])
    passed = links.count
    links.copy(mine1, slot(in_o, shard), sibling)
    tokens_in = links.copy(etok, etok_b, partner)
    second = links.count - 1
    for k in range(1, 8):
        links.copy(mine2, slot(zo_o, shard), others[k])
    passed2 = links.count + 7
    links.copy(mine2, slot(zo_o, shard), sibling)
    mine_slot = pl.ds(pl.multiple_of(shard * 64, 64), 64)
    in_o[mine_slot] = mine1[...]
    zo_o[mine_slot] = mine2[...]

    seg_in.wait_recv()
    seg_t = seg[...].astype(F32).T
    edge_t = jnp.where(context > 0, eseg[...].astype(F32).T, 0.0)
    edge_col = edge_t[120:128, 7:8]
    start = jnp.where(edge_col[7:8] == seg_t[0:1, 0:1], seg_t[0:1, 0:1], -1.0)
    colm_o[1024:1032] = jnp.zeros((8, 8), F32)
    for b in range(8):
        col = seg_t[:, b : b + 1]
        before = edge_col if b == 0 else seg_t[120:128, b - 1 : b]
        longer = jnp.concatenate([before, col], axis=0)
        entering = start if b == 0 else before[7:8]
        marks = [col]
        for d in range(1, 4):
            marks.append(jnp.where(longer[8 - d : 136 - d] == col, 1.0, 0.0))
        for value in (start, entering, col[127:128]):
            marks.append(jnp.where(col == value, 1.0, 0.0))
        marks.append(jnp.zeros_like(col))
        colm_o[b * Q : b * Q + Q] = jnp.concatenate(marks, axis=1)

    for k in (1, 7, 2, 6, 3, 5, 4):
        source = lax.rem(chip + 8 - k, 8) * 2 + core
        arrival(None, slot(in_o, source), recv.at[first + k], others[k]).wait_recv()
        made = pltpu.make_async_remote_copy(
            src_ref=slot(in_o, source), dst_ref=slot(in_o, source), send_sem=send.at[24 + k], recv_sem=recv.at[24 + k],
            device_id=sibling, device_id_type=MESH,
        )
        made.start()
        links.started.append(made)
    for k in range(8):
        source = lax.rem(chip + 8 - k, 8) * 2 + (1 - core)
        sem = recv.at[passed] if k == 0 else recv.at[24 + k]
        arrival(None, slot(in_o, source), sem, sibling).wait_recv()
    tokens_in.wait_recv()

    a_neg = -jnp.exp(alog[...])
    causal, _ = triangles()
    lower = as_low(causal)
    gain_row = in_o[:, 768:896].astype(F32).T[8:9]
    gain_o[...] = gain_row

    def normed(block):
        plain = block.astype(F32)
        root = lax.rsqrt(jnp.mean(plain * plain, axis=1, keepdims=True) + EPSILON)
        return (plain * root * gain_row).astype(BF)

    edge_tokens = jnp.where(context > 0, etok_b[...].astype(F32), 0.0)
    edge = mm(normed(edge_tokens), in_o[:, 0:768]).astype(BF)
    xbc_o[0:EDGE] = edge
    xs[0:EDGE] = edge.astype(F32)
    st[...] = jnp.zeros_like(st)
    expand = ex[...]
    dsk_e = mm2(dsk[...], expand)

    def forwarding(k):
        source = lax.rem(chip + 8 - k, 8) * 2 + core
        return pltpu.make_async_remote_copy(
            src_ref=slot(zo_o, source), dst_ref=slot(zo_o, source), send_sem=send.at[32 + k], recv_sem=recv.at[32 + k],
            device_id=sibling, device_id_type=MESH,
        )

    def body(b, run):
        r = pl.ds(pl.multiple_of(b * Q, Q), Q)
        rn = pl.ds(pl.multiple_of(b * Q + EDGE, EDGE), Q)
        xn = normed(tok[r])
        xn_o[r] = xn
        both = mm(xn, in_o[...])
        xb = both[:, 0:768].astype(BF)
        xbc_o[rn] = xb
        xs[rn] = xb.astype(F32)
        raw = both[:, 768:776]
        dtr_o[r] = raw
        marks = colm_o[r]
        acts = []
        for c in range(6):
            lanes = slice(c * 128, c * 128 + 128)
            cw, cb, at = (cwx, cbx, lanes) if c < 4 else (cwb, cbb, slice(c * 128 - 512, c * 128 - 384))
            slab = xs[pl.ds(pl.multiple_of(b * Q, Q), Q + EDGE), lanes]
            pre = cb[:, at] + cw[3:4, at] * slab[EDGE:]
            for d in range(1, 4):
                pre = pre + (cw[3 - d : 4 - d, at] * slab[EDGE - d : Q + EDGE - d]) * marks[:, d : d + 1]
            pre_o[r, lanes] = pre
            acts.append(pre * sigmoid(pre))
        b_low = acts[4].astype(BF)
        c_low = acts[5].astype(BF)
        c_s[r] = c_low
        dt = softplus(raw + dtb[...])
        cum = mm3_left(lower, dt * a_neg)
        er_s[r] = jnp.exp(run + cum) * marks[:, 4:5]
        cum_t = cum.T
        last = cum[Q - 1 : Q]
        enter = jnp.exp(cum) * marks[:, 5:6]
        tail = jnp.exp(last - cum) * marks[:, 6:7]
        dt_e = mm2(dt, expand)
        enter_e = mm2(enter, expand)
        tail_e = mm2(tail, expand)
        mask = causal & (marks[:, 0:1] == seg[pl.ds(b, 1), :].astype(F32))
        scores = jnp.where(mask, mm_nt(c_low, b_low), 0.0)
        state = st[...]
        inter = mm(c_low, state.astype(BF))
        pieces = []
        for p in range(4):
            lanes = slice(p * 128, p * 128 + 128)
            xdt = acts[p] * dt_e[:, lanes]
            pieces.append((xdt * tail_e[:, lanes]).astype(BF))
            ws = []
            for h in (2 * p, 2 * p + 1):
                decay = jnp.exp(jnp.minimum(cum[:, h : h + 1] - cum_t[h : h + 1, :], 0.0))
                ws.append((decay * scores).astype(BF))
            intra = mm(jnp.concatenate(ws, axis=1), halves(xdt.astype(BF)))
            y_s[r, lanes] = intra + enter_e[:, lanes] * inter[:, lanes] + dsk_e[:, lanes] * acts[p]
        fresh = mm_tn(b_low, jnp.concatenate(pieces, axis=1))
        st[...] = enter_e[Q - 1 : Q] * state + fresh

        @pl.when(b < 7)
        def _():
            k = b + 1
            source = lax.rem(chip + 8 - k, 8) * 2 + core
            arrival(None, slot(zo_o, source), recv.at[second + k], sibling).wait_recv()
            forwarding(k).start()

        return run + last

    lax.fori_loop(0, 8, body, jnp.zeros((1, 8), F32))
    st_low[...] = st[...].astype(BF)
    links.count = 40
    state_in = links.copy(st_low, st_in, partner)
    for k in range(8):
        source = lax.rem(chip + 8 - k, 8) * 2 + (1 - core)
        sem = recv.at[passed2 - 7] if k == 0 else recv.at[32 + k]
        arrival(None, slot(zo_o, source), sem, sibling).wait_recv()

    def project(b, carry):
        r = pl.ds(pl.multiple_of(b * Q, Q), Q)
        z_s[r] = mm(xn_o[r], zo_o[:, 0:512])
        dn_s[r] = mm(cot[r], zo_o[:, 512:1024])
        return carry

    lax.fori_loop(0, 8, project, 0)
    state_in.wait_recv()
    st_o[...] = jnp.where(context > 0, st_in[...].astype(F32), 0.0)

    def sums(b, carry):
        r = pl.ds(pl.multiple_of(b * Q, Q), Q)
        y = y_s[r] + mm2(er_s[r], expand) * mm(c_s[r], st_o[...].astype(BF))
        y_s[r] = y
        z = z_s[r]
        gated = y * (z * sigmoid(z))
        first_sum = jnp.sum(gated * gated, axis=1, keepdims=True)
        second_sum = jnp.sum(dn_s[r] * gg[...] * gated, axis=1, keepdims=True)
        row_s[b] = jnp.concatenate([first_sum, second_sum, jnp.zeros((Q, 6), F32)], axis=1).T
        return carry

    lax.fori_loop(0, 8, sums, 0)
    rows_in = [links.copy(row_s, row_r.at[k - 1], group[k]) for k in range(1, 4)]
    for copy in rows_in:
        copy.wait_recv()
    gate_o[...] = jnp.zeros_like(gate_o)
    st[...] = jnp.zeros_like(st)

    def finish(b, carry):
        r = pl.ds(pl.multiple_of(b * Q, Q), Q)
        total = (row_s[b] + row_r[0, b] + row_r[1, b] + row_r[2, b]).T
        root = lax.rsqrt(total[:, 0:1] * (1.0 / INNER) + EPSILON)
        cross = (root * root * root) * (total[:, 1:2] * (1.0 / INNER))
        er_e = mm2(er_s[r], expand)
        normals, carries = [], []
        for p in range(4):
            lanes = slice(p * 128, p * 128 + 128)
            y = y_s[r, lanes]
            z = z_s[r, lanes]
            dn = dn_s[r, lanes]
            sig = sigmoid(z)
            gate = z * sig
            gated = y * gate
            scaled = gated * root
            normals.append((scaled * gg[:, lanes]).astype(BF))
            gate_o[p : p + 1] += jnp.sum(dn * scaled, axis=0, keepdims=True)
            d_gated = root * (dn * gg[:, lanes]) - gated * cross
            d_y = d_gated * gate
            dy_o[r, lanes] = d_y
            dz_o[r, lanes] = (d_gated * y * (sig * (1.0 + z * (1.0 - sig)))).astype(BF)
            carries.append((d_y * er_e[:, lanes]).astype(BF))
        low = jnp.concatenate(normals, axis=1)
        yn_o[r] = low
        branch_o[r] = mm_nt(low, zo_o[:, 512:1024]).astype(BF)
        st[...] += mm_tn(c_s[r], jnp.concatenate(carries, axis=1))
        return carry

    lax.fori_loop(0, 8, finish, 0)
    carry_o[...] = st[...].astype(BF)
    links.finish()
    for k in range(1, 8):
        forwarding(k).wait_send()


def tail_kernel(
    part, dbc, gz, gx, go, gd, small, gate, gain, tok, cot, xn, w,
    dtok_o, oz, ox, oo, odt, obc, onorm, conv_o, convb_o, bc_o, bcb_o, gate_o, heads_o,
    near, relay, from_d, from_u, near2, relay2, from_d2, from_u2, sz, sx, so, sd, chunk, rg, cs, cr,
    g2, s2, chunk2, rg2, c2s, c2r, t2,
    sm, sm_s, sm_c, sm_x, sm_r, sm_t,
    tok_r, cot_r, xn_r, wbc, send, recv, local_sem,
):
    shard, context, tensor, core, chip, chips, sibling, others, partner, ranks, group = places()
    own = pl.ds(pl.multiple_of(tensor * 256, 256), 256)
    fetch = [
        pltpu.make_async_copy(tok.at[own], tok_r, local_sem.at[0]),
        pltpu.make_async_copy(cot.at[own], cot_r, local_sem.at[1]),
        pltpu.make_async_copy(xn.at[own], xn_r, local_sem.at[2]),
        pltpu.make_async_copy(w.at[:, pl.ds(512, 256)], wbc, local_sem.at[3]),
    ]
    for copy in fetch:
        copy.start()
    greet([sibling, partner] + others[1:] + group[1:])
    links = Links(send, recv)
    sm[...] = small[...]
    sm[20:24] = gate[...]
    wide, thin = Ring(links, tensor, group), Ring(links, tensor, group)
    thin.reduce_first(dbc, near2, from_d2, from_u2)
    wide.reduce_first(part, near, from_d, from_u)
    sib_in = [
        links.copy(sm, sm_s, sibling),
        links.copy(gz.at[:, 1 - core], sz, sibling),
        links.copy(gx.at[:, 1 - core], sx, sibling),
        links.copy(go.at[:, 1 - core], so, sibling),
        links.copy(gd.at[:, 1 - core], sd, sibling),
    ]
    thin.reduce_second(dbc, near2, relay2, from_d2, from_u2)
    for copy in sib_in:
        copy.wait_recv()
    sm_c[chip] = sm[...] + sm_s[...]
    small_in = [links.copy(sm_c.at[chip], sm_c.at[chip], others[k]) for k in range(1, 8)]
    small_base = links.count - 8

    def merge(c, carry):
        for mine, theirs, at in ((gz, sz, 0), (gx, sx, 512), (go, so, 1024)):
            chunk[c, :, at : at + 512] = (mine[c, core].astype(F32) + theirs[c].astype(F32)).astype(BF)
        chunk[c, :, 1536:1664] = (gd[c, core].astype(F32) + sd[c].astype(F32)).astype(BF)
        return carry

    lax.fori_loop(0, 8, merge, 0)
    wide.reduce_second(part, near, relay, from_d, from_u)
    grads_in = [links.copy(chunk.at[chips[k]], rg.at[k - 1], others[k]) for k in range(1, 8)]

    for copy in fetch:
        copy.wait()
    thin.reduce_wait()
    wide.reduce_wait()
    ones = jnp.full((64, 128), 1.0, BF)

    def slice_rows(i):
        r = pl.ds(pl.multiple_of(i * 64, 64), 64)
        rt = pl.ds(pl.multiple_of(tensor * 256 + i * 64, 64), 64)
        return r, rt

    def inner(i, carry):
        r, rt = slice_rows(i)
        d_bc = dbc[rt].astype(F32) + from_d2[r].astype(F32) + from_u2[r].astype(F32)
        d_bc_low = d_bc.astype(BF)
        total = part[rt].astype(F32) + from_d[r].astype(F32) + from_u[r].astype(F32)
        total = total + mm_nt(d_bc_low, wbc[...])
        plain = tok_r[r].astype(F32)
        root = lax.rsqrt(jnp.mean(plain * plain, axis=1, keepdims=True) + EPSILON)
        stat = plain * root
        d_plain = total * gain[...]
        mean = jnp.mean(d_plain * plain, axis=1, keepdims=True)
        dtok_o[rt] = (cot_r[r].astype(F32) + root * d_plain - stat * (root * root) * mean).astype(BF)
        g_bc, g_norm = carry
        g_bc = g_bc + mm_tn(xn_r[r], d_bc_low)
        g_norm = g_norm + mm_tn((total * stat).astype(BF), ones)
        return g_bc, g_norm

    g_bc, g_norm = lax.fori_loop(0, 4, inner, (jnp.zeros((1024, 256), F32), jnp.zeros((1024, 128), F32)))
    g2[:, :, :, 0:256] = g_bc.astype(BF).reshape(8, 2, 64, 256)
    g2[:, :, :, 256:384] = g_norm.astype(BF).reshape(8, 2, 64, 128)
    sib2_in = links.copy(g2.at[:, 1 - core], s2, sibling)
    wide.gather_first(dtok_o)
    sib2_in.wait_recv()
    for c in range(8):
        chunk2[c] = (g2[c, core].astype(F32) + s2[c].astype(F32)).astype(BF)
    grads2_in = [links.copy(chunk2.at[chips[k]], rg2.at[k - 1], others[k]) for k in range(1, 8)]

    for k in range(1, 8):
        source = lax.rem(chip + 8 - k, 8)
        arrival(None, sm_c.at[source], recv.at[small_base + k], others[k]).wait_recv()
    total = sm_c[0]
    for c in range(1, 8):
        total = total + sm_c[c]
    sm_x[...] = total
    small_ctx = links.copy(sm_x, sm_r, partner)
    for copy in grads_in:
        copy.wait_recv()
    for at in range(0, 1664, 128):
        lanes = slice(at, at + 128)
        acc = chunk[chip, :, lanes].astype(F32)
        for k in range(7):
            acc = acc + rg[k, :, lanes].astype(F32)
        cs[:, lanes] = acc.astype(BF)
    grads_ctx = links.copy(cs, cr, partner)
    wide.gather_second(dtok_o)
    for copy in grads2_in:
        copy.wait_recv()
    for at in range(0, 384, 128):
        lanes = slice(at, at + 128)
        acc = chunk2[chip, :, lanes].astype(F32)
        for k in range(7):
            acc = acc + rg2[k, :, lanes].astype(F32)
        c2s[:, lanes] = acc
    grads2_ctx = links.copy(c2s, c2r, partner)
    small_ctx.wait_recv()
    sums = sm_x[...] + sm_r[...]
    for k in range(4):
        for p in range(4):
            conv_o[k : k + 1, p * 128 : p * 128 + 128] = sums[k * 4 + p : k * 4 + p + 1]
    for p in range(4):
        convb_o[:, p * 128 : p * 128 + 128] = sums[16 + p : 17 + p]
        gate_o[:, p * 128 : p * 128 + 128] = sums[20 + p : 21 + p]
    heads_o[...] = sums[24:32]
    sm_t[tensor] = sums[32:48]
    small_t = links.count
    for k in range(1, 4):
        links.copy(sm_t.at[tensor], sm_t.at[tensor], group[k])
    grads2_ctx.wait_recv()
    t2[tensor] = c2s[...] + c2r[...]
    grads2_t = links.count
    for k in range(1, 4):
        links.copy(t2.at[tensor], t2.at[tensor], group[k])
    grads_ctx.wait_recv()
    oz[...] = cs[:, 0:512].astype(F32) + cr[:, 0:512].astype(F32)
    ox[...] = cs[:, 512:1024].astype(F32) + cr[:, 512:1024].astype(F32)
    oo[...] = cs[:, 1024:1536].astype(F32) + cr[:, 1024:1536].astype(F32)
    odt[...] = cs[:, 1536:1664].astype(F32) + cr[:, 1536:1664].astype(F32)
    for k in range(1, 4):
        source = lax.rem(tensor + 4 - k, 4)
        arrival(None, sm_t.at[source], recv.at[small_t + k - 1], group[k]).wait_recv()
        arrival(None, t2.at[source], recv.at[grads2_t + k - 1], group[k]).wait_recv()
    sums = (sm_t[0] + sm_t[1]) + (sm_t[2] + sm_t[3])
    for k in range(4):
        for p in range(2):
            bc_o[k : k + 1, p * 128 : p * 128 + 128] = sums[k * 2 + p : k * 2 + p + 1]
    for p in range(2):
        bcb_o[:, p * 128 : p * 128 + 128] = sums[8 + p : 9 + p]
    both = (t2[0] + t2[1]) + (t2[2] + t2[3])
    obc[...] = both[:, 0:256]
    onorm[...] = both[:, 256:384]
    wide.gather_wait(dtok_o)
    links.finish()


def against(left, right):
    return lax.dot_general(
        left, right, (((1,), (1,)), ((), ())), preferred_element_type=jnp.float32
    )


def over_rows(left, right):
    return lax.dot_general(
        left, right, (((0,), (0,)), ((), ())), preferred_element_type=jnp.float32
    )


def call(kernel, out_shapes, scratch, *args, specs=None, collective_id=None):
    return pl.pallas_call(
        kernel,
        out_shape=[jax.ShapeDtypeStruct(s, d) for s, d in out_shapes],
        in_specs=[pl.BlockSpec(memory_space=pl.ANY if n in (specs or ()) else pltpu.VMEM) for n in range(len(args))],
        out_specs=[pl.BlockSpec(memory_space=pltpu.VMEM)] * len(out_shapes),
        scratch_shapes=[pltpu.SemaphoreType.DMA(s) if d is None else pltpu.VMEM(s, d) for s, d in scratch],
        compiler_params=pltpu.CompilerParams(vmem_limit_bytes=VMEM_LIMIT, collective_id=collective_id, has_side_effects=collective_id is not None
        ),
    )(*args)


def local(
    tokens,
    segment,
    norm_gain,
    w_z,
    w_x,
    w_dt,
    w_bc,
    conv_x,
    conv_xb,
    conv_bc,
    conv_bcb,
    dt_bias,
    a_log,
    d_skip,
    gate_gain,
    w_out,
    cotangent,
):
    length = tokens.shape[0]
    head_count = dt_bias.shape[0]
    inner_width = head_count * HEADDIM
    bc_width = 2 * STATE
    seg = segment.reshape(8, 128)
    segr = seg.astype(F32)
    expand_np = np.kron(np.eye(8), np.ones((1, HEADDIM)))
    expand = jnp.asarray(expand_np, BF)
    expand_t = jnp.asarray(expand_np.T, BF)
    wide = (length, inner_width)
    state = (STATE, inner_width)
    heads = (dt_bias[None], a_log[None], d_skip[None])
    (w_in, w_zo, x_normed, xbc, pre, dt_raw, colm, gain_row, state_in, d_y, d_z, y_normed, branch_part, d_carry, g_gate_gain) = call(
        forward_kernel,
        [((1024, 896), BF), ((1024, 1024), BF), ((length, 1024), BF), ((length + EDGE, 768), BF), ((length, 768), F32), ((length, 8), F32),
         ((length + 8, 8), F32), ((1, 1024), F32), (state, F32), (wide, F32), (wide, BF), (wide, BF), ((length, 1024), BF), (state, BF), ((4, 128), F32)],
        [((64, 896), BF), ((64, 1024), BF), ((EDGE, 1024), BF), ((8, 128), jnp.int32), ((length + EDGE, 768), F32), (state, F32), (state, BF), (state, BF),
         (wide, F32), ((length, 8), F32), ((length, STATE), BF), (wide, F32), (wide, F32), ((8, 8, 128), F32), ((3, 8, 8, 128), F32),
         ((48,), None), ((48,), None)],
        w_z, w_x, w_bc, w_dt, norm_gain[:, None], w_out, tokens[length - EDGE :], tokens, cotangent, seg,
        conv_x, conv_bc, conv_xb[None], conv_bcb[None], *heads, gate_gain[None], expand, expand_t,
        collective_id=1,
    )
    conv_w = jnp.concatenate([conv_x, conv_bc], axis=1)
    g_w_out = over_rows(cotangent, y_normed).astype(BF)
    d_x_low, d_bc, d_dt_raw, small, output = call(
        back_kernel,
        [(wide, BF), ((length, bc_width), BF), ((length, 8), F32), ((48, 128), F32), ((length, 1024), BF)],
        [((8, STATE, inner_width), F32), ((length, 768), F32), ((length + 16, 768), F32), ((STATE, inner_width), F32), ((8, 8), F32),
         ((STATE, inner_width), BF), ((EDGE, 768), F32), ((8, 768), F32), ((8, 768), F32),
         ((2, 128, 1024), BF), ((2, 128, 1024), BF), ((256, 1024), BF), ((256, 1024), BF), ((256, 1024), BF),
         ((16,), None), ((16,), None), ((1,), None)],
        d_y, colm, segr, xbc, pre, dt_raw, state_in, d_carry, conv_w, *heads, expand, expand_t,
        branch_part, tokens,
        specs=(15,), collective_id=3,
    )
    d_dt_low = jnp.pad(d_dt_raw.astype(BF), ((0, 0), (0, 120)))
    part_in = (against(d_z, w_zo[:, :512]) + against(d_x_low, w_in[:, :512]) + against(d_dt_low, w_in[:, 768:])).astype(BF)
    g_w_z = over_rows(x_normed, d_z).astype(BF)
    g_w_x = over_rows(x_normed, d_x_low).astype(BF)
    g_w_dt = over_rows(x_normed, d_dt_low).astype(BF)
    grid = (8, 2, 64)
    d_tokens, o_z, o_x, o_out, o_dt, o_bc, o_norm, conv_o, convb_o, cbc_o, cbcb_o, gate_o, heads_o = call(
        tail_kernel,
        [((length, 1024), BF), ((64, 512), F32), ((64, 512), F32), ((64, 512), F32), ((64, 128), F32),
         ((64, 256), F32), ((64, 128), F32), ((4, 512), F32), ((1, 512), F32), ((4, 256), F32), ((1, 256), F32), ((1, 512), F32), ((8, 128), F32)],
        [((2, 128, 1024), BF), ((2, 128, 1024), BF), ((256, 1024), BF), ((256, 1024), BF),
         ((2, 128, 256), BF), ((2, 128, 256), BF), ((256, 256), BF), ((256, 256), BF),
         ((8, 64, 512), BF), ((8, 64, 512), BF), ((8, 64, 512), BF), ((8, 64, 128), BF), ((8, 64, 1664), BF), ((7, 64, 1664), BF),
         ((64, 1664), BF), ((64, 1664), BF),
         ((8, 2, 64, 384), BF), ((8, 64, 384), BF), ((8, 64, 384), BF), ((7, 64, 384), BF),
         ((64, 384), F32), ((64, 384), F32), ((4, 64, 384), F32),
         ((48, 128), F32), ((48, 128), F32), ((8, 48, 128), F32), ((48, 128), F32), ((48, 128), F32), ((4, 16, 128), F32),
         ((256, 1024), BF), ((256, 1024), BF), ((256, 1024), BF), ((1024, 256), BF),
         ((64,), None), ((64,), None), ((4,), None)],
        part_in, d_bc, g_w_z.reshape(grid + (512,)), g_w_x.reshape(grid + (512,)), g_w_out.reshape(grid + (512,)),
        g_w_dt.reshape(grid + (128,)), small, g_gate_gain, gain_row, tokens, cotangent, x_normed, w_in,
        specs=(9, 10, 11, 12), collective_id=2,
    )
    return (
        output,
        d_tokens,
        o_norm[:, 0],
        o_z,
        o_x,
        o_dt[:, 0:8],
        o_bc,
        conv_o,
        convb_o[0],
        cbc_o,
        cbcb_o[0],
        heads_o[0, 0:8],
        heads_o[1, 0:8],
        heads_o[2, 0:8],
        gate_o[0],
        o_out,
    )


def solution(mesh):
    in_specs = (
        P(("shard", "context"), None),
        P(("shard", "context")),
        P("shard"),
        P("shard", "tensor"),
        P("shard", "tensor"),
        P("shard", "tensor"),
        P("shard", None),
        P(None, "tensor"),
        P("tensor"),
        P(),
        P(),
        P("tensor"),
        P("tensor"),
        P("tensor"),
        P("tensor"),
        P("shard", "tensor"),
        P(("shard", "context"), None),
    )
    out_specs = (
        P(("shard", "context"), None),
        P(("shard", "context"), None),
        P("shard"),
        P("shard", "tensor"),
        P("shard", "tensor"),
        P("shard", "tensor"),
        P("shard", None),
        P(None, "tensor"),
        P("tensor"),
        P(),
        P(),
        P("tensor"),
        P("tensor"),
        P("tensor"),
        P("tensor"),
        P("shard", "tensor"),
    )
    return jax.shard_map(local, mesh=mesh, in_specs=in_specs, out_specs=out_specs, check_vma=False)
```

```python
from functools import partial

import jax
import jax.numpy as jnp
import numpy as np
from jax import lax
from jax.experimental import pallas as pl
from jax.experimental.pallas import tpu as pltpu
from jax.sharding import PartitionSpec as P

HEADDIM = 64
STATE = 128
CONV = 4
INNER = 2048


EPSILON = 1e-05


F32 = jnp.float32
BF = jnp.bfloat16
Q = 128
EDGE = 16
VMEM_LIMIT = 58 * 1024 * 1024


def mm(a, b):
    return lax.dot_general(a, b, (((1,), (0,)), ((), ())), preferred_element_type=F32)


def mm_nt(a, b):
    return lax.dot_general(a, b, (((1,), (1,)), ((), ())), preferred_element_type=F32)


def mm_tn(a, b):
    return lax.dot_general(a, b, (((0,), (0,)), ((), ())), preferred_element_type=F32)


def split2(v):
    hi = v.astype(BF)
    return hi, (v - hi.astype(F32)).astype(BF)


def mm2(a, b):
    hi, lo = split2(a)
    return mm(hi, b) + mm(lo, b)


def mm3_left(a, b):
    hi, lo = split2(b)
    lo2 = (b - hi.astype(F32) - lo.astype(F32)).astype(BF)
    return mm(a, hi) + (mm(a, lo) + mm(a, lo2))


def softplus(v):
    return jnp.maximum(v, 0.0) + jnp.log1p(jnp.exp(-jnp.abs(v)))


def sigmoid(v):
    return 1.0 / (1.0 + jnp.exp(-v))


def triangles():
    rows = lax.broadcasted_iota(jnp.int32, (Q, Q), 0)
    cols = lax.broadcasted_iota(jnp.int32, (Q, Q), 1)
    return rows >= cols, rows <= cols


def as_low(mask):
    return jnp.where(mask, 1.0, 0.0).astype(BF)


def halves(slab):
    lane = lax.broadcasted_iota(jnp.int32, slab.shape, 1)
    zero = jnp.zeros_like(slab)
    first = jnp.where(lane < HEADDIM, slab, zero)
    second = jnp.where(lane >= HEADDIM, slab, zero)
    return jnp.concatenate([first, second], axis=0)


def back_kernel(
    dy, colm, seg, xbc, pre_r, dtr, st_in, g_send, cwx, cwb, dtb, alog, dsk, ex, ext, branch, gz, go, tok,
    dx_o, dbc_o, ddt_o, small_o, out_o, oz, oo,
    states, acts, dpre, grad, heads, g_in, tail_r, ret_s, ret_r, near, relay, from_d, from_u, tok_r,
    sz, so, chunk, rg, cs, cr, send, recv, local_sem,
):
    shard, context, tensor, core, chip, chips, sibling, others, partner, ranks, group, at = places()
    own = pl.ds(pl.multiple_of(tensor * 256, 256), 256)
    fetch = pltpu.make_async_copy(tok.at[own], tok_r, local_sem.at[0])
    fetch.start()
    greet([partner, sibling, group[1], group[3]] + others[1:])
    links = Links(send, recv)
    carry_in = links.copy(g_send, g_in, partner)
    ring = Ring(links, tensor, group)
    ring.reduce_first(branch, near, from_d, from_u)
    sib_in = (links.copy(gz.at[:, 1 - core], sz, sibling), links.copy(go.at[:, 1 - core], so, sibling))
    a_neg = -jnp.exp(alog[...])
    causal, anti = triangles()
    lower = as_low(causal)
    upper = as_low(anti)
    expand = ex[...]
    expand_t = ext[...]
    dsk_e = mm2(dsk[...], expand)

    def head_sum(v):
        return mm2(v, expand_t)

    states[0] = st_in[...]

    def forward(b, carry):
        r = pl.ds(pl.multiple_of(b * Q, Q), Q)
        marks = colm[r]
        dt = softplus(dtr[r] + dtb[...])
        cum = mm3_left(lower, dt * a_neg)
        last = cum[Q - 1 : Q]
        tail = jnp.exp(last - cum) * marks[:, 6:7] * dt
        keep_e = mm2(jnp.exp(last) * marks[Q - 1 : Q, 5:6], expand)
        tail_e = mm2(tail, expand)
        pieces = []
        for c in range(6):
            lanes = slice(c * 128, c * 128 + 128)
            pre = pre_r[r, lanes]
            act = pre * sigmoid(pre)
            acts[r, lanes] = act
            if c < 4:
                pieces.append((act * tail_e[:, lanes]).astype(BF))
            if c == 4:
                b_low = act.astype(BF)
        fresh = mm_tn(b_low, jnp.concatenate(pieces, axis=1))
        states[b + 1] = keep_e * states[b] + fresh
        return carry

    lax.fori_loop(0, 7, forward, 0)
    r7 = slice(7 * Q, 8 * Q)
    for c in range(6):
        lanes = slice(c * 128, c * 128 + 128)
        pre = pre_r[r7, lanes]
        acts[r7, lanes] = pre * sigmoid(pre)
    for copy in sib_in:
        copy.wait_recv()

    def merge(c, carry):
        for mine, theirs, at in ((gz, sz, 0), (go, so, 512)):
            chunk[c, :, at : at + 512] = (mine[c, core].astype(F32) + theirs[c].astype(F32)).astype(BF)
        return carry

    lax.fori_loop(0, 8, merge, 0)
    grads_in = [links.copy(chunk.at[chips[k]], rg.at[k - 1], others[k]) for k in range(1, 8)]
    carry_in.wait_recv()
    grad[...] = jnp.where(context == 0, g_in[...].astype(F32), 0.0)
    heads[...] = jnp.zeros_like(heads)
    dpre[0:8] = jnp.zeros((8, 768), F32)
    dpre[1032:1040] = jnp.zeros((8, 768), F32)

    def backward(i, carry):
        b = 7 - i
        r = pl.ds(pl.multiple_of(b * Q, Q), Q)
        rp = pl.ds(pl.multiple_of(b * Q + 8, 8), Q)
        marks = colm[r]
        raw = dtr[r] + dtb[...]
        dt = softplus(raw)
        cum = mm3_left(lower, dt * a_neg)
        cum_t = cum.T
        last = cum[Q - 1 : Q]
        enter = jnp.exp(cum) * marks[:, 5:6]
        tail = jnp.exp(last - cum) * marks[:, 6:7]
        dt_e = mm2(dt, expand)
        enter_e = mm2(enter, expand)
        tail_e = mm2(tail, expand)
        keep_e = enter_e[Q - 1 : Q]
        b_low = acts[r, 512:640].astype(BF)
        c_low = acts[r, 640:768].astype(BF)
        state = states[b]
        state_low = state.astype(BF)
        g_now = grad[...]
        g_low = g_now.astype(BF)
        inter = mm(c_low, state_low)
        back = mm(b_low, g_low)
        mask = causal & (marks[:, 0:1] == seg[pl.ds(b, 1), :].astype(F32))
        scores = jnp.where(mask, mm_nt(c_low, b_low), 0.0)
        kept = jnp.sum(state * g_now, axis=0, keepdims=True) * keep_e
        entered, tailed, e_terms, q_terms, x_terms, k_terms = [], [], [], [], [], []
        rows, cols = [], []
        d_scores = jnp.zeros((Q, Q), F32)
        for p in range(4):
            lanes = slice(p * 128, p * 128 + 128)
            x = acts[r, lanes]
            dys = dy[r, lanes]
            xdt = x * dt_e[:, lanes]
            xdt_low = xdt.astype(BF)
            ed = enter_e[:, lanes] * dys
            tx = tail_e[:, lanes] * xdt
            entered.append(ed.astype(BF))
            tailed.append(tx.astype(BF))
            dy_two = halves(dys.astype(BF))
            dw_two = mm_nt(dy_two, xdt_low)
            ws = []
            for k in range(2):
                h = 2 * p + k
                decay = jnp.exp(jnp.minimum(cum[:, h : h + 1] - cum_t[h : h + 1, :], 0.0))
                weight = decay * scores
                dw = dw_two[k * Q : k * Q + Q]
                d_scores = d_scores + decay * dw
                both = weight * dw
                rows.append(jnp.sum(both, axis=1, keepdims=True))
                cols.append(jnp.sum(both, axis=0, keepdims=True))
                ws.append(weight.astype(BF))
            dxdt = mm_tn(jnp.concatenate(ws, axis=0), dy_two) + tail_e[:, lanes] * back[:, lanes]
            e_terms.append(ed * inter[:, lanes] - tx * back[:, lanes])
            q_terms.append(jnp.sum(tx * back[:, lanes], axis=0, keepdims=True) + kept[:, lanes])
            x_terms.append(dxdt * x)
            k_terms.append(jnp.sum(dys * x, axis=0, keepdims=True))
            pre = pre_r[r, lanes]
            sig = sigmoid(pre)
            dpre[rp, lanes] = (dxdt * dt_e[:, lanes] + dsk_e[:, lanes] * dys) * (sig * (1.0 + pre * (1.0 - sig)))
        entered = jnp.concatenate(entered, axis=1)
        tailed = jnp.concatenate(tailed, axis=1)
        ds_low = jnp.where(mask, d_scores, 0.0).astype(BF)
        d_c = mm_nt(entered, state_low) + mm(ds_low, b_low)
        d_b = mm_nt(tailed, g_low) + mm_tn(ds_low, c_low)
        grad[...] = keep_e * g_now + mm_tn(c_low, entered)
        for c, value in ((4, d_b), (5, d_c)):
            lanes = slice(c * 128, c * 128 + 128)
            pre = pre_r[r, lanes]
            sig = sigmoid(pre)
            dpre[rp, lanes] = value * (sig * (1.0 + pre * (1.0 - sig)))
        d_cum = jnp.concatenate(rows, axis=1) - jnp.concatenate(cols, axis=0).T
        d_cum = d_cum + head_sum(jnp.concatenate(e_terms, axis=1))
        d_log = mm3_left(upper, d_cum) + head_sum(jnp.concatenate(q_terms, axis=1))
        d_dt = d_log * a_neg + head_sum(jnp.concatenate(x_terms, axis=1))
        d_raw = d_dt * sigmoid(raw)
        ddt_o[r] = jnp.concatenate([d_raw, jnp.zeros((Q, 120), F32)], axis=1).astype(BF)
        heads[0:1] += jnp.sum(d_raw, axis=0, keepdims=True)
        heads[1:2] += jnp.sum(d_log * dt, axis=0, keepdims=True) * a_neg
        heads[2:3] += head_sum(jnp.concatenate(k_terms, axis=1))
        return carry

    lax.fori_loop(0, 1, backward, 0)
    ring.reduce_second(branch, near, relay, from_d, from_u)
    lax.fori_loop(1, 4, backward, 0)
    fetch.wait()
    ring.reduce_wait()

    def finish_out(i, carry):
        r = pl.ds(pl.multiple_of(i * 64, 64), 64)
        rt = pl.ds(pl.multiple_of(tensor * 256 + i * 64, 64), 64)
        total = branch[rt].astype(F32) + from_d[r].astype(F32) + from_u[r].astype(F32)
        out_o[rt] = (tok_r[r].astype(F32) + total).astype(BF)
        return carry

    lax.fori_loop(0, 4, finish_out, 0)
    ring.gather_first(out_o)
    lax.fori_loop(4, 8, backward, 0)
    small_o[...] = jnp.zeros_like(small_o)
    small_o[24:32, 0:8] = heads[...]

    for c in range(6):
        lanes = slice(c * 128, c * 128 + 128)
        first = dpre[0:16, lanes]
        cw, wl = (cwx, lanes) if c < 4 else (cwb, slice(c * 128 - 512, c * 128 - 384))
        flags = jnp.concatenate([jnp.zeros((8, 8), F32), colm[0:8]], axis=0)
        total = jnp.zeros((8, 128), F32)
        for d in range(1, 4):
            total = total + cw[3 - d : 4 - d, wl] * (first * flags[:, d : d + 1])[d : d + 8]
        ret_s[:, lanes] = total
    ret_in = links.copy(ret_s, ret_r, partner)
    ring.gather_second(out_o)
    for copy in grads_in:
        copy.wait_recv()
    for at in range(0, 1024, 128):
        lanes = slice(at, at + 128)
        cs[:, lanes] = add_slots(chunk[chip, :, lanes].astype(F32), rg, lanes).astype(BF)
    grads_ctx = links.copy(cs, cr, partner)
    for c in range(6):
        lanes = slice(c * 128, c * 128 + 128)
        cw, wl = (cwx, lanes) if c < 4 else (cwb, slice(c * 128 - 512, c * 128 - 384))

        def conv(b, sums, lanes=lanes, c=c, cw=cw, wl=wl):
            r = pl.ds(pl.multiple_of(b * Q, Q), Q)
            slab = dpre[pl.ds(pl.multiple_of(b * Q + 8, 8), Q + 8), lanes]
            marks = colm[pl.ds(pl.multiple_of(b * Q, Q), Q + 8)]
            xin = xbc[pl.ds(pl.multiple_of(b * Q, Q), Q + EDGE), lanes].astype(F32)
            main = slab[0:Q]
            out = cw[3:4, wl] * main
            new = [sums[0] + jnp.sum(main, axis=0, keepdims=True),
                   sums[1] + jnp.sum(main * xin[EDGE:], axis=0, keepdims=True)]
            for d in range(1, 4):
                masked = slab * marks[:, d : d + 1]
                out = out + cw[3 - d : 4 - d, wl] * masked[d : d + Q]
                new.append(sums[d + 1] + jnp.sum(masked[0:Q] * xin[EDGE - d : Q + EDGE - d], axis=0, keepdims=True))
            if c < 4:
                dx_o[r, lanes] = out.astype(BF)
            else:
                dbc_o[r, slice(c * 128 - 512, c * 128 - 384)] = out.astype(BF)

            @pl.when(b == 7)
            def _():
                tail_r[:, lanes] = out[Q - EDGE :]

            return tuple(new)

        zero = jnp.zeros((1, 128), F32)
        sums = lax.fori_loop(0, 8, conv, (zero,) * 5)
        at = 16 + c if c < 4 else 36 + c
        small_o[at : at + 1] = sums[0]
        for d in range(4):
            at = (3 - d) * 4 + c if c < 4 else 28 + (3 - d) * 2 + c
            small_o[at : at + 1] = sums[d + 1]
    ret_in.wait_recv()
    returned = jnp.where(context == 0, ret_r[...], 0.0)
    last = tail_r[...] + jnp.concatenate([jnp.zeros((EDGE - 8, 768), F32), returned], axis=0)
    dx_o[1024 - EDGE : 1024] = last[:, 0:512].astype(BF)
    dbc_o[1024 - EDGE : 1024] = last[:, 512:768].astype(BF)
    grads_ctx.wait_recv()
    oz[...] = cs[:, 0:512].astype(F32) + cr[:, 0:512].astype(F32)
    oo[...] = cs[:, 512:1024].astype(F32) + cr[:, 512:1024].astype(F32)
    ring.gather_wait(out_o)
    links.finish()


MESH = pl.DeviceIdType.MESH


class Links:
    def __init__(self, send, recv):
        self.send, self.recv, self.count, self.started = send, recv, 0, []

    def copy(self, src, dst, device):
        made = pltpu.make_async_remote_copy(
            src_ref=src,
            dst_ref=dst,
            send_sem=self.send.at[self.count],
            recv_sem=self.recv.at[self.count],
            device_id=device,
            device_id_type=MESH,
        )
        self.count += 1
        self.started.append(made)
        made.start()
        return made

    def finish(self):
        for made in self.started:
            made.wait_send()


def arrival(like, dst, links_recv, device):
    return pltpu.make_async_remote_copy(
        src_ref=dst, dst_ref=dst, send_sem=links_recv, recv_sem=links_recv, device_id=device, device_id_type=MESH
    )


def greet(devices):
    barrier = pltpu.get_barrier_semaphore()
    for device in devices:
        pl.semaphore_signal(barrier, inc=1, device_id=device, device_id_type=MESH)
    pl.semaphore_wait(barrier, len(devices))


def places():
    shard, context, tensor = (lax.axis_index(name) for name in ("shard", "context", "tensor"))
    core, chip = lax.rem(shard, 2), lax.div(shard, 2)

    def at(shard_to=None, context_to=None, tensor_to=None):
        return (
            shard if shard_to is None else shard_to,
            context if context_to is None else context_to,
            tensor if tensor_to is None else tensor_to,
        )

    chips = [None] + [lax.rem(chip + k, 8) for k in range(1, 8)]
    sibling = at(shard_to=chip * 2 + (1 - core))
    others = [None] + [at(shard_to=c * 2 + core) for c in chips[1:]]
    partner = at(context_to=1 - context)
    ranks = [None] + [lax.rem(tensor + k, 4) for k in range(1, 4)]
    group = [None] + [at(tensor_to=t) for t in ranks[1:]]
    return shard, context, tensor, core, chip, chips, sibling, others, partner, ranks, group, at


class Ring:
    def __init__(self, links, tensor, group):
        self.links, self.tensor = links, tensor
        self.up, self.down = group[1], group[3]
        self.t_up, self.t_down, self.t_far = (lax.rem(tensor + k, 4) for k in (1, 3, 2))

    def half(self, rank, which):
        return pl.ds(pl.multiple_of(rank * 256 + which * 128, 128), 128)

    def whole(self, rank):
        return pl.ds(pl.multiple_of(rank * 256, 256), 256)

    def reduce_first(self, src, near, from_down, from_up, make=None):
        def send(rank, which, dst, device):
            rows = self.half(rank, which)
            if make is not None:
                make(rows)
            return self.links.copy(src.at[rows], dst, device)

        self.first = (send(self.t_far, 0, near.at[0], self.up), send(self.t_far, 1, near.at[1], self.down))
        self.alone = (
            send(self.t_up, 1, from_down.at[pl.ds(128, 128)], self.up),
            send(self.t_down, 0, from_up.at[pl.ds(0, 128)], self.down),
        )

    def reduce_second(self, src, near, relay, from_down, from_up):
        copy = self.links.copy
        self.first[0].wait_recv()
        relay[0] = (near[0].astype(F32) + src[self.half(self.t_up, 0)].astype(F32)).astype(BF)
        up = copy(relay.at[0], from_down.at[pl.ds(0, 128)], self.up)
        self.first[1].wait_recv()
        relay[1] = (near[1].astype(F32) + src[self.half(self.t_down, 1)].astype(F32)).astype(BF)
        down = copy(relay.at[1], from_up.at[pl.ds(128, 128)], self.down)
        self.summed = (up, down)

    def reduce_wait(self):
        for made in self.alone + self.summed:
            made.wait_recv()

    def gather_first(self, ref):
        mine = ref.at[self.whole(self.tensor)]
        self.base = self.links.count
        self.links.copy(mine, mine, self.up)
        self.links.copy(mine, mine, self.down)

    def landed(self, slot, which, device):
        arrival(None, slot, self.links.recv.at[self.base + which], device).wait_recv()

    def gather_second(self, ref):
        self.landed(ref.at[self.whole(self.t_down)], 0, self.down)
        self.base2 = self.links.count
        up = ref.at[self.half(self.t_down, 0)]
        self.links.copy(up, up, self.up)
        self.landed(ref.at[self.whole(self.t_up)], 1, self.up)
        down = ref.at[self.half(self.t_up, 1)]
        self.links.copy(down, down, self.down)

    def gather_wait(self, ref):
        offset = self.base2 - self.base
        self.landed(ref.at[self.half(self.t_far, 0)], offset, self.down)
        self.landed(ref.at[self.half(self.t_far, 1)], offset + 1, self.up)


class Spread:
    def __init__(self, mine, out, base, send, recv, core, chip, at):
        self.mine, self.out, self.base, self.send, self.recv, self.core, self.chip = mine, out, base, send, recv, core, chip
        x = lax.rem(chip, 4)
        right, left, far = (chip - x + lax.rem(x + k, 4) for k in (1, 3, 2))
        over = lax.rem(chip + 4, 8)
        o_right, o_left, o_far = (lax.rem(c + 4, 8) for c in (right, left, far))
        there = [at(shard_to=c * 2 + core) for c in (over, right, left)]
        sibling = at(shard_to=chip * 2 + (1 - core))
        to_over, to_right, to_left = there
        self.copies = [
            (None, None, to_over), (None, None, to_right), (None, None, to_left), (None, None, sibling),
            (over, None, to_right), (over, None, to_left),
            (left, 0, to_right), (right, 1, to_left), (o_left, 0, to_right), (o_right, 1, to_left),
        ]
        owners = [over, left, right, o_left, o_right, far, o_far]
        self.copies += [(owner, None, sibling) for owner in owners]
        self.arrivals = [
            (over, None, core), (left, None, core), (right, None, core), (chip, None, 1 - core), (o_left, None, core), (o_right, None, core),
            (far, 0, core), (far, 1, core), (o_far, 0, core), (o_far, 1, core),
        ]
        self.arrivals += [(owner, None, 1 - core) for owner in owners]

    def slot(self, owner, core, half):
        start = (owner * 2 + core) * 64
        if half is None:
            return self.out.at[pl.ds(pl.multiple_of(start, 64), 64)]
        return self.out.at[pl.ds(pl.multiple_of(start + half * 32, 32), 32)]

    def copy(self, i):
        owner, half, device = self.copies[i]
        dst = self.slot(self.chip if owner is None else owner, self.core, half)
        src = self.mine if owner is None else dst
        return pltpu.make_async_remote_copy(
            src_ref=src, dst_ref=dst, send_sem=self.send.at[self.base + i], recv_sem=self.recv.at[self.base + i],
            device_id=device, device_id_type=MESH,
        )

    def wait(self, i):
        owner, half, core = self.arrivals[i]
        arrival(None, self.slot(owner, core, half), self.recv.at[self.base + i], self.copies[i][2]).wait_recv()

    def begin(self):
        for i in (0, 1, 2, 3):
            self.copy(i).start()
        self.out[pl.ds(pl.multiple_of((self.chip * 2 + self.core) * 64, 64), 64)] = self.mine[...]

    def event(self, n):
        waits, starts = (
            ((1,), (6, 11)), ((2,), (7, 12)), ((0,), (4, 5, 10)), ((6, 7), (15,)),
            ((4,), (8, 13)), ((5,), (9, 14)), ((8, 9), (16,)),
        )[n]
        for i in waits:
            self.wait(i)
        for i in starts:
            self.copy(i).start()

    def collect(self):
        for i in (3,) + tuple(range(10, 17)):
            self.wait(i)

    def sent(self):
        for i in range(17):
            self.copy(i).wait_send()


def forward_kernel(
    wz, wx, wbc, wdt, norm, wo, tok, cot, seg, cwx, cwb, cbx, cbb, dtb, alog, dsk, gg, ex, ext,
    in_o, zo_o, xn_o, xbc_o, pre_o, dtr_o, colm_o, gain_o, st_o, dy_o, dz_o, branch_o, carry_o, gate_o, gz_o, go_o,
    mine1, mine2, etok_b, eseg, xs, st, st_low, st_in, y_s, er_s, c_s, z_s, dn_s, row_s, row_r, yn_o, send, recv,
):
    shard, context, tensor, core, chip, chips, sibling, others, partner, ranks, group, at = places()
    mine1[:, 0:512] = wx[...]
    mine1[:, 512:768] = wbc[...]
    mine1[:, 768:896] = jnp.zeros((64, 128), BF)
    mine1[:, 768:776] = wdt[...]
    mine1[:, 776:777] = jnp.broadcast_to(norm[...].astype(F32), (8, 64)).T[:, 0:1].astype(BF)
    mine2[:, 0:512] = wz[...]
    mine2[:, 512:1024] = wo[...]
    greet([sibling, partner] + others[1:] + group[1:])
    links = Links(send, recv)

    links.count = 34
    seg_in = links.copy(seg, eseg, partner)
    tokens_in = links.copy(tok.at[pl.ds(1024 - EDGE, EDGE)], etok_b, partner)
    spread1 = Spread(mine1, in_o, 0, send, recv, core, chip, at)
    spread2 = Spread(mine2, zo_o, 17, send, recv, core, chip, at)
    spread1.begin()
    seg_in.wait_recv()
    seg_t = seg[...].astype(F32).T
    edge_t = jnp.where(context > 0, eseg[...].astype(F32).T, 0.0)
    edge_col = edge_t[120:128, 7:8]
    start = jnp.where(edge_col[7:8] == seg_t[0:1, 0:1], seg_t[0:1, 0:1], -1.0)
    colm_o[1024:1032] = jnp.zeros((8, 8), F32)
    for b in range(8):
        col = seg_t[:, b : b + 1]
        before = edge_col if b == 0 else seg_t[120:128, b - 1 : b]
        longer = jnp.concatenate([before, col], axis=0)
        entering = start if b == 0 else before[7:8]
        marks = [col]
        for d in range(1, 4):
            marks.append(jnp.where(longer[8 - d : 136 - d] == col, 1.0, 0.0))
        for value in (start, entering, col[127:128]):
            marks.append(jnp.where(col == value, 1.0, 0.0))
        marks.append(jnp.zeros_like(col))
        colm_o[b * Q : b * Q + Q] = jnp.concatenate(marks, axis=1)

    for n in range(7):
        spread1.event(n)
    spread2.begin()
    spread1.collect()
    tokens_in.wait_recv()

    a_neg = -jnp.exp(alog[...])
    causal, _ = triangles()
    lower = as_low(causal)
    gain_row = in_o[:, 768:896].astype(F32).T[8:9]
    gain_o[...] = gain_row

    def normed(block):
        plain = block.astype(F32)
        root = lax.rsqrt(jnp.mean(plain * plain, axis=1, keepdims=True) + EPSILON)
        return (plain * root * gain_row).astype(BF)

    edge_tokens = jnp.where(context > 0, etok_b[...].astype(F32), 0.0)
    edge = mm(normed(edge_tokens), in_o[:, 0:768]).astype(BF)
    xbc_o[0:EDGE] = edge
    xs[0:EDGE] = edge.astype(F32)
    st[...] = jnp.zeros_like(st)
    expand = ex[...]
    dsk_e = mm2(dsk[...], expand)

    def body(b, run):
        r = pl.ds(pl.multiple_of(b * Q, Q), Q)
        rn = pl.ds(pl.multiple_of(b * Q + EDGE, EDGE), Q)
        xn = normed(tok[r])
        xn_o[r] = xn
        both = mm(xn, in_o[...])
        xb = both[:, 0:768].astype(BF)
        xbc_o[rn] = xb
        xs[rn] = xb.astype(F32)
        raw = both[:, 768:776]
        dtr_o[r] = raw
        marks = colm_o[r]
        acts = []
        for c in range(6):
            lanes = slice(c * 128, c * 128 + 128)
            cw, cb, at = (cwx, cbx, lanes) if c < 4 else (cwb, cbb, slice(c * 128 - 512, c * 128 - 384))
            slab = xs[pl.ds(pl.multiple_of(b * Q, Q), Q + EDGE), lanes]
            pre = cb[:, at] + cw[3:4, at] * slab[EDGE:]
            for d in range(1, 4):
                pre = pre + (cw[3 - d : 4 - d, at] * slab[EDGE - d : Q + EDGE - d]) * marks[:, d : d + 1]
            pre_o[r, lanes] = pre
            acts.append(pre * sigmoid(pre))
        b_low = acts[4].astype(BF)
        c_low = acts[5].astype(BF)
        c_s[r] = c_low
        dt = softplus(raw + dtb[...])
        cum = mm3_left(lower, dt * a_neg)
        er_s[r] = jnp.exp(run + cum) * marks[:, 4:5]
        cum_t = cum.T
        last = cum[Q - 1 : Q]
        enter = jnp.exp(cum) * marks[:, 5:6]
        tail = jnp.exp(last - cum) * marks[:, 6:7]
        dt_e = mm2(dt, expand)
        enter_e = mm2(enter, expand)
        tail_e = mm2(tail, expand)
        mask = causal & (marks[:, 0:1] == seg[pl.ds(b, 1), :].astype(F32))
        scores = jnp.where(mask, mm_nt(c_low, b_low), 0.0)
        state = st[...]
        inter = mm(c_low, state.astype(BF))
        pieces = []
        for p in range(4):
            lanes = slice(p * 128, p * 128 + 128)
            xdt = acts[p] * dt_e[:, lanes]
            pieces.append((xdt * tail_e[:, lanes]).astype(BF))
            ws = []
            for h in (2 * p, 2 * p + 1):
                decay = jnp.exp(jnp.minimum(cum[:, h : h + 1] - cum_t[h : h + 1, :], 0.0))
                ws.append((decay * scores).astype(BF))
            intra = mm(jnp.concatenate(ws, axis=1), halves(xdt.astype(BF)))
            y_s[r, lanes] = intra + enter_e[:, lanes] * inter[:, lanes] + dsk_e[:, lanes] * acts[p]
        fresh = mm_tn(b_low, jnp.concatenate(pieces, axis=1))
        st[...] = enter_e[Q - 1 : Q] * state + fresh

        for n in range(7):
            pl.when(b == n)(partial(spread2.event, n))

        return run + last

    lax.fori_loop(0, 8, body, jnp.zeros((1, 8), F32))
    st_low[...] = st[...].astype(BF)
    state_in = links.copy(st_low, st_in, partner)
    spread2.collect()

    def project(b, carry):
        r = pl.ds(pl.multiple_of(b * Q, Q), Q)
        z_s[r] = mm(xn_o[r], zo_o[:, 0:512])
        dn_s[r] = mm(cot[r], zo_o[:, 512:1024])
        return carry

    lax.fori_loop(0, 8, project, 0)
    state_in.wait_recv()
    st_o[...] = jnp.where(context > 0, st_in[...].astype(F32), 0.0)

    def sums(b, carry):
        r = pl.ds(pl.multiple_of(b * Q, Q), Q)
        y = y_s[r] + mm2(er_s[r], expand) * mm(c_s[r], st_o[...].astype(BF))
        y_s[r] = y
        z = z_s[r]
        gated = y * (z * sigmoid(z))
        first_sum = jnp.sum(gated * gated, axis=1, keepdims=True)
        second_sum = jnp.sum(dn_s[r] * gg[...] * gated, axis=1, keepdims=True)
        row_s[b] = jnp.concatenate([first_sum, second_sum, jnp.zeros((Q, 6), F32)], axis=1).T
        return carry

    lax.fori_loop(0, 8, sums, 0)
    rows_in = [links.copy(row_s, row_r.at[k - 1], group[k]) for k in range(1, 4)]
    for copy in rows_in:
        copy.wait_recv()
    gate_o[...] = jnp.zeros_like(gate_o)
    st[...] = jnp.zeros_like(st)

    def finish(b, carry):
        r = pl.ds(pl.multiple_of(b * Q, Q), Q)
        total = (row_s[b] + row_r[0, b] + row_r[1, b] + row_r[2, b]).T
        root = lax.rsqrt(total[:, 0:1] * (1.0 / INNER) + EPSILON)
        cross = (root * root * root) * (total[:, 1:2] * (1.0 / INNER))
        er_e = mm2(er_s[r], expand)
        normals, carries = [], []
        for p in range(4):
            lanes = slice(p * 128, p * 128 + 128)
            y = y_s[r, lanes]
            z = z_s[r, lanes]
            dn = dn_s[r, lanes]
            sig = sigmoid(z)
            gate = z * sig
            gated = y * gate
            scaled = gated * root
            normals.append((scaled * gg[:, lanes]).astype(BF))
            gate_o[p : p + 1] += jnp.sum(dn * scaled, axis=0, keepdims=True)
            d_gated = root * (dn * gg[:, lanes]) - gated * cross
            d_y = d_gated * gate
            dy_o[r, lanes] = d_y
            dz_o[r, lanes] = (d_gated * y * (sig * (1.0 + z * (1.0 - sig)))).astype(BF)
            carries.append((d_y * er_e[:, lanes]).astype(BF))
        low = jnp.concatenate(normals, axis=1)
        yn_o[r] = low
        branch_o[r] = mm_nt(low, zo_o[:, 512:1024]).astype(BF)
        st[...] += mm_tn(c_s[r], jnp.concatenate(carries, axis=1))
        return carry

    lax.fori_loop(0, 8, finish, 0)
    carry_o[...] = st[...].astype(BF)
    for m in range(8):
        lanes = slice(m * 128, m * 128 + 128)
        gz_o[m] = mm_tn(xn_o[:, lanes], dz_o[...]).astype(BF).reshape(2, 64, 512)
        go_o[m] = mm_tn(cot[:, lanes], yn_o[...]).astype(BF).reshape(2, 64, 512)
    links.finish()
    spread1.sent()
    spread2.sent()


def add_slots(total, slots, lanes):
    for k in range(7):
        total = total + slots[k, :, lanes].astype(F32)
    return total


def tail_kernel(
    dz, dx, ddt, dbc, small, gate, gain, w_in, w_zo, xn, tok, cot,
    dtok_o, ox, odt, obc, onorm, conv_o, convb_o, bc_o, bcb_o, gate_o, dtb_o, alog_o, dsk_o,
    part, gx, near, relay, from_d, from_u, sx, chunk, rg, cs, cr, t2,
    sm, sm_s, sm_c, sm_x, sm_r, sm_t, nm, nm_s, nm_c, nm_x, nm_r, nm_t, tok_r, cot_r, send, recv, local_sem,
):
    shard, context, tensor, core, chip, chips, sibling, others, partner, ranks, group, at = places()
    own = pl.ds(pl.multiple_of(tensor * 256, 256), 256)
    fetch = [
        pltpu.make_async_copy(tok.at[own], tok_r, local_sem.at[0]),
        pltpu.make_async_copy(cot.at[own], cot_r, local_sem.at[1]),
    ]
    for copy in fetch:
        copy.start()
    greet([sibling, partner] + others[1:] + group[1:])
    links = Links(send, recv)
    sm[...] = small[...]
    sm[20:24] = gate[...]
    wide = Ring(links, tensor, group)

    def make(r):
        total = mm_nt(dz[r], w_zo[:, 0:512]) + mm_nt(dx[r], w_in[:, 0:512]) + mm_nt(ddt[r], w_in[:, 768:896]) + mm_nt(dbc[r], w_in[:, 512:768])
        part[r] = total.astype(BF)

    wide.reduce_first(part, near, from_d, from_u, make)
    small_in = links.copy(sm, sm_s, sibling)

    def outer(m):
        block = xn[:, m * 128 : m * 128 + 128]
        gx[m, :, :, 0:512] = mm_tn(block, dx[...]).astype(BF).reshape(2, 64, 512)
        gx[m, :, :, 512:640] = mm_tn(block, ddt[...]).astype(BF).reshape(2, 64, 128)
        gx[m, :, :, 640:896] = mm_tn(block, dbc[...]).astype(BF).reshape(2, 64, 256)

    make(wide.half(wide.t_up, 0))
    make(wide.half(wide.t_down, 1))
    for m in range(4):
        outer(m)
    wide.reduce_second(part, near, relay, from_d, from_u)
    for m in range(4, 8):
        outer(m)
    sib_in = links.copy(gx.at[:, 1 - core], sx, sibling)
    small_in.wait_recv()
    sm_c[chip] = sm[...] + sm_s[...]
    small_base = links.count - 1
    for k in range(1, 8):
        links.copy(sm_c.at[chip], sm_c.at[chip], others[k])
    make(wide.half(tensor, 0))
    make(wide.half(tensor, 1))
    sib_in.wait_recv()

    def merge(c, carry):
        chunk[c] = (gx[c, core].astype(F32) + sx[c].astype(F32)).astype(BF)
        return carry

    lax.fori_loop(0, 8, merge, 0)
    grads_in = [links.copy(chunk.at[chips[k]], rg.at[k - 1], others[k]) for k in range(1, 8)]

    for copy in fetch:
        copy.wait()
    wide.reduce_wait()

    def inner(i, g_norm):
        r = pl.ds(pl.multiple_of(i * 64, 64), 64)
        rt = pl.ds(pl.multiple_of(tensor * 256 + i * 64, 64), 64)
        total = part[rt].astype(F32) + from_d[r].astype(F32) + from_u[r].astype(F32)
        plain = tok_r[r].astype(F32)
        root = lax.rsqrt(jnp.mean(plain * plain, axis=1, keepdims=True) + EPSILON)
        stat = plain * root
        d_plain = total * gain[...]
        mean = jnp.mean(d_plain * plain, axis=1, keepdims=True)
        dtok_o[rt] = (cot_r[r].astype(F32) + root * d_plain - stat * (root * root) * mean).astype(BF)
        return g_norm + jnp.sum(total * stat, axis=0, keepdims=True)

    g_norm = lax.fori_loop(0, 4, inner, jnp.zeros((1, 1024), F32))
    wide.gather_first(dtok_o)
    for c in range(8):
        nm[c : c + 1] = g_norm[:, c * 128 : c * 128 + 128]
    norm_sib = links.copy(nm, nm_s, sibling)

    for k in range(1, 8):
        source = lax.rem(chip + 8 - k, 8)
        arrival(None, sm_c.at[source], recv.at[small_base + k], others[k]).wait_recv()
    total = sm_c[0]
    for c in range(1, 8):
        total = total + sm_c[c]
    sm_x[...] = total
    small_ctx = links.copy(sm_x, sm_r, partner)
    norm_sib.wait_recv()
    nm_c[chip] = nm[...] + nm_s[...]
    norm_base = links.count - 1
    for k in range(1, 8):
        links.copy(nm_c.at[chip], nm_c.at[chip], others[k])
    for copy in grads_in:
        copy.wait_recv()
    for col in range(0, 896, 128):
        lanes = slice(col, col + 128)
        cs[:, lanes] = add_slots(chunk[chip, :, lanes].astype(F32), rg, lanes).astype(BF)
    grads_ctx = links.copy(cs, cr, partner)
    wide.gather_second(dtok_o)
    for k in range(1, 8):
        source = lax.rem(chip + 8 - k, 8)
        arrival(None, nm_c.at[source], recv.at[norm_base + k], others[k]).wait_recv()
    total = nm_c[0]
    for c in range(1, 8):
        total = total + nm_c[c]
    nm_x[...] = total
    norm_ctx = links.copy(nm_x, nm_r, partner)
    small_ctx.wait_recv()
    sums = sm_x[...] + sm_r[...]
    for k in range(4):
        for p in range(4):
            conv_o[k : k + 1, p * 128 : p * 128 + 128] = sums[k * 4 + p : k * 4 + p + 1]
    for p in range(4):
        convb_o[:, p * 128 : p * 128 + 128] = sums[16 + p : 17 + p]
        gate_o[:, p * 128 : p * 128 + 128] = sums[20 + p : 21 + p]
    dtb_o[...] = sums[24:25, 0:8]
    alog_o[...] = sums[25:26, 0:8]
    dsk_o[...] = sums[26:27, 0:8]
    sm_t[tensor] = sums[32:48]
    small_t = links.count
    for k in range(1, 4):
        links.copy(sm_t.at[tensor], sm_t.at[tensor], group[k])
    norm_ctx.wait_recv()
    nm_t[tensor] = nm_x[...] + nm_r[...]
    norm_t = links.count
    for k in range(1, 4):
        links.copy(nm_t.at[tensor], nm_t.at[tensor], group[k])
    grads_ctx.wait_recv()
    ox[...] = cs[:, 0:512].astype(F32) + cr[:, 0:512].astype(F32)
    t2[tensor] = cs[:, 640:896].astype(F32) + cr[:, 640:896].astype(F32)
    grads2_t = links.count
    for k in range(1, 4):
        links.copy(t2.at[tensor], t2.at[tensor], group[k])
    odt[...] = (cs[:, 512:640].astype(F32) + cr[:, 512:640].astype(F32))[:, 0:8]
    for k in range(1, 4):
        source = lax.rem(tensor + 4 - k, 4)
        arrival(None, sm_t.at[source], recv.at[small_t + k - 1], group[k]).wait_recv()
        arrival(None, nm_t.at[source], recv.at[norm_t + k - 1], group[k]).wait_recv()
        arrival(None, t2.at[source], recv.at[grads2_t + k - 1], group[k]).wait_recv()
    sums = (sm_t[0] + sm_t[1]) + (sm_t[2] + sm_t[3])
    for k in range(4):
        for p in range(2):
            bc_o[k : k + 1, p * 128 : p * 128 + 128] = sums[k * 2 + p : k * 2 + p + 1]
    for p in range(2):
        bcb_o[:, p * 128 : p * 128 + 128] = sums[8 + p : 9 + p]
    obc[...] = (t2[0] + t2[1]) + (t2[2] + t2[3])
    nm_s[...] = (nm_t[0] + nm_t[1]) + (nm_t[2] + nm_t[3])
    row = nm_s[pl.ds(chip, 1), :]
    onorm[...] = jnp.where(core == 0, row[:, 0:64], row[:, 64:128])
    wide.gather_wait(dtok_o)
    links.finish()


def call(kernel, out_shapes, scratch, *args, specs=None, collective_id=None):
    return pl.pallas_call(
        kernel,
        out_shape=[jax.ShapeDtypeStruct(s, d) for s, d in out_shapes],
        in_specs=[pl.BlockSpec(memory_space=pl.ANY if n in (specs or ()) else pltpu.VMEM) for n in range(len(args))],
        out_specs=[pl.BlockSpec(memory_space=pltpu.VMEM)] * len(out_shapes),
        scratch_shapes=[pltpu.SemaphoreType.DMA(s) if d is None else pltpu.VMEM(s, d) for s, d in scratch],
        compiler_params=pltpu.CompilerParams(vmem_limit_bytes=VMEM_LIMIT, collective_id=collective_id, has_side_effects=collective_id is not None
        ),
    )(*args)


def local(
    tokens,
    segment,
    norm_gain,
    w_z,
    w_x,
    w_dt,
    w_bc,
    conv_x,
    conv_xb,
    conv_bc,
    conv_bcb,
    dt_bias,
    a_log,
    d_skip,
    gate_gain,
    w_out,
    cotangent,
):
    length = tokens.shape[0]
    head_count = dt_bias.shape[0]
    inner_width = head_count * HEADDIM
    bc_width = 2 * STATE
    seg = segment.reshape(8, 128)
    expand_np = np.kron(np.eye(8), np.ones((1, HEADDIM)))
    expand = jnp.asarray(expand_np, BF)
    expand_t = jnp.asarray(expand_np.T, BF)
    wide = (length, inner_width)
    state = (STATE, inner_width)
    grid = (8, 2, 64, 512)
    heads = (dt_bias[None], a_log[None], d_skip[None])
    (w_in, w_zo, x_normed, xbc, pre, dt_raw, colm, gain_row, state_in, d_y, d_z, branch_part, d_carry, g_gate_gain, g_w_z, g_w_out) = call(
        forward_kernel,
        [((1024, 896), BF), ((1024, 1024), BF), ((length, 1024), BF), ((length + EDGE, 768), BF), ((length, 768), F32), ((length, 8), F32),
         ((length + 8, 8), F32), ((1, 1024), F32), (state, F32), (wide, F32), (wide, BF), ((length, 1024), BF), (state, BF), ((4, 128), F32), (grid, BF), (grid, BF)],
        [((64, 896), BF), ((64, 1024), BF), ((EDGE, 1024), BF), ((8, 128), jnp.int32), ((length + EDGE, 768), F32), (state, F32), (state, BF), (state, BF),
         (wide, F32), ((length, 8), F32), ((length, STATE), BF), (wide, F32), (wide, F32), ((8, 8, 128), F32), ((3, 8, 8, 128), F32), (wide, BF),
         ((48,), None), ((48,), None)],
        w_z, w_x, w_bc, w_dt, norm_gain[None], w_out, tokens, cotangent, seg,
        conv_x, conv_bc, conv_xb[None], conv_bcb[None], *heads, gate_gain[None], expand, expand_t,
        collective_id=1,
    )
    own = (64, 512)

    def vector(shape, last):
        return [(s, F32) for s in (shape, shape, (8,) + shape, shape, shape, last)]

    half = ((2, 128, 1024), BF)
    rows = ((256, 1024), BF)
    d_x_low, d_bc, d_dt_low, small, output, o_z, o_out = call(
        back_kernel,
        [(wide, BF), ((length, 2 * STATE), BF), ((length, 128), BF), ((48, 128), F32), ((length, 1024), BF), (own, F32), (own, F32)],
        [((8, STATE, inner_width), F32), ((length, 768), F32), ((length + 16, 768), F32), (state, F32), ((8, 8), F32),
         (state, BF), ((EDGE, 768), F32), ((8, 768), F32), ((8, 768), F32),
         half, half, rows, rows, rows,
         ((8, 64, 512), BF), ((8, 64, 512), BF), ((8, 64, 1024), BF), ((7, 64, 1024), BF), ((64, 1024), BF), ((64, 1024), BF),
         ((32,), None), ((32,), None), ((1,), None)],
        d_y, colm, seg, xbc, pre, dt_raw, state_in, d_carry, conv_x, conv_bc, *heads, expand, expand_t,
        branch_part, g_w_z, g_w_out, tokens,
        specs=(18,), collective_id=3,
    )
    d_tokens, o_x, o_dt, o_bc, o_norm, conv_o, convb_o, cbc_o, cbcb_o, gate_o, dtb_o, alog_o, dsk_o = call(
        tail_kernel,
        [((length, 1024), BF), (own, F32), ((64, 8), F32), ((64, 256), F32), ((1, 64), F32),
         ((4, 512), F32), ((1, 512), F32), ((4, 256), F32), ((1, 256), F32), ((1, 512), F32), ((1, 8), F32), ((1, 8), F32), ((1, 8), F32)],
        [((length, 1024), BF), ((8, 2, 64, 896), BF), half, half, rows, rows,
         ((8, 64, 896), BF), ((8, 64, 896), BF), ((7, 64, 896), BF), ((64, 896), BF), ((64, 896), BF), ((4, 64, 256), F32),
         *vector((48, 128), (4, 16, 128)), *vector((8, 128), (4, 8, 128)),
         rows, rows, ((64,), None), ((64,), None), ((2,), None)],
        d_z, d_x_low, d_dt_low, d_bc, small, g_gate_gain, gain_row, w_in, w_zo, x_normed, tokens, cotangent,
        specs=(10, 11), collective_id=2,
    )
    return (
        output, d_tokens, o_norm[0], o_z, o_x, o_dt, o_bc, conv_o, convb_o[0], cbc_o, cbcb_o[0],
        dtb_o[0], alog_o[0], dsk_o[0], gate_o[0], o_out,
    )


def solution(mesh):
    in_specs = (
        P(("shard", "context"), None),
        P(("shard", "context")),
        P("shard"),
        P("shard", "tensor"),
        P("shard", "tensor"),
        P("shard", "tensor"),
        P("shard", None),
        P(None, "tensor"),
        P("tensor"),
        P(),
        P(),
        P("tensor"),
        P("tensor"),
        P("tensor"),
        P("tensor"),
        P("shard", "tensor"),
        P(("shard", "context"), None),
    )
    out_specs = (
        P(("shard", "context"), None),
        P(("shard", "context"), None),
        P("shard"),
        P("shard", "tensor"),
        P("shard", "tensor"),
        P("shard", "tensor"),
        P("shard", None),
        P(None, "tensor"),
        P("tensor"),
        P(),
        P(),
        P("tensor"),
        P("tensor"),
        P("tensor"),
        P("tensor"),
        P("shard", "tensor"),
    )
    return jax.shard_map(local, mesh=mesh, in_specs=in_specs, out_specs=out_specs, check_vma=False)
```

```python
from functools import partial

import jax
import jax.numpy as jnp
import numpy as np
from jax import lax
from jax.experimental import pallas as pl
from jax.experimental.pallas import tpu as pltpu
from jax.sharding import PartitionSpec as P

HEADDIM = 64
STATE = 128
CONV = 4
INNER = 2048


EPSILON = 1e-05


F32 = jnp.float32
BF = jnp.bfloat16
Q = 128
EDGE = 16
VMEM_LIMIT = 58 * 1024 * 1024


def mm(a, b):
    return lax.dot_general(a, b, (((1,), (0,)), ((), ())), preferred_element_type=F32)


def mm_nt(a, b):
    return lax.dot_general(a, b, (((1,), (1,)), ((), ())), preferred_element_type=F32)


def mm_tn(a, b):
    return lax.dot_general(a, b, (((0,), (0,)), ((), ())), preferred_element_type=F32)


def split2(v):
    hi = v.astype(BF)
    return hi, (v - hi.astype(F32)).astype(BF)


def mm2(a, b):
    hi, lo = split2(a)
    return mm(hi, b) + mm(lo, b)


def mm3_left(a, b):
    hi, lo = split2(b)
    lo2 = (b - hi.astype(F32) - lo.astype(F32)).astype(BF)
    return mm(a, hi) + (mm(a, lo) + mm(a, lo2))


def softplus(v):
    return jnp.maximum(v, 0.0) + jnp.log1p(jnp.exp(-jnp.abs(v)))


def sigmoid(v):
    return 1.0 / (1.0 + jnp.exp(-v))


def triangles():
    rows = lax.broadcasted_iota(jnp.int32, (Q, Q), 0)
    cols = lax.broadcasted_iota(jnp.int32, (Q, Q), 1)
    return rows >= cols, rows <= cols


def as_low(mask):
    return jnp.where(mask, 1.0, 0.0).astype(BF)


def halves(slab):
    lane = lax.broadcasted_iota(jnp.int32, slab.shape, 1)
    zero = jnp.zeros_like(slab)
    first = jnp.where(lane < HEADDIM, slab, zero)
    second = jnp.where(lane >= HEADDIM, slab, zero)
    return jnp.concatenate([first, second], axis=0)


MESH = pl.DeviceIdType.MESH


class Links:
    def __init__(self, send, recv):
        self.send, self.recv, self.count, self.started = send, recv, 0, []

    def copy(self, src, dst, device):
        made = pltpu.make_async_remote_copy(
            src_ref=src,
            dst_ref=dst,
            send_sem=self.send.at[self.count],
            recv_sem=self.recv.at[self.count],
            device_id=device,
            device_id_type=MESH,
        )
        self.count += 1
        self.started.append(made)
        made.start()
        return made

    def finish(self):
        for made in self.started:
            made.wait_send()


def arrival(like, dst, links_recv, device):
    return pltpu.make_async_remote_copy(
        src_ref=dst, dst_ref=dst, send_sem=links_recv, recv_sem=links_recv, device_id=device, device_id_type=MESH
    )


def greet(devices):
    barrier = pltpu.get_barrier_semaphore()
    for device in devices:
        pl.semaphore_signal(barrier, inc=1, device_id=device, device_id_type=MESH)
    pl.semaphore_wait(barrier, len(devices))


def places():
    shard, context, tensor = (lax.axis_index(name) for name in ("shard", "context", "tensor"))
    core, chip = lax.rem(shard, 2), lax.div(shard, 2)

    def at(shard_to=None, context_to=None, tensor_to=None):
        return (
            shard if shard_to is None else shard_to,
            context if context_to is None else context_to,
            tensor if tensor_to is None else tensor_to,
        )

    chips = [None] + [lax.rem(chip + k, 8) for k in range(1, 8)]
    sibling = at(shard_to=chip * 2 + (1 - core))
    others = [None] + [at(shard_to=c * 2 + core) for c in chips[1:]]
    partner = at(context_to=1 - context)
    ranks = [None] + [lax.rem(tensor + k, 4) for k in range(1, 4)]
    group = [None] + [at(tensor_to=t) for t in ranks[1:]]
    return shard, context, tensor, core, chip, chips, sibling, others, partner, ranks, group, at


class Ring:
    def __init__(self, links, tensor, group):
        self.links, self.tensor = links, tensor
        self.up, self.down = group[1], group[3]
        self.t_up, self.t_down, self.t_far = (lax.rem(tensor + k, 4) for k in (1, 3, 2))

    def half(self, rank, which):
        return pl.ds(pl.multiple_of(rank * 256 + which * 128, 128), 128)

    def whole(self, rank):
        return pl.ds(pl.multiple_of(rank * 256, 256), 256)

    def reduce_first(self, src, near, from_down, from_up, make=None):
        def send(rank, which, dst, device):
            rows = self.half(rank, which)
            if make is not None:
                make(rows)
            return self.links.copy(src.at[rows], dst, device)

        self.first = (send(self.t_far, 0, near.at[0], self.up), send(self.t_far, 1, near.at[1], self.down))
        self.alone = (
            send(self.t_up, 1, from_down.at[pl.ds(128, 128)], self.up),
            send(self.t_down, 0, from_up.at[pl.ds(0, 128)], self.down),
        )

    def reduce_second(self, src, near, relay, from_down, from_up):
        copy = self.links.copy
        self.first[0].wait_recv()
        relay[0] = (near[0].astype(F32) + src[self.half(self.t_up, 0)].astype(F32)).astype(BF)
        up = copy(relay.at[0], from_down.at[pl.ds(0, 128)], self.up)
        self.first[1].wait_recv()
        relay[1] = (near[1].astype(F32) + src[self.half(self.t_down, 1)].astype(F32)).astype(BF)
        down = copy(relay.at[1], from_up.at[pl.ds(128, 128)], self.down)
        self.summed = (up, down)

    def reduce_wait(self):
        for made in self.alone + self.summed:
            made.wait_recv()

    def gather_first(self, ref):
        mine = ref.at[self.whole(self.tensor)]
        self.base = self.links.count
        self.links.copy(mine, mine, self.up)
        self.links.copy(mine, mine, self.down)

    def landed(self, slot, which, device):
        arrival(None, slot, self.links.recv.at[self.base + which], device).wait_recv()

    def gather_second(self, ref):
        self.landed(ref.at[self.whole(self.t_down)], 0, self.down)
        self.base2 = self.links.count
        up = ref.at[self.half(self.t_down, 0)]
        self.links.copy(up, up, self.up)
        self.landed(ref.at[self.whole(self.t_up)], 1, self.up)
        down = ref.at[self.half(self.t_up, 1)]
        self.links.copy(down, down, self.down)

    def gather_wait(self, ref):
        offset = self.base2 - self.base
        self.landed(ref.at[self.half(self.t_far, 0)], offset, self.down)
        self.landed(ref.at[self.half(self.t_far, 1)], offset + 1, self.up)


class Spread:
    def __init__(self, mine, out, base, send, recv, core, chip, at):
        self.mine, self.out, self.base, self.send, self.recv, self.core, self.chip = mine, out, base, send, recv, core, chip
        x = lax.rem(chip, 4)
        right, left, far = (chip - x + lax.rem(x + k, 4) for k in (1, 3, 2))
        over = lax.rem(chip + 4, 8)
        o_right, o_left, o_far = (lax.rem(c + 4, 8) for c in (right, left, far))
        there = [at(shard_to=c * 2 + core) for c in (over, right, left)]
        sibling = at(shard_to=chip * 2 + (1 - core))
        to_over, to_right, to_left = there
        self.copies = [
            (None, None, to_over), (None, None, to_right), (None, None, to_left), (None, None, sibling),
            (over, None, to_right), (over, None, to_left),
            (left, 0, to_right), (right, 1, to_left), (o_left, 0, to_right), (o_right, 1, to_left),
        ]
        owners = [over, left, right, o_left, o_right, far, o_far]
        self.copies += [(owner, None, sibling) for owner in owners]
        self.arrivals = [
            (over, None, core), (left, None, core), (right, None, core), (chip, None, 1 - core), (o_left, None, core), (o_right, None, core),
            (far, 0, core), (far, 1, core), (o_far, 0, core), (o_far, 1, core),
        ]
        self.arrivals += [(owner, None, 1 - core) for owner in owners]

    def slot(self, owner, core, half):
        start = (owner * 2 + core) * 64
        if half is None:
            return self.out.at[pl.ds(pl.multiple_of(start, 64), 64)]
        return self.out.at[pl.ds(pl.multiple_of(start + half * 32, 32), 32)]

    def copy(self, i):
        owner, half, device = self.copies[i]
        dst = self.slot(self.chip if owner is None else owner, self.core, half)
        src = self.mine if owner is None else dst
        return pltpu.make_async_remote_copy(
            src_ref=src, dst_ref=dst, send_sem=self.send.at[self.base + i], recv_sem=self.recv.at[self.base + i],
            device_id=device, device_id_type=MESH,
        )

    def wait(self, i):
        owner, half, core = self.arrivals[i]
        arrival(None, self.slot(owner, core, half), self.recv.at[self.base + i], self.copies[i][2]).wait_recv()

    def begin(self):
        for i in (0, 1, 2, 3):
            self.copy(i).start()
        self.out[pl.ds(pl.multiple_of((self.chip * 2 + self.core) * 64, 64), 64)] = self.mine[...]

    def event(self, n):
        waits, starts = (
            ((1,), (6, 11)), ((2,), (7, 12)), ((0,), (4, 5, 10)), ((6, 7), (15,)),
            ((4,), (8, 13)), ((5,), (9, 14)), ((8, 9), (16,)),
        )[n]
        for i in waits:
            self.wait(i)
        for i in starts:
            self.copy(i).start()

    def collect(self):
        for i in (3,) + tuple(range(10, 17)):
            self.wait(i)

    def sent(self):
        for i in range(17):
            self.copy(i).wait_send()


def main_kernel(
    wz, wx, wbc, wdt, norm, wo, tok, cot, seg, cwx, cwb, cbx, cbb, dtb, alog, dsk, gg, ex, ext,
    in_o, zo_o, xn_o, gain_o, dz_o, gate_o, dx_o, dbc_o, ddt_o, small_o, out_o, oz, oo,
    mine1, mine2, etok_b, eseg, xs, st, st_low, st_in, y_s, er_s, c_s, z_s, dn_s, row_s, row_r, yn_o,
    xbc_o, pre_o, dtr_o, colm_o, st_o, dy_o, branch_o, carry_o, gz_o, go_o,
    acts, grad, heads, g_in, tail_r, ret_s, ret_r, near, relay, from_d, from_u,
    sz, so, chunk, rg, cs, cr, send, recv,
):
    shard, context, tensor, core, chip, chips, sibling, others, partner, ranks, group, at = places()
    mine1[:, 0:512] = wx[...]
    mine1[:, 512:768] = wbc[...]
    mine1[:, 768:896] = jnp.zeros((64, 128), BF)
    mine1[:, 768:776] = wdt[...]
    mine1[:, 776:777] = jnp.broadcast_to(norm[...].astype(F32), (8, 64)).T[:, 0:1].astype(BF)
    mine2[:, 0:512] = wz[...]
    mine2[:, 512:1024] = wo[...]
    greet([sibling, partner] + others[1:] + group[1:])
    links = Links(send, recv)

    links.count = 34
    seg_in = links.copy(seg, eseg, partner)
    tokens_in = links.copy(tok.at[pl.ds(1024 - EDGE, EDGE)], etok_b, partner)
    spread1 = Spread(mine1, in_o, 0, send, recv, core, chip, at)
    spread2 = Spread(mine2, zo_o, 17, send, recv, core, chip, at)
    spread1.begin()
    seg_in.wait_recv()
    seg_t = seg[...].astype(F32).T
    edge_t = jnp.where(context > 0, eseg[...].astype(F32).T, 0.0)
    edge_col = edge_t[120:128, 7:8]
    start = jnp.where(edge_col[7:8] == seg_t[0:1, 0:1], seg_t[0:1, 0:1], -1.0)
    colm_o[1024:1032] = jnp.zeros((8, 8), F32)
    for b in range(8):
        col = seg_t[:, b : b + 1]
        before = edge_col if b == 0 else seg_t[120:128, b - 1 : b]
        longer = jnp.concatenate([before, col], axis=0)
        entering = start if b == 0 else before[7:8]
        marks = [col]
        for d in range(1, 4):
            marks.append(jnp.where(longer[8 - d : 136 - d] == col, 1.0, 0.0))
        for value in (start, entering, col[127:128]):
            marks.append(jnp.where(col == value, 1.0, 0.0))
        marks.append(jnp.zeros_like(col))
        colm_o[b * Q : b * Q + Q] = jnp.concatenate(marks, axis=1)

    for n in range(7):
        spread1.event(n)
    spread2.begin()
    spread1.collect()
    tokens_in.wait_recv()

    a_neg = -jnp.exp(alog[...])
    causal, _ = triangles()
    lower = as_low(causal)
    gain_row = in_o[:, 768:896].astype(F32).T[8:9]
    gain_o[...] = gain_row

    def normed(block):
        plain = block.astype(F32)
        root = lax.rsqrt(jnp.mean(plain * plain, axis=1, keepdims=True) + EPSILON)
        return (plain * root * gain_row).astype(BF)

    edge_tokens = jnp.where(context > 0, etok_b[...].astype(F32), 0.0)
    edge = mm(normed(edge_tokens), in_o[:, 0:768]).astype(BF)
    xbc_o[0:EDGE] = edge
    xs[0:EDGE] = edge.astype(F32)
    st[...] = jnp.zeros_like(st)
    expand = ex[...]
    dsk_e = mm2(dsk[...], expand)

    def body(b, run):
        r = pl.ds(pl.multiple_of(b * Q, Q), Q)
        rn = pl.ds(pl.multiple_of(b * Q + EDGE, EDGE), Q)
        xn = normed(tok[r])
        xn_o[r] = xn
        both = mm(xn, in_o[...])
        xb = both[:, 0:768].astype(BF)
        xbc_o[rn] = xb
        xs[rn] = xb.astype(F32)
        raw = both[:, 768:776]
        dtr_o[r] = raw
        marks = colm_o[r]
        acts = []
        for c in range(6):
            lanes = slice(c * 128, c * 128 + 128)
            cw, cb, at = (cwx, cbx, lanes) if c < 4 else (cwb, cbb, slice(c * 128 - 512, c * 128 - 384))
            slab = xs[pl.ds(pl.multiple_of(b * Q, Q), Q + EDGE), lanes]
            pre = cb[:, at] + cw[3:4, at] * slab[EDGE:]
            for d in range(1, 4):
                pre = pre + (cw[3 - d : 4 - d, at] * slab[EDGE - d : Q + EDGE - d]) * marks[:, d : d + 1]
            pre_o[r, lanes] = pre
            acts.append(pre * sigmoid(pre))
        b_low = acts[4].astype(BF)
        c_low = acts[5].astype(BF)
        c_s[r] = c_low
        dt = softplus(raw + dtb[...])
        cum = mm3_left(lower, dt * a_neg)
        er_s[r] = jnp.exp(run + cum) * marks[:, 4:5]
        cum_t = cum.T
        last = cum[Q - 1 : Q]
        enter = jnp.exp(cum) * marks[:, 5:6]
        tail = jnp.exp(last - cum) * marks[:, 6:7]
        dt_e = mm2(dt, expand)
        enter_e = mm2(enter, expand)
        tail_e = mm2(tail, expand)
        mask = causal & (marks[:, 0:1] == seg[pl.ds(b, 1), :].astype(F32))
        scores = jnp.where(mask, mm_nt(c_low, b_low), 0.0)
        state = st[...]
        inter = mm(c_low, state.astype(BF))
        pieces = []
        for p in range(4):
            lanes = slice(p * 128, p * 128 + 128)
            xdt = acts[p] * dt_e[:, lanes]
            pieces.append((xdt * tail_e[:, lanes]).astype(BF))
            ws = []
            for h in (2 * p, 2 * p + 1):
                decay = jnp.exp(jnp.minimum(cum[:, h : h + 1] - cum_t[h : h + 1, :], 0.0))
                ws.append((decay * scores).astype(BF))
            intra = mm(jnp.concatenate(ws, axis=1), halves(xdt.astype(BF)))
            y_s[r, lanes] = intra + enter_e[:, lanes] * inter[:, lanes] + dsk_e[:, lanes] * acts[p]
        fresh = mm_tn(b_low, jnp.concatenate(pieces, axis=1))
        st[...] = enter_e[Q - 1 : Q] * state + fresh

        for n in range(7):
            pl.when(b == n)(partial(spread2.event, n))

        return run + last

    lax.fori_loop(0, 8, body, jnp.zeros((1, 8), F32))
    st_low[...] = st[...].astype(BF)
    state_in = links.copy(st_low, st_in, partner)
    spread2.collect()

    def project(b, carry):
        r = pl.ds(pl.multiple_of(b * Q, Q), Q)
        z_s[r] = mm(xn_o[r], zo_o[:, 0:512])
        dn_s[r] = mm(cot[r], zo_o[:, 512:1024])
        return carry

    lax.fori_loop(0, 8, project, 0)
    state_in.wait_recv()
    st_o[...] = jnp.where(context > 0, st_in[...].astype(F32), 0.0)

    def sums(b, carry):
        r = pl.ds(pl.multiple_of(b * Q, Q), Q)
        y = y_s[r] + mm2(er_s[r], expand) * mm(c_s[r], st_o[...].astype(BF))
        y_s[r] = y
        z = z_s[r]
        gated = y * (z * sigmoid(z))
        first_sum = jnp.sum(gated * gated, axis=1, keepdims=True)
        second_sum = jnp.sum(dn_s[r] * gg[...] * gated, axis=1, keepdims=True)
        row_s[b] = jnp.concatenate([first_sum, second_sum, jnp.zeros((Q, 6), F32)], axis=1).T
        return carry

    lax.fori_loop(0, 8, sums, 0)
    rows_in = [links.copy(row_s, row_r.at[k - 1], group[k]) for k in range(1, 4)]
    for copy in rows_in:
        copy.wait_recv()
    gate_o[...] = jnp.zeros_like(gate_o)
    st[...] = jnp.zeros_like(st)

    def finish(b, carry):
        r = pl.ds(pl.multiple_of(b * Q, Q), Q)
        total = (row_s[b] + row_r[0, b] + row_r[1, b] + row_r[2, b]).T
        root = lax.rsqrt(total[:, 0:1] * (1.0 / INNER) + EPSILON)
        cross = (root * root * root) * (total[:, 1:2] * (1.0 / INNER))
        er_e = mm2(er_s[r], expand)
        normals, carries = [], []
        for p in range(4):
            lanes = slice(p * 128, p * 128 + 128)
            y = y_s[r, lanes]
            z = z_s[r, lanes]
            dn = dn_s[r, lanes]
            sig = sigmoid(z)
            gate = z * sig
            gated = y * gate
            scaled = gated * root
            normals.append((scaled * gg[:, lanes]).astype(BF))
            gate_o[p : p + 1] += jnp.sum(dn * scaled, axis=0, keepdims=True)
            d_gated = root * (dn * gg[:, lanes]) - gated * cross
            d_y = d_gated * gate
            dy_o[r, lanes] = d_y
            dz_o[r, lanes] = (d_gated * y * (sig * (1.0 + z * (1.0 - sig)))).astype(BF)
            carries.append((d_y * er_e[:, lanes]).astype(BF))
        low = jnp.concatenate(normals, axis=1)
        yn_o[r] = low
        branch_o[r] = mm_nt(low, zo_o[:, 512:1024]).astype(BF)
        st[...] += mm_tn(c_s[r], jnp.concatenate(carries, axis=1))
        return carry

    lax.fori_loop(0, 8, finish, 0)
    carry_o[...] = st[...].astype(BF)
    carry_in = links.copy(carry_o, g_in, partner)
    ring = Ring(links, tensor, group)
    ring.reduce_first(branch_o, near, from_d, from_u)
    for m in range(8):
        lanes = slice(m * 128, m * 128 + 128)
        gz_o[m] = mm_tn(xn_o[:, lanes], dz_o[...]).astype(BF).reshape(2, 64, 512)
        go_o[m] = mm_tn(cot[:, lanes], yn_o[...]).astype(BF).reshape(2, 64, 512)
    sib_in = (links.copy(gz_o.at[:, 1 - core], sz, sibling), links.copy(go_o.at[:, 1 - core], so, sibling))
    a_neg = -jnp.exp(alog[...])
    causal, anti = triangles()
    lower = as_low(causal)
    upper = as_low(anti)
    expand = ex[...]
    expand_t = ext[...]
    dsk_e = mm2(dsk[...], expand)

    def head_sum(v):
        return mm2(v, expand_t)

    y_s[0:Q] = st_o[...]

    def forward(b, carry):
        r = pl.ds(pl.multiple_of(b * Q, Q), Q)
        marks = colm_o[r]
        dt = softplus(dtr_o[r] + dtb[...])
        cum = mm3_left(lower, dt * a_neg)
        last = cum[Q - 1 : Q]
        tail = jnp.exp(last - cum) * marks[:, 6:7] * dt
        keep_e = mm2(jnp.exp(last) * marks[Q - 1 : Q, 5:6], expand)
        tail_e = mm2(tail, expand)
        pieces = []
        for c in range(6):
            lanes = slice(c * 128, c * 128 + 128)
            pre = pre_o[r, lanes]
            act = pre * sigmoid(pre)
            acts[r, lanes] = act
            if c < 4:
                pieces.append((act * tail_e[:, lanes]).astype(BF))
            if c == 4:
                b_low = act.astype(BF)
        fresh = mm_tn(b_low, jnp.concatenate(pieces, axis=1))
        y_s[pl.ds(pl.multiple_of(b * Q + Q, Q), Q)] = keep_e * y_s[r] + fresh
        return carry

    lax.fori_loop(0, 7, forward, 0)
    r7 = slice(7 * Q, 8 * Q)
    for c in range(6):
        lanes = slice(c * 128, c * 128 + 128)
        pre = pre_o[r7, lanes]
        acts[r7, lanes] = pre * sigmoid(pre)
    for copy in sib_in:
        copy.wait_recv()

    def merge(c, carry):
        for mine, theirs, at in ((gz_o, sz, 0), (go_o, so, 512)):
            chunk[c, :, at : at + 512] = (mine[c, core].astype(F32) + theirs[c].astype(F32)).astype(BF)
        return carry

    lax.fori_loop(0, 8, merge, 0)
    grads_in = [links.copy(chunk.at[chips[k]], rg.at[k - 1], others[k]) for k in range(1, 8)]
    carry_in.wait_recv()
    grad[...] = jnp.where(context == 0, g_in[...].astype(F32), 0.0)
    heads[...] = jnp.zeros_like(heads)
    xs[0:8] = jnp.zeros((8, 768), F32)
    xs[1032:1040] = jnp.zeros((8, 768), F32)

    def backward(i, carry):
        b = 7 - i
        r = pl.ds(pl.multiple_of(b * Q, Q), Q)
        rp = pl.ds(pl.multiple_of(b * Q + 8, 8), Q)
        marks = colm_o[r]
        raw = dtr_o[r] + dtb[...]
        dt = softplus(raw)
        cum = mm3_left(lower, dt * a_neg)
        cum_t = cum.T
        last = cum[Q - 1 : Q]
        enter = jnp.exp(cum) * marks[:, 5:6]
        tail = jnp.exp(last - cum) * marks[:, 6:7]
        dt_e = mm2(dt, expand)
        enter_e = mm2(enter, expand)
        tail_e = mm2(tail, expand)
        keep_e = enter_e[Q - 1 : Q]
        b_low = acts[r, 512:640].astype(BF)
        c_low = acts[r, 640:768].astype(BF)
        state = y_s[r]
        state_low = state.astype(BF)
        g_now = grad[...]
        g_low = g_now.astype(BF)
        inter = mm(c_low, state_low)
        back = mm(b_low, g_low)
        mask = causal & (marks[:, 0:1] == seg[pl.ds(b, 1), :].astype(F32))
        scores = jnp.where(mask, mm_nt(c_low, b_low), 0.0)
        kept = jnp.sum(state * g_now, axis=0, keepdims=True) * keep_e
        entered, tailed, e_terms, q_terms, x_terms, k_terms = [], [], [], [], [], []
        rows, cols = [], []
        d_scores = jnp.zeros((Q, Q), F32)
        for p in range(4):
            lanes = slice(p * 128, p * 128 + 128)
            x = acts[r, lanes]
            dys = dy_o[r, lanes]
            xdt = x * dt_e[:, lanes]
            xdt_low = xdt.astype(BF)
            ed = enter_e[:, lanes] * dys
            tx = tail_e[:, lanes] * xdt
            entered.append(ed.astype(BF))
            tailed.append(tx.astype(BF))
            dy_two = halves(dys.astype(BF))
            dw_two = mm_nt(dy_two, xdt_low)
            ws = []
            for k in range(2):
                h = 2 * p + k
                decay = jnp.exp(jnp.minimum(cum[:, h : h + 1] - cum_t[h : h + 1, :], 0.0))
                weight = decay * scores
                dw = dw_two[k * Q : k * Q + Q]
                d_scores = d_scores + decay * dw
                both = weight * dw
                rows.append(jnp.sum(both, axis=1, keepdims=True))
                cols.append(jnp.sum(both, axis=0, keepdims=True))
                ws.append(weight.astype(BF))
            dxdt = mm_tn(jnp.concatenate(ws, axis=0), dy_two) + tail_e[:, lanes] * back[:, lanes]
            e_terms.append(ed * inter[:, lanes] - tx * back[:, lanes])
            q_terms.append(jnp.sum(tx * back[:, lanes], axis=0, keepdims=True) + kept[:, lanes])
            x_terms.append(dxdt * x)
            k_terms.append(jnp.sum(dys * x, axis=0, keepdims=True))
            pre = pre_o[r, lanes]
            sig = sigmoid(pre)
            xs[rp, lanes] = (dxdt * dt_e[:, lanes] + dsk_e[:, lanes] * dys) * (sig * (1.0 + pre * (1.0 - sig)))
        entered = jnp.concatenate(entered, axis=1)
        tailed = jnp.concatenate(tailed, axis=1)
        ds_low = jnp.where(mask, d_scores, 0.0).astype(BF)
        d_c = mm_nt(entered, state_low) + mm(ds_low, b_low)
        d_b = mm_nt(tailed, g_low) + mm_tn(ds_low, c_low)
        grad[...] = keep_e * g_now + mm_tn(c_low, entered)
        for c, value in ((4, d_b), (5, d_c)):
            lanes = slice(c * 128, c * 128 + 128)
            pre = pre_o[r, lanes]
            sig = sigmoid(pre)
            xs[rp, lanes] = value * (sig * (1.0 + pre * (1.0 - sig)))
        d_cum = jnp.concatenate(rows, axis=1) - jnp.concatenate(cols, axis=0).T
        d_cum = d_cum + head_sum(jnp.concatenate(e_terms, axis=1))
        d_log = mm3_left(upper, d_cum) + head_sum(jnp.concatenate(q_terms, axis=1))
        d_dt = d_log * a_neg + head_sum(jnp.concatenate(x_terms, axis=1))
        d_raw = d_dt * sigmoid(raw)
        ddt_o[r] = jnp.concatenate([d_raw, jnp.zeros((Q, 120), F32)], axis=1).astype(BF)
        heads[0:1] += jnp.sum(d_raw, axis=0, keepdims=True)
        heads[1:2] += jnp.sum(d_log * dt, axis=0, keepdims=True) * a_neg
        heads[2:3] += head_sum(jnp.concatenate(k_terms, axis=1))
        return carry

    lax.fori_loop(0, 1, backward, 0)
    ring.reduce_second(branch_o, near, relay, from_d, from_u)
    lax.fori_loop(1, 4, backward, 0)
    ring.reduce_wait()

    def finish_out(i, carry):
        r = pl.ds(pl.multiple_of(i * 64, 64), 64)
        rt = pl.ds(pl.multiple_of(tensor * 256 + i * 64, 64), 64)
        total = branch_o[rt].astype(F32) + from_d[r].astype(F32) + from_u[r].astype(F32)
        out_o[rt] = (tok[rt].astype(F32) + total).astype(BF)
        return carry

    lax.fori_loop(0, 4, finish_out, 0)
    ring.gather_first(out_o)
    lax.fori_loop(4, 8, backward, 0)
    small_o[...] = jnp.zeros_like(small_o)
    small_o[24:32, 0:8] = heads[...]

    for c in range(6):
        lanes = slice(c * 128, c * 128 + 128)
        first = xs[0:16, lanes]
        cw, wl = (cwx, lanes) if c < 4 else (cwb, slice(c * 128 - 512, c * 128 - 384))
        flags = jnp.concatenate([jnp.zeros((8, 8), F32), colm_o[0:8]], axis=0)
        total = jnp.zeros((8, 128), F32)
        for d in range(1, 4):
            total = total + cw[3 - d : 4 - d, wl] * (first * flags[:, d : d + 1])[d : d + 8]
        ret_s[:, lanes] = total
    ret_in = links.copy(ret_s, ret_r, partner)
    ring.gather_second(out_o)
    for copy in grads_in:
        copy.wait_recv()
    for at in range(0, 1024, 128):
        lanes = slice(at, at + 128)
        cs[:, lanes] = add_slots(chunk[chip, :, lanes].astype(F32), rg, lanes).astype(BF)
    grads_ctx = links.copy(cs, cr, partner)
    for c in range(6):
        lanes = slice(c * 128, c * 128 + 128)
        cw, wl = (cwx, lanes) if c < 4 else (cwb, slice(c * 128 - 512, c * 128 - 384))

        def conv(b, sums, lanes=lanes, c=c, cw=cw, wl=wl):
            r = pl.ds(pl.multiple_of(b * Q, Q), Q)
            slab = xs[pl.ds(pl.multiple_of(b * Q + 8, 8), Q + 8), lanes]
            marks = colm_o[pl.ds(pl.multiple_of(b * Q, Q), Q + 8)]
            xin = xbc_o[pl.ds(pl.multiple_of(b * Q, Q), Q + EDGE), lanes].astype(F32)
            main = slab[0:Q]
            out = cw[3:4, wl] * main
            new = [sums[0] + jnp.sum(main, axis=0, keepdims=True),
                   sums[1] + jnp.sum(main * xin[EDGE:], axis=0, keepdims=True)]
            for d in range(1, 4):
                masked = slab * marks[:, d : d + 1]
                out = out + cw[3 - d : 4 - d, wl] * masked[d : d + Q]
                new.append(sums[d + 1] + jnp.sum(masked[0:Q] * xin[EDGE - d : Q + EDGE - d], axis=0, keepdims=True))
            if c < 4:
                dx_o[r, lanes] = out.astype(BF)
            else:
                dbc_o[r, slice(c * 128 - 512, c * 128 - 384)] = out.astype(BF)

            @pl.when(b == 7)
            def _():
                tail_r[:, lanes] = out[Q - EDGE :]

            return tuple(new)

        zero = jnp.zeros((1, 128), F32)
        sums = lax.fori_loop(0, 8, conv, (zero,) * 5)
        at = 16 + c if c < 4 else 36 + c
        small_o[at : at + 1] = sums[0]
        for d in range(4):
            at = (3 - d) * 4 + c if c < 4 else 28 + (3 - d) * 2 + c
            small_o[at : at + 1] = sums[d + 1]
    ret_in.wait_recv()
    returned = jnp.where(context == 0, ret_r[...], 0.0)
    last = tail_r[...] + jnp.concatenate([jnp.zeros((EDGE - 8, 768), F32), returned], axis=0)
    dx_o[1024 - EDGE : 1024] = last[:, 0:512].astype(BF)
    dbc_o[1024 - EDGE : 1024] = last[:, 512:768].astype(BF)
    grads_ctx.wait_recv()
    oz[...] = cs[:, 0:512].astype(F32) + cr[:, 0:512].astype(F32)
    oo[...] = cs[:, 512:1024].astype(F32) + cr[:, 512:1024].astype(F32)
    ring.gather_wait(out_o)
    links.finish()
    spread1.sent()
    spread2.sent()


def add_slots(total, slots, lanes):
    for k in range(7):
        total = total + slots[k, :, lanes].astype(F32)
    return total


def tail_kernel(
    dz, dx, ddt, dbc, small, gate, gain, w_in, w_zo, xn, tok, cot,
    dtok_o, ox, odt, obc, onorm, conv_o, convb_o, bc_o, bcb_o, gate_o, dtb_o, alog_o, dsk_o,
    part, gx, near, relay, from_d, from_u, sx, chunk, rg, cs, cr, t2,
    sm, sm_s, sm_c, sm_x, sm_r, sm_t, nm, nm_s, nm_c, nm_x, nm_r, nm_t, tok_r, cot_r, send, recv, local_sem,
):
    shard, context, tensor, core, chip, chips, sibling, others, partner, ranks, group, at = places()
    own = pl.ds(pl.multiple_of(tensor * 256, 256), 256)
    fetch = [
        pltpu.make_async_copy(tok.at[own], tok_r, local_sem.at[0]),
        pltpu.make_async_copy(cot.at[own], cot_r, local_sem.at[1]),
    ]
    for copy in fetch:
        copy.start()
    greet([sibling, partner] + others[1:] + group[1:])
    links = Links(send, recv)
    sm[...] = small[...]
    sm[20:24] = gate[...]
    wide = Ring(links, tensor, group)

    def make(r):
        total = mm_nt(dz[r], w_zo[:, 0:512]) + mm_nt(dx[r], w_in[:, 0:512]) + mm_nt(ddt[r], w_in[:, 768:896]) + mm_nt(dbc[r], w_in[:, 512:768])
        part[r] = total.astype(BF)

    wide.reduce_first(part, near, from_d, from_u, make)
    small_in = links.copy(sm, sm_s, sibling)

    def outer(m):
        block = xn[:, m * 128 : m * 128 + 128]
        gx[m, :, :, 0:512] = mm_tn(block, dx[...]).astype(BF).reshape(2, 64, 512)
        gx[m, :, :, 512:640] = mm_tn(block, ddt[...]).astype(BF).reshape(2, 64, 128)
        gx[m, :, :, 640:896] = mm_tn(block, dbc[...]).astype(BF).reshape(2, 64, 256)

    make(wide.half(wide.t_up, 0))
    make(wide.half(wide.t_down, 1))
    for m in range(4):
        outer(m)
    wide.reduce_second(part, near, relay, from_d, from_u)
    for m in range(4, 8):
        outer(m)
    sib_in = links.copy(gx.at[:, 1 - core], sx, sibling)
    small_in.wait_recv()
    sm_c[chip] = sm[...] + sm_s[...]
    small_base = links.count - 1
    for k in range(1, 8):
        links.copy(sm_c.at[chip], sm_c.at[chip], others[k])
    make(wide.half(tensor, 0))
    make(wide.half(tensor, 1))
    sib_in.wait_recv()

    def merge(c, carry):
        chunk[c] = (gx[c, core].astype(F32) + sx[c].astype(F32)).astype(BF)
        return carry

    lax.fori_loop(0, 8, merge, 0)
    grads_in = [links.copy(chunk.at[chips[k]], rg.at[k - 1], others[k]) for k in range(1, 8)]

    for copy in fetch:
        copy.wait()
    wide.reduce_wait()

    def inner(i, g_norm):
        r = pl.ds(pl.multiple_of(i * 64, 64), 64)
        rt = pl.ds(pl.multiple_of(tensor * 256 + i * 64, 64), 64)
        total = part[rt].astype(F32) + from_d[r].astype(F32) + from_u[r].astype(F32)
        plain = tok_r[r].astype(F32)
        root = lax.rsqrt(jnp.mean(plain * plain, axis=1, keepdims=True) + EPSILON)
        stat = plain * root
        d_plain = total * gain[...]
        mean = jnp.mean(d_plain * plain, axis=1, keepdims=True)
        dtok_o[rt] = (cot_r[r].astype(F32) + root * d_plain - stat * (root * root) * mean).astype(BF)
        return g_norm + jnp.sum(total * stat, axis=0, keepdims=True)

    g_norm = lax.fori_loop(0, 4, inner, jnp.zeros((1, 1024), F32))
    wide.gather_first(dtok_o)
    for c in range(8):
        nm[c : c + 1] = g_norm[:, c * 128 : c * 128 + 128]
    norm_sib = links.copy(nm, nm_s, sibling)

    for k in range(1, 8):
        source = lax.rem(chip + 8 - k, 8)
        arrival(None, sm_c.at[source], recv.at[small_base + k], others[k]).wait_recv()
    total = sm_c[0]
    for c in range(1, 8):
        total = total + sm_c[c]
    sm_x[...] = total
    small_ctx = links.copy(sm_x, sm_r, partner)
    norm_sib.wait_recv()
    nm_c[chip] = nm[...] + nm_s[...]
    norm_base = links.count - 1
    for k in range(1, 8):
        links.copy(nm_c.at[chip], nm_c.at[chip], others[k])
    for copy in grads_in:
        copy.wait_recv()
    for col in range(0, 896, 128):
        lanes = slice(col, col + 128)
        cs[:, lanes] = add_slots(chunk[chip, :, lanes].astype(F32), rg, lanes).astype(BF)
    grads_ctx = links.copy(cs, cr, partner)
    wide.gather_second(dtok_o)
    for k in range(1, 8):
        source = lax.rem(chip + 8 - k, 8)
        arrival(None, nm_c.at[source], recv.at[norm_base + k], others[k]).wait_recv()
    total = nm_c[0]
    for c in range(1, 8):
        total = total + nm_c[c]
    nm_x[...] = total
    norm_ctx = links.copy(nm_x, nm_r, partner)
    small_ctx.wait_recv()
    sums = sm_x[...] + sm_r[...]
    for k in range(4):
        for p in range(4):
            conv_o[k : k + 1, p * 128 : p * 128 + 128] = sums[k * 4 + p : k * 4 + p + 1]
    for p in range(4):
        convb_o[:, p * 128 : p * 128 + 128] = sums[16 + p : 17 + p]
        gate_o[:, p * 128 : p * 128 + 128] = sums[20 + p : 21 + p]
    dtb_o[...] = sums[24:25, 0:8]
    alog_o[...] = sums[25:26, 0:8]
    dsk_o[...] = sums[26:27, 0:8]
    sm_t[tensor] = sums[32:48]
    small_t = links.count
    for k in range(1, 4):
        links.copy(sm_t.at[tensor], sm_t.at[tensor], group[k])
    norm_ctx.wait_recv()
    nm_t[tensor] = nm_x[...] + nm_r[...]
    norm_t = links.count
    for k in range(1, 4):
        links.copy(nm_t.at[tensor], nm_t.at[tensor], group[k])
    grads_ctx.wait_recv()
    ox[...] = cs[:, 0:512].astype(F32) + cr[:, 0:512].astype(F32)
    t2[tensor] = cs[:, 640:896].astype(F32) + cr[:, 640:896].astype(F32)
    grads2_t = links.count
    for k in range(1, 4):
        links.copy(t2.at[tensor], t2.at[tensor], group[k])
    odt[...] = (cs[:, 512:640].astype(F32) + cr[:, 512:640].astype(F32))[:, 0:8]
    for k in range(1, 4):
        source = lax.rem(tensor + 4 - k, 4)
        arrival(None, sm_t.at[source], recv.at[small_t + k - 1], group[k]).wait_recv()
        arrival(None, nm_t.at[source], recv.at[norm_t + k - 1], group[k]).wait_recv()
        arrival(None, t2.at[source], recv.at[grads2_t + k - 1], group[k]).wait_recv()
    sums = (sm_t[0] + sm_t[1]) + (sm_t[2] + sm_t[3])
    for k in range(4):
        for p in range(2):
            bc_o[k : k + 1, p * 128 : p * 128 + 128] = sums[k * 2 + p : k * 2 + p + 1]
    for p in range(2):
        bcb_o[:, p * 128 : p * 128 + 128] = sums[8 + p : 9 + p]
    obc[...] = (t2[0] + t2[1]) + (t2[2] + t2[3])
    nm_s[...] = (nm_t[0] + nm_t[1]) + (nm_t[2] + nm_t[3])
    row = nm_s[pl.ds(chip, 1), :]
    onorm[...] = jnp.where(core == 0, row[:, 0:64], row[:, 64:128])
    wide.gather_wait(dtok_o)
    links.finish()


def call(kernel, out_shapes, scratch, *args, specs=None, collective_id=None):
    return pl.pallas_call(
        kernel,
        out_shape=[jax.ShapeDtypeStruct(s, d) for s, d in out_shapes],
        in_specs=[pl.BlockSpec(memory_space=pl.ANY if n in (specs or ()) else pltpu.VMEM) for n in range(len(args))],
        out_specs=[pl.BlockSpec(memory_space=pltpu.VMEM)] * len(out_shapes),
        scratch_shapes=[pltpu.SemaphoreType.DMA(s) if d is None else pltpu.VMEM(s, d) for s, d in scratch],
        compiler_params=pltpu.CompilerParams(vmem_limit_bytes=VMEM_LIMIT, collective_id=collective_id, has_side_effects=collective_id is not None
        ),
    )(*args)


def local(
    tokens,
    segment,
    norm_gain,
    w_z,
    w_x,
    w_dt,
    w_bc,
    conv_x,
    conv_xb,
    conv_bc,
    conv_bcb,
    dt_bias,
    a_log,
    d_skip,
    gate_gain,
    w_out,
    cotangent,
):
    length = tokens.shape[0]
    head_count = dt_bias.shape[0]
    inner_width = head_count * HEADDIM
    bc_width = 2 * STATE
    seg = segment.reshape(8, 128)
    expand_np = np.kron(np.eye(8), np.ones((1, HEADDIM)))
    expand = jnp.asarray(expand_np, BF)
    expand_t = jnp.asarray(expand_np.T, BF)
    wide = (length, inner_width)
    state = (STATE, inner_width)
    grid = (8, 2, 64, 512)
    heads = (dt_bias[None], a_log[None], d_skip[None])
    own = (64, 512)
    half = ((2, 128, 1024), BF)
    rows = ((256, 1024), BF)

    def vector(shape, last):
        return [(s, F32) for s in (shape, shape, (8,) + shape, shape, shape, last)]

    (w_in, w_zo, x_normed, gain_row, d_z, g_gate_gain, d_x_low, d_bc, d_dt_low, small, output, o_z, o_out) = call(
        main_kernel,
        [((1024, 896), BF), ((1024, 1024), BF), ((length, 1024), BF), ((1, 1024), F32), (wide, BF), ((4, 128), F32),
         (wide, BF), ((length, 2 * STATE), BF), ((length, 128), BF), ((48, 128), F32), ((length, 1024), BF), (own, F32), (own, F32)],
        [((64, 896), BF), ((64, 1024), BF), ((EDGE, 1024), BF), ((8, 128), jnp.int32), ((length + EDGE, 768), F32), (state, F32), (state, BF), (state, BF),
         (wide, F32), ((length, 8), F32), ((length, STATE), BF), (wide, F32), (wide, F32), ((8, 8, 128), F32), ((3, 8, 8, 128), F32), (wide, BF),
         ((length + EDGE, 768), BF), ((length, 768), F32), ((length, 8), F32), ((length + 8, 8), F32), (state, F32), (wide, F32),
         ((length, 1024), BF), (state, BF), (grid, BF), (grid, BF),
         ((length, 768), F32), (state, F32), ((8, 8), F32),
         (state, BF), ((EDGE, 768), F32), ((8, 768), F32), ((8, 768), F32), half, half, rows, rows,
         ((8, 64, 512), BF), ((8, 64, 512), BF), ((8, 64, 1024), BF), ((7, 64, 1024), BF), ((64, 1024), BF), ((64, 1024), BF),
         ((72,), None), ((72,), None)],
        w_z, w_x, w_bc, w_dt, norm_gain[None], w_out, tokens, cotangent, seg,
        conv_x, conv_bc, conv_xb[None], conv_bcb[None], *heads, gate_gain[None], expand, expand_t,
        collective_id=1,
    )
    d_tokens, o_x, o_dt, o_bc, o_norm, conv_o, convb_o, cbc_o, cbcb_o, gate_o, dtb_o, alog_o, dsk_o = call(
        tail_kernel,
        [((length, 1024), BF), (own, F32), ((64, 8), F32), ((64, 256), F32), ((1, 64), F32),
         ((4, 512), F32), ((1, 512), F32), ((4, 256), F32), ((1, 256), F32), ((1, 512), F32), ((1, 8), F32), ((1, 8), F32), ((1, 8), F32)],
        [((length, 1024), BF), ((8, 2, 64, 896), BF), half, half, rows, rows,
         ((8, 64, 896), BF), ((8, 64, 896), BF), ((7, 64, 896), BF), ((64, 896), BF), ((64, 896), BF), ((4, 64, 256), F32),
         *vector((48, 128), (4, 16, 128)), *vector((8, 128), (4, 8, 128)),
         rows, rows, ((64,), None), ((64,), None), ((2,), None)],
        d_z, d_x_low, d_dt_low, d_bc, small, g_gate_gain, gain_row, w_in, w_zo, x_normed, tokens, cotangent,
        specs=(10, 11), collective_id=2,
    )
    return (
        output, d_tokens, o_norm[0], o_z, o_x, o_dt, o_bc, conv_o, convb_o[0], cbc_o, cbcb_o[0],
        dtb_o[0], alog_o[0], dsk_o[0], gate_o[0], o_out,
    )


def solution(mesh):
    in_specs = (
        P(("shard", "context"), None),
        P(("shard", "context")),
        P("shard"),
        P("shard", "tensor"),
        P("shard", "tensor"),
        P("shard", "tensor"),
        P("shard", None),
        P(None, "tensor"),
        P("tensor"),
        P(),
        P(),
        P("tensor"),
        P("tensor"),
        P("tensor"),
        P("tensor"),
        P("shard", "tensor"),
        P(("shard", "context"), None),
    )
    out_specs = (
        P(("shard", "context"), None),
        P(("shard", "context"), None),
        P("shard"),
        P("shard", "tensor"),
        P("shard", "tensor"),
        P("shard", "tensor"),
        P("shard", None),
        P(None, "tensor"),
        P("tensor"),
        P(),
        P(),
        P("tensor"),
        P("tensor"),
        P("tensor"),
        P("tensor"),
        P("shard", "tensor"),
    )
    return jax.shard_map(local, mesh=mesh, in_specs=in_specs, out_specs=out_specs, check_vma=False)
```

```python
from functools import partial

import jax
import jax.numpy as jnp
import numpy as np
from jax import lax
from jax.experimental import pallas as pl
from jax.experimental.pallas import tpu as pltpu
from jax.sharding import PartitionSpec as P

HEADDIM = 64
STATE = 128
CONV = 4
INNER = 2048


EPSILON = 1e-05


F32 = jnp.float32
BF = jnp.bfloat16
Q = 128
EDGE = 16
VMEM_LIMIT = 60 * 1024 * 1024


def mm(a, b):
    return lax.dot_general(a, b, (((1,), (0,)), ((), ())), preferred_element_type=F32)


def mm_nt(a, b):
    return lax.dot_general(a, b, (((1,), (1,)), ((), ())), preferred_element_type=F32)


def mm_tn(a, b):
    return lax.dot_general(a, b, (((0,), (0,)), ((), ())), preferred_element_type=F32)


def split2(v):
    hi = v.astype(BF)
    return hi, (v - hi.astype(F32)).astype(BF)


def mm2(a, b):
    hi, lo = split2(a)
    return mm(hi, b) + mm(lo, b)


def mm3_left(a, b):
    hi, lo = split2(b)
    lo2 = (b - hi.astype(F32) - lo.astype(F32)).astype(BF)
    return mm(a, hi) + (mm(a, lo) + mm(a, lo2))


def softplus(v):
    return jnp.maximum(v, 0.0) + jnp.log1p(jnp.exp(-jnp.abs(v)))


def sigmoid(v):
    return 1.0 / (1.0 + jnp.exp(-v))


def triangles():
    rows = lax.broadcasted_iota(jnp.int32, (Q, Q), 0)
    cols = lax.broadcasted_iota(jnp.int32, (Q, Q), 1)
    return rows >= cols, rows <= cols


def as_low(mask):
    return jnp.where(mask, 1.0, 0.0).astype(BF)


def halves(slab):
    lane = lax.broadcasted_iota(jnp.int32, slab.shape, 1)
    zero = jnp.zeros_like(slab)
    first = jnp.where(lane < HEADDIM, slab, zero)
    second = jnp.where(lane >= HEADDIM, slab, zero)
    return jnp.concatenate([first, second], axis=0)


MESH = pl.DeviceIdType.MESH


class Links:
    def __init__(self, send, recv):
        self.send, self.recv, self.count, self.started = send, recv, 0, []

    def copy(self, src, dst, device):
        made = pltpu.make_async_remote_copy(
            src_ref=src,
            dst_ref=dst,
            send_sem=self.send.at[self.count],
            recv_sem=self.recv.at[self.count],
            device_id=device,
            device_id_type=MESH,
        )
        self.count += 1
        self.started.append(made)
        made.start()
        return made

    def finish(self):
        for made in self.started:
            made.wait_send()


def arrival(like, dst, links_recv, device):
    return pltpu.make_async_remote_copy(
        src_ref=dst, dst_ref=dst, send_sem=links_recv, recv_sem=links_recv, device_id=device, device_id_type=MESH
    )


def greet(devices):
    barrier = pltpu.get_barrier_semaphore()
    for device in devices:
        pl.semaphore_signal(barrier, inc=1, device_id=device, device_id_type=MESH)
    pl.semaphore_wait(barrier, len(devices))


def places():
    shard, context, tensor = (lax.axis_index(name) for name in ("shard", "context", "tensor"))
    core, chip = lax.rem(shard, 2), lax.div(shard, 2)

    def at(shard_to=None, context_to=None, tensor_to=None):
        return (
            shard if shard_to is None else shard_to,
            context if context_to is None else context_to,
            tensor if tensor_to is None else tensor_to,
        )

    chips = [None] + [lax.rem(chip + k, 8) for k in range(1, 8)]
    sibling = at(shard_to=chip * 2 + (1 - core))
    others = [None] + [at(shard_to=c * 2 + core) for c in chips[1:]]
    partner = at(context_to=1 - context)
    ranks = [None] + [lax.rem(tensor + k, 4) for k in range(1, 4)]
    group = [None] + [at(tensor_to=t) for t in ranks[1:]]
    return shard, context, tensor, core, chip, chips, sibling, others, partner, ranks, group, at


class Ring:
    def __init__(self, links, tensor, group):
        self.links, self.tensor = links, tensor
        self.up, self.down = group[1], group[3]
        self.t_up, self.t_down, self.t_far = (lax.rem(tensor + k, 4) for k in (1, 3, 2))

    def half(self, rank, which):
        return pl.ds(pl.multiple_of(rank * 256 + which * 128, 128), 128)

    def whole(self, rank):
        return pl.ds(pl.multiple_of(rank * 256, 256), 256)

    def reduce_first(self, src, near, from_down, from_up, make=None):
        def send(rank, which, dst, device):
            rows = self.half(rank, which)
            if make is not None:
                make(rows)
            return self.links.copy(src.at[rows], dst, device)

        self.first = (send(self.t_far, 0, near.at[0], self.up), send(self.t_far, 1, near.at[1], self.down))
        self.alone = (
            send(self.t_up, 1, from_down.at[pl.ds(128, 128)], self.up),
            send(self.t_down, 0, from_up.at[pl.ds(0, 128)], self.down),
        )

    def reduce_second(self, src, near, relay, from_down, from_up):
        copy = self.links.copy
        self.first[0].wait_recv()
        relay[0] = (near[0].astype(F32) + src[self.half(self.t_up, 0)].astype(F32)).astype(BF)
        up = copy(relay.at[0], from_down.at[pl.ds(0, 128)], self.up)
        self.first[1].wait_recv()
        relay[1] = (near[1].astype(F32) + src[self.half(self.t_down, 1)].astype(F32)).astype(BF)
        down = copy(relay.at[1], from_up.at[pl.ds(128, 128)], self.down)
        self.summed = (up, down)

    def reduce_wait(self):
        for made in self.alone + self.summed:
            made.wait_recv()

    def gather_first(self, ref):
        mine = ref.at[self.whole(self.tensor)]
        self.base = self.links.count
        self.links.copy(mine, mine, self.up)
        self.links.copy(mine, mine, self.down)

    def landed(self, slot, which, device):
        arrival(None, slot, self.links.recv.at[self.base + which], device).wait_recv()

    def gather_second(self, ref):
        self.landed(ref.at[self.whole(self.t_down)], 0, self.down)
        self.base2 = self.links.count
        up = ref.at[self.half(self.t_down, 0)]
        self.links.copy(up, up, self.up)
        self.landed(ref.at[self.whole(self.t_up)], 1, self.up)
        down = ref.at[self.half(self.t_up, 1)]
        self.links.copy(down, down, self.down)

    def gather_wait(self, ref):
        offset = self.base2 - self.base
        self.landed(ref.at[self.half(self.t_far, 0)], offset, self.down)
        self.landed(ref.at[self.half(self.t_far, 1)], offset + 1, self.up)


class Spread:
    def __init__(self, mine, out, base, send, recv, core, chip, at):
        self.mine, self.out, self.base, self.send, self.recv, self.core, self.chip = mine, out, base, send, recv, core, chip
        x = lax.rem(chip, 4)
        right, left, far = (chip - x + lax.rem(x + k, 4) for k in (1, 3, 2))
        over = lax.rem(chip + 4, 8)
        o_right, o_left, o_far = (lax.rem(c + 4, 8) for c in (right, left, far))
        there = [at(shard_to=c * 2 + core) for c in (over, right, left)]
        sibling = at(shard_to=chip * 2 + (1 - core))
        to_over, to_right, to_left = there
        self.copies = [
            (None, None, to_over), (None, None, to_right), (None, None, to_left), (None, None, sibling),
            (over, None, to_right), (over, None, to_left),
            (left, 0, to_right), (right, 1, to_left), (o_left, 0, to_right), (o_right, 1, to_left),
        ]
        owners = [over, left, right, o_left, o_right, far, o_far]
        self.copies += [(owner, None, sibling) for owner in owners]
        self.arrivals = [
            (over, None, core), (left, None, core), (right, None, core), (chip, None, 1 - core), (o_left, None, core), (o_right, None, core),
            (far, 0, core), (far, 1, core), (o_far, 0, core), (o_far, 1, core),
        ]
        self.arrivals += [(owner, None, 1 - core) for owner in owners]

    def slot(self, owner, core, half):
        start = (owner * 2 + core) * 64
        if half is None:
            return self.out.at[pl.ds(pl.multiple_of(start, 64), 64)]
        return self.out.at[pl.ds(pl.multiple_of(start + half * 32, 32), 32)]

    def copy(self, i):
        owner, half, device = self.copies[i]
        dst = self.slot(self.chip if owner is None else owner, self.core, half)
        src = self.mine if owner is None else dst
        return pltpu.make_async_remote_copy(
            src_ref=src, dst_ref=dst, send_sem=self.send.at[self.base + i], recv_sem=self.recv.at[self.base + i],
            device_id=device, device_id_type=MESH,
        )

    def wait(self, i):
        owner, half, core = self.arrivals[i]
        arrival(None, self.slot(owner, core, half), self.recv.at[self.base + i], self.copies[i][2]).wait_recv()

    def begin(self):
        for i in (0, 1, 2, 3):
            self.copy(i).start()
        self.out[pl.ds(pl.multiple_of((self.chip * 2 + self.core) * 64, 64), 64)] = self.mine[...]

    def event(self, n):
        waits, starts = (
            ((1,), (6, 11)), ((2,), (7, 12)), ((0,), (4, 5, 10)), ((6, 7), (15,)),
            ((4,), (8, 13)), ((5,), (9, 14)), ((8, 9), (16,)),
        )[n]
        for i in waits:
            self.wait(i)
        for i in starts:
            self.copy(i).start()

    def collect(self):
        for i in (3,) + tuple(range(10, 17)):
            self.wait(i)

    def sent(self):
        for i in range(17):
            self.copy(i).wait_send()


def add_slots(total, slots, lanes):
    for k in range(7):
        total = total + slots[k, :, lanes].astype(F32)
    return total


def main_kernel(
    wz, wx, wbc, wdt, norm, wo, tok, cot, seg, cwx, cwb, cbx, cbb, dtb, alog, dsk, gg, ex, ext,
    out_o, oz, oo, dtok_o, ox, odt, obc, onorm, conv_o, convb_o, bc_o, bcb_o, ggate_o, dtb_o, alog_o, dsk_o,
    in_o, zo_o, xn_o, gain_o, dz_o, gate_o, dx_o, dbc_o, ddt_o, small_o,
    mine1, mine2, etok_b, eseg, xs, st, st_low, st_in, y_s, er_s, c_s, row_s, row_r, yn_o,
    xbc_o, pre_o, dtr_o, colm_o, st_o, dy_o, branch_o, carry_o, gz_o, go_o,
    acts, grad, heads, g_in, tail_r, ret_s, ret_r, near, relay, from_d, from_u,
    sz, so, chunk, rg, cs, cr,
    gx, near2, relay2, from_d2, from_u2, sx, chunk2, rg2, cs2, cr2, t2,
    sm, sm_s, sm_c, sm_x, sm_r, sm_t, nm, nm_s, nm_c, nm_x, nm_r, nm_t, send, recv,
):
    shard, context, tensor, core, chip, chips, sibling, others, partner, ranks, group, at = places()
    mine1[:, 0:512] = wx[...]
    mine1[:, 512:768] = wbc[...]
    mine1[:, 768:896] = jnp.zeros((64, 128), BF)
    mine1[:, 768:776] = wdt[...]
    mine1[:, 776:777] = jnp.broadcast_to(norm[...].astype(F32), (8, 64)).T[:, 0:1].astype(BF)
    mine2[:, 0:512] = wz[...]
    mine2[:, 512:1024] = wo[...]
    greet([sibling, partner] + others[1:] + group[1:])
    links = Links(send, recv)

    links.count = 34
    seg_in = links.copy(seg, eseg, partner)
    tokens_in = links.copy(tok.at[pl.ds(1024 - EDGE, EDGE)], etok_b, partner)
    spread1 = Spread(mine1, in_o, 0, send, recv, core, chip, at)
    spread2 = Spread(mine2, zo_o, 17, send, recv, core, chip, at)
    spread1.begin()
    seg_in.wait_recv()
    seg_t = seg[...].astype(F32).T
    edge_t = jnp.where(context > 0, eseg[...].astype(F32).T, 0.0)
    edge_col = edge_t[120:128, 7:8]
    start = jnp.where(edge_col[7:8] == seg_t[0:1, 0:1], seg_t[0:1, 0:1], -1.0)
    colm_o[1024:1032] = jnp.zeros((8, 8), F32)
    for b in range(8):
        col = seg_t[:, b : b + 1]
        before = edge_col if b == 0 else seg_t[120:128, b - 1 : b]
        longer = jnp.concatenate([before, col], axis=0)
        entering = start if b == 0 else before[7:8]
        marks = [col]
        for d in range(1, 4):
            marks.append(jnp.where(longer[8 - d : 136 - d] == col, 1.0, 0.0))
        for value in (start, entering, col[127:128]):
            marks.append(jnp.where(col == value, 1.0, 0.0))
        marks.append(jnp.zeros_like(col))
        colm_o[b * Q : b * Q + Q] = jnp.concatenate(marks, axis=1)

    for n in range(7):
        spread1.event(n)
    spread2.begin()
    spread1.collect()
    tokens_in.wait_recv()

    a_neg = -jnp.exp(alog[...])
    causal, _ = triangles()
    lower = as_low(causal)
    gain_row = in_o[:, 768:896].astype(F32).T[8:9]
    gain_o[...] = gain_row

    def normed(block):
        plain = block.astype(F32)
        root = lax.rsqrt(jnp.mean(plain * plain, axis=1, keepdims=True) + EPSILON)
        return (plain * root * gain_row).astype(BF)

    edge_tokens = jnp.where(context > 0, etok_b[...].astype(F32), 0.0)
    edge = mm(normed(edge_tokens), in_o[:, 0:768]).astype(BF)
    xbc_o[0:EDGE] = edge
    xs[0:EDGE] = edge.astype(F32)
    st[...] = jnp.zeros_like(st)
    expand = ex[...]
    dsk_e = mm2(dsk[...], expand)

    def body(b, run):
        r = pl.ds(pl.multiple_of(b * Q, Q), Q)
        rn = pl.ds(pl.multiple_of(b * Q + EDGE, EDGE), Q)
        xn = normed(tok[r])
        xn_o[r] = xn
        both = mm(xn, in_o[...])
        xb = both[:, 0:768].astype(BF)
        xbc_o[rn] = xb
        xs[rn] = xb.astype(F32)
        raw = both[:, 768:776]
        dtr_o[r] = raw
        marks = colm_o[r]
        acts = []
        for c in range(6):
            lanes = slice(c * 128, c * 128 + 128)
            cw, cb, at = (cwx, cbx, lanes) if c < 4 else (cwb, cbb, slice(c * 128 - 512, c * 128 - 384))
            slab = xs[pl.ds(pl.multiple_of(b * Q, Q), Q + EDGE), lanes]
            pre = cb[:, at] + cw[3:4, at] * slab[EDGE:]
            for d in range(1, 4):
                pre = pre + (cw[3 - d : 4 - d, at] * slab[EDGE - d : Q + EDGE - d]) * marks[:, d : d + 1]
            pre_o[r, lanes] = pre
            acts.append(pre * sigmoid(pre))
        b_low = acts[4].astype(BF)
        c_low = acts[5].astype(BF)
        c_s[r] = c_low
        dt = softplus(raw + dtb[...])
        cum = mm3_left(lower, dt * a_neg)
        er_s[r] = jnp.exp(run + cum) * marks[:, 4:5]
        cum_t = cum.T
        last = cum[Q - 1 : Q]
        enter = jnp.exp(cum) * marks[:, 5:6]
        tail = jnp.exp(last - cum) * marks[:, 6:7]
        dt_e = mm2(dt, expand)
        enter_e = mm2(enter, expand)
        tail_e = mm2(tail, expand)
        mask = causal & (marks[:, 0:1] == seg[pl.ds(b, 1), :].astype(F32))
        scores = jnp.where(mask, mm_nt(c_low, b_low), 0.0)
        state = st[...]
        inter = mm(c_low, state.astype(BF))
        pieces = []
        for p in range(4):
            lanes = slice(p * 128, p * 128 + 128)
            xdt = acts[p] * dt_e[:, lanes]
            pieces.append((xdt * tail_e[:, lanes]).astype(BF))
            ws = []
            for h in (2 * p, 2 * p + 1):
                decay = jnp.exp(jnp.minimum(cum[:, h : h + 1] - cum_t[h : h + 1, :], 0.0))
                ws.append((decay * scores).astype(BF))
            intra = mm(jnp.concatenate(ws, axis=1), halves(xdt.astype(BF)))
            y_s[r, lanes] = intra + enter_e[:, lanes] * inter[:, lanes] + dsk_e[:, lanes] * acts[p]
        fresh = mm_tn(b_low, jnp.concatenate(pieces, axis=1))
        st[...] = enter_e[Q - 1 : Q] * state + fresh

        for n in range(7):
            pl.when(b == n)(partial(spread2.event, n))

        return run + last

    lax.fori_loop(0, 8, body, jnp.zeros((1, 8), F32))
    st_low[...] = st[...].astype(BF)
    state_in = links.copy(st_low, st_in, partner)
    spread2.collect()

    def project(b, carry):
        r = pl.ds(pl.multiple_of(b * Q, Q), Q)
        acts[r, 0:512] = mm(xn_o[r], zo_o[:, 0:512])
        dy_o[r] = mm(cot[r], zo_o[:, 512:1024])
        return carry

    lax.fori_loop(0, 8, project, 0)
    state_in.wait_recv()
    st_o[...] = jnp.where(context > 0, st_in[...].astype(F32), 0.0)

    def sums(b, carry):
        r = pl.ds(pl.multiple_of(b * Q, Q), Q)
        y = y_s[r] + mm2(er_s[r], expand) * mm(c_s[r], st_o[...].astype(BF))
        y_s[r] = y
        z = acts[r, 0:512]
        gated = y * (z * sigmoid(z))
        first_sum = jnp.sum(gated * gated, axis=1, keepdims=True)
        second_sum = jnp.sum(dy_o[r] * gg[...] * gated, axis=1, keepdims=True)
        row_s[b] = jnp.concatenate([first_sum, second_sum, jnp.zeros((Q, 6), F32)], axis=1).T
        return carry

    lax.fori_loop(0, 8, sums, 0)
    rows_in = [links.copy(row_s, row_r.at[k - 1], group[k]) for k in range(1, 4)]
    for copy in rows_in:
        copy.wait_recv()
    gate_o[...] = jnp.zeros_like(gate_o)
    st[...] = jnp.zeros_like(st)

    def finish(b, carry):
        r = pl.ds(pl.multiple_of(b * Q, Q), Q)
        total = (row_s[b] + row_r[0, b] + row_r[1, b] + row_r[2, b]).T
        root = lax.rsqrt(total[:, 0:1] * (1.0 / INNER) + EPSILON)
        cross = (root * root * root) * (total[:, 1:2] * (1.0 / INNER))
        er_e = mm2(er_s[r], expand)
        normals, carries = [], []
        for p in range(4):
            lanes = slice(p * 128, p * 128 + 128)
            y = y_s[r, lanes]
            z = acts[r, lanes]
            dn = dy_o[r, lanes]
            sig = sigmoid(z)
            gate = z * sig
            gated = y * gate
            scaled = gated * root
            normals.append((scaled * gg[:, lanes]).astype(BF))
            gate_o[p : p + 1] += jnp.sum(dn * scaled, axis=0, keepdims=True)
            d_gated = root * (dn * gg[:, lanes]) - gated * cross
            d_y = d_gated * gate
            dy_o[r, lanes] = d_y
            dz_o[r, lanes] = (d_gated * y * (sig * (1.0 + z * (1.0 - sig)))).astype(BF)
            carries.append((d_y * er_e[:, lanes]).astype(BF))
        low = jnp.concatenate(normals, axis=1)
        yn_o[r] = low
        branch_o[r] = mm_nt(low, zo_o[:, 512:1024]).astype(BF)
        st[...] += mm_tn(c_s[r], jnp.concatenate(carries, axis=1))
        return carry

    lax.fori_loop(0, 8, finish, 0)
    carry_o[...] = st[...].astype(BF)
    carry_in = links.copy(carry_o, g_in, partner)
    ring = Ring(links, tensor, group)
    ring.reduce_first(branch_o, near, from_d, from_u)
    for m in range(8):
        lanes = slice(m * 128, m * 128 + 128)
        gz_o[m] = mm_tn(xn_o[:, lanes], dz_o[...]).astype(BF).reshape(2, 64, 512)
        go_o[m] = mm_tn(cot[:, lanes], yn_o[...]).astype(BF).reshape(2, 64, 512)
    sib_in = (links.copy(gz_o.at[:, 1 - core], sz, sibling), links.copy(go_o.at[:, 1 - core], so, sibling))
    a_neg = -jnp.exp(alog[...])
    causal, anti = triangles()
    lower = as_low(causal)
    upper = as_low(anti)
    expand = ex[...]
    expand_t = ext[...]
    dsk_e = mm2(dsk[...], expand)

    def head_sum(v):
        return mm2(v, expand_t)

    y_s[0:Q] = st_o[...]

    def forward(b, carry):
        r = pl.ds(pl.multiple_of(b * Q, Q), Q)
        marks = colm_o[r]
        dt = softplus(dtr_o[r] + dtb[...])
        cum = mm3_left(lower, dt * a_neg)
        last = cum[Q - 1 : Q]
        tail = jnp.exp(last - cum) * marks[:, 6:7] * dt
        keep_e = mm2(jnp.exp(last) * marks[Q - 1 : Q, 5:6], expand)
        tail_e = mm2(tail, expand)
        pieces = []
        for c in range(6):
            lanes = slice(c * 128, c * 128 + 128)
            pre = pre_o[r, lanes]
            act = pre * sigmoid(pre)
            acts[r, lanes] = act
            if c < 4:
                pieces.append((act * tail_e[:, lanes]).astype(BF))
            if c == 4:
                b_low = act.astype(BF)
        fresh = mm_tn(b_low, jnp.concatenate(pieces, axis=1))
        y_s[pl.ds(pl.multiple_of(b * Q + Q, Q), Q)] = keep_e * y_s[r] + fresh
        return carry

    lax.fori_loop(0, 7, forward, 0)
    r7 = slice(7 * Q, 8 * Q)
    for c in range(6):
        lanes = slice(c * 128, c * 128 + 128)
        pre = pre_o[r7, lanes]
        acts[r7, lanes] = pre * sigmoid(pre)
    for copy in sib_in:
        copy.wait_recv()

    def merge(c, carry):
        for mine, theirs, at in ((gz_o, sz, 0), (go_o, so, 512)):
            chunk[c, :, at : at + 512] = (mine[c, core].astype(F32) + theirs[c].astype(F32)).astype(BF)
        return carry

    lax.fori_loop(0, 8, merge, 0)
    grads_in = [links.copy(chunk.at[chips[k]], rg.at[k - 1], others[k]) for k in range(1, 8)]
    carry_in.wait_recv()
    grad[...] = jnp.where(context == 0, g_in[...].astype(F32), 0.0)
    heads[...] = jnp.zeros_like(heads)
    xs[0:8] = jnp.zeros((8, 768), F32)
    xs[1032:1040] = jnp.zeros((8, 768), F32)

    def backward(i, carry):
        b = 7 - i
        r = pl.ds(pl.multiple_of(b * Q, Q), Q)
        rp = pl.ds(pl.multiple_of(b * Q + 8, 8), Q)
        marks = colm_o[r]
        raw = dtr_o[r] + dtb[...]
        dt = softplus(raw)
        cum = mm3_left(lower, dt * a_neg)
        cum_t = cum.T
        last = cum[Q - 1 : Q]
        enter = jnp.exp(cum) * marks[:, 5:6]
        tail = jnp.exp(last - cum) * marks[:, 6:7]
        dt_e = mm2(dt, expand)
        enter_e = mm2(enter, expand)
        tail_e = mm2(tail, expand)
        keep_e = enter_e[Q - 1 : Q]
        b_low = acts[r, 512:640].astype(BF)
        c_low = acts[r, 640:768].astype(BF)
        state = y_s[r]
        state_low = state.astype(BF)
        g_now = grad[...]
        g_low = g_now.astype(BF)
        inter = mm(c_low, state_low)
        back = mm(b_low, g_low)
        mask = causal & (marks[:, 0:1] == seg[pl.ds(b, 1), :].astype(F32))
        scores = jnp.where(mask, mm_nt(c_low, b_low), 0.0)
        kept = jnp.sum(state * g_now, axis=0, keepdims=True) * keep_e
        entered, tailed, e_terms, q_terms, x_terms, k_terms = [], [], [], [], [], []
        rows, cols = [], []
        d_scores = jnp.zeros((Q, Q), F32)
        for p in range(4):
            lanes = slice(p * 128, p * 128 + 128)
            x = acts[r, lanes]
            dys = dy_o[r, lanes]
            xdt = x * dt_e[:, lanes]
            xdt_low = xdt.astype(BF)
            ed = enter_e[:, lanes] * dys
            tx = tail_e[:, lanes] * xdt
            entered.append(ed.astype(BF))
            tailed.append(tx.astype(BF))
            dy_two = halves(dys.astype(BF))
            dw_two = mm_nt(dy_two, xdt_low)
            ws = []
            for k in range(2):
                h = 2 * p + k
                decay = jnp.exp(jnp.minimum(cum[:, h : h + 1] - cum_t[h : h + 1, :], 0.0))
                weight = decay * scores
                dw = dw_two[k * Q : k * Q + Q]
                d_scores = d_scores + decay * dw
                both = weight * dw
                rows.append(jnp.sum(both, axis=1, keepdims=True))
                cols.append(jnp.sum(both, axis=0, keepdims=True))
                ws.append(weight.astype(BF))
            dxdt = mm_tn(jnp.concatenate(ws, axis=0), dy_two) + tail_e[:, lanes] * back[:, lanes]
            e_terms.append(ed * inter[:, lanes] - tx * back[:, lanes])
            q_terms.append(jnp.sum(tx * back[:, lanes], axis=0, keepdims=True) + kept[:, lanes])
            x_terms.append(dxdt * x)
            k_terms.append(jnp.sum(dys * x, axis=0, keepdims=True))
            pre = pre_o[r, lanes]
            sig = sigmoid(pre)
            xs[rp, lanes] = (dxdt * dt_e[:, lanes] + dsk_e[:, lanes] * dys) * (sig * (1.0 + pre * (1.0 - sig)))
        entered = jnp.concatenate(entered, axis=1)
        tailed = jnp.concatenate(tailed, axis=1)
        ds_low = jnp.where(mask, d_scores, 0.0).astype(BF)
        d_c = mm_nt(entered, state_low) + mm(ds_low, b_low)
        d_b = mm_nt(tailed, g_low) + mm_tn(ds_low, c_low)
        grad[...] = keep_e * g_now + mm_tn(c_low, entered)
        for c, value in ((4, d_b), (5, d_c)):
            lanes = slice(c * 128, c * 128 + 128)
            pre = pre_o[r, lanes]
            sig = sigmoid(pre)
            xs[rp, lanes] = value * (sig * (1.0 + pre * (1.0 - sig)))
        d_cum = jnp.concatenate(rows, axis=1) - jnp.concatenate(cols, axis=0).T
        d_cum = d_cum + head_sum(jnp.concatenate(e_terms, axis=1))
        d_log = mm3_left(upper, d_cum) + head_sum(jnp.concatenate(q_terms, axis=1))
        d_dt = d_log * a_neg + head_sum(jnp.concatenate(x_terms, axis=1))
        d_raw = d_dt * sigmoid(raw)
        ddt_o[r] = jnp.concatenate([d_raw, jnp.zeros((Q, 120), F32)], axis=1).astype(BF)
        heads[0:1] += jnp.sum(d_raw, axis=0, keepdims=True)
        heads[1:2] += jnp.sum(d_log * dt, axis=0, keepdims=True) * a_neg
        heads[2:3] += head_sum(jnp.concatenate(k_terms, axis=1))
        return carry

    lax.fori_loop(0, 1, backward, 0)
    ring.reduce_second(branch_o, near, relay, from_d, from_u)
    lax.fori_loop(1, 4, backward, 0)
    ring.reduce_wait()

    def finish_out(i, carry):
        r = pl.ds(pl.multiple_of(i * 64, 64), 64)
        rt = pl.ds(pl.multiple_of(tensor * 256 + i * 64, 64), 64)
        total = branch_o[rt].astype(F32) + from_d[r].astype(F32) + from_u[r].astype(F32)
        out_o[rt] = (tok[rt].astype(F32) + total).astype(BF)
        return carry

    lax.fori_loop(0, 4, finish_out, 0)
    ring.gather_first(out_o)
    lax.fori_loop(4, 8, backward, 0)
    small_o[...] = jnp.zeros_like(small_o)
    small_o[24:32, 0:8] = heads[...]

    for c in range(6):
        lanes = slice(c * 128, c * 128 + 128)
        first = xs[0:16, lanes]
        cw, wl = (cwx, lanes) if c < 4 else (cwb, slice(c * 128 - 512, c * 128 - 384))
        flags = jnp.concatenate([jnp.zeros((8, 8), F32), colm_o[0:8]], axis=0)
        total = jnp.zeros((8, 128), F32)
        for d in range(1, 4):
            total = total + cw[3 - d : 4 - d, wl] * (first * flags[:, d : d + 1])[d : d + 8]
        ret_s[:, lanes] = total
    ret_in = links.copy(ret_s, ret_r, partner)
    ring.gather_second(out_o)
    for copy in grads_in:
        copy.wait_recv()
    for at in range(0, 1024, 128):
        lanes = slice(at, at + 128)
        cs[:, lanes] = add_slots(chunk[chip, :, lanes].astype(F32), rg, lanes).astype(BF)
    grads_ctx = links.copy(cs, cr, partner)
    for c in range(6):
        lanes = slice(c * 128, c * 128 + 128)
        cw, wl = (cwx, lanes) if c < 4 else (cwb, slice(c * 128 - 512, c * 128 - 384))

        def conv(b, sums, lanes=lanes, c=c, cw=cw, wl=wl):
            r = pl.ds(pl.multiple_of(b * Q, Q), Q)
            slab = xs[pl.ds(pl.multiple_of(b * Q + 8, 8), Q + 8), lanes]
            marks = colm_o[pl.ds(pl.multiple_of(b * Q, Q), Q + 8)]
            xin = xbc_o[pl.ds(pl.multiple_of(b * Q, Q), Q + EDGE), lanes].astype(F32)
            main = slab[0:Q]
            out = cw[3:4, wl] * main
            new = [sums[0] + jnp.sum(main, axis=0, keepdims=True),
                   sums[1] + jnp.sum(main * xin[EDGE:], axis=0, keepdims=True)]
            for d in range(1, 4):
                masked = slab * marks[:, d : d + 1]
                out = out + cw[3 - d : 4 - d, wl] * masked[d : d + Q]
                new.append(sums[d + 1] + jnp.sum(masked[0:Q] * xin[EDGE - d : Q + EDGE - d], axis=0, keepdims=True))
            if c < 4:
                dx_o[r, lanes] = out.astype(BF)
            else:
                dbc_o[r, slice(c * 128 - 512, c * 128 - 384)] = out.astype(BF)

            @pl.when(b == 7)
            def _():
                tail_r[:, lanes] = out[Q - EDGE :]

            return tuple(new)

        zero = jnp.zeros((1, 128), F32)
        sums = lax.fori_loop(0, 8, conv, (zero,) * 5)
        at = 16 + c if c < 4 else 36 + c
        small_o[at : at + 1] = sums[0]
        for d in range(4):
            at = (3 - d) * 4 + c if c < 4 else 28 + (3 - d) * 2 + c
            small_o[at : at + 1] = sums[d + 1]
    ret_in.wait_recv()
    returned = jnp.where(context == 0, ret_r[...], 0.0)
    last = tail_r[...] + jnp.concatenate([jnp.zeros((EDGE - 8, 768), F32), returned], axis=0)
    dx_o[1024 - EDGE : 1024] = last[:, 0:512].astype(BF)
    dbc_o[1024 - EDGE : 1024] = last[:, 512:768].astype(BF)
    grads_ctx.wait_recv()
    oz[...] = cs[:, 0:512].astype(F32) + cr[:, 0:512].astype(F32)
    oo[...] = cs[:, 512:1024].astype(F32) + cr[:, 512:1024].astype(F32)
    for made in ring.first + ring.alone:
        made.wait_send()
        links.started = [other for other in links.started if other is not made]
    sm[...] = small_o[...]
    sm[20:24] = gate_o[...]
    wide = Ring(links, tensor, group)

    def make(r):
        total = mm_nt(dz_o[r], zo_o[:, 0:512]) + mm_nt(dx_o[r], in_o[:, 0:512]) + mm_nt(ddt_o[r], in_o[:, 768:896]) + mm_nt(dbc_o[r], in_o[:, 512:768])
        branch_o[r] = total.astype(BF)

    wide.reduce_first(branch_o, near2, from_d2, from_u2, make)
    small_in = links.copy(sm, sm_s, sibling)

    def outer(m):
        block = xn_o[:, m * 128 : m * 128 + 128]
        gx[m, :, :, 0:512] = mm_tn(block, dx_o[...]).astype(BF).reshape(2, 64, 512)
        gx[m, :, :, 512:640] = mm_tn(block, ddt_o[...]).astype(BF).reshape(2, 64, 128)
        gx[m, :, :, 640:896] = mm_tn(block, dbc_o[...]).astype(BF).reshape(2, 64, 256)

    make(wide.half(wide.t_up, 0))
    make(wide.half(wide.t_down, 1))
    for m in range(4):
        outer(m)
    wide.reduce_second(branch_o, near2, relay2, from_d2, from_u2)
    for m in range(4, 8):
        outer(m)
    sib_in = links.copy(gx.at[:, 1 - core], sx, sibling)
    small_in.wait_recv()
    sm_c[chip] = sm[...] + sm_s[...]
    small_base = links.count - 1
    for k in range(1, 8):
        links.copy(sm_c.at[chip], sm_c.at[chip], others[k])
    make(wide.half(tensor, 0))
    make(wide.half(tensor, 1))
    sib_in.wait_recv()

    def merge(c, carry):
        chunk2[c] = (gx[c, core].astype(F32) + sx[c].astype(F32)).astype(BF)
        return carry

    lax.fori_loop(0, 8, merge, 0)
    grads_in = [links.copy(chunk2.at[chips[k]], rg2.at[k - 1], others[k]) for k in range(1, 8)]

    wide.reduce_wait()

    def inner(i, g_norm):
        r = pl.ds(pl.multiple_of(i * 64, 64), 64)
        rt = pl.ds(pl.multiple_of(tensor * 256 + i * 64, 64), 64)
        total = branch_o[rt].astype(F32) + from_d2[r].astype(F32) + from_u2[r].astype(F32)
        plain = tok[rt].astype(F32)
        root = lax.rsqrt(jnp.mean(plain * plain, axis=1, keepdims=True) + EPSILON)
        stat = plain * root
        d_plain = total * gain_o[...]
        mean = jnp.mean(d_plain * plain, axis=1, keepdims=True)
        dtok_o[rt] = (cot[rt].astype(F32) + root * d_plain - stat * (root * root) * mean).astype(BF)
        return g_norm + jnp.sum(total * stat, axis=0, keepdims=True)

    g_norm = lax.fori_loop(0, 4, inner, jnp.zeros((1, 1024), F32))
    wide.gather_first(dtok_o)
    for c in range(8):
        nm[c : c + 1] = g_norm[:, c * 128 : c * 128 + 128]
    norm_sib = links.copy(nm, nm_s, sibling)

    for k in range(1, 8):
        source = lax.rem(chip + 8 - k, 8)
        arrival(None, sm_c.at[source], recv.at[small_base + k], others[k]).wait_recv()
    total = sm_c[0]
    for c in range(1, 8):
        total = total + sm_c[c]
    sm_x[...] = total
    small_ctx = links.copy(sm_x, sm_r, partner)
    norm_sib.wait_recv()
    nm_c[chip] = nm[...] + nm_s[...]
    norm_base = links.count - 1
    for k in range(1, 8):
        links.copy(nm_c.at[chip], nm_c.at[chip], others[k])
    for copy in grads_in:
        copy.wait_recv()
    for col in range(0, 896, 128):
        lanes = slice(col, col + 128)
        cs2[:, lanes] = add_slots(chunk2[chip, :, lanes].astype(F32), rg2, lanes).astype(BF)
    grads_ctx = links.copy(cs2, cr2, partner)
    wide.gather_second(dtok_o)
    for k in range(1, 8):
        source = lax.rem(chip + 8 - k, 8)
        arrival(None, nm_c.at[source], recv.at[norm_base + k], others[k]).wait_recv()
    total = nm_c[0]
    for c in range(1, 8):
        total = total + nm_c[c]
    nm_x[...] = total
    norm_ctx = links.copy(nm_x, nm_r, partner)
    small_ctx.wait_recv()
    sums = sm_x[...] + sm_r[...]
    for k in range(4):
        for p in range(4):
            conv_o[k : k + 1, p * 128 : p * 128 + 128] = sums[k * 4 + p : k * 4 + p + 1]
    for p in range(4):
        convb_o[:, p * 128 : p * 128 + 128] = sums[16 + p : 17 + p]
        ggate_o[:, p * 128 : p * 128 + 128] = sums[20 + p : 21 + p]
    dtb_o[...] = sums[24:25, 0:8]
    alog_o[...] = sums[25:26, 0:8]
    dsk_o[...] = sums[26:27, 0:8]
    sm_t[tensor] = sums[32:48]
    small_t = links.count
    for k in range(1, 4):
        links.copy(sm_t.at[tensor], sm_t.at[tensor], group[k])
    norm_ctx.wait_recv()
    nm_t[tensor] = nm_x[...] + nm_r[...]
    norm_t = links.count
    for k in range(1, 4):
        links.copy(nm_t.at[tensor], nm_t.at[tensor], group[k])
    grads_ctx.wait_recv()
    ox[...] = cs2[:, 0:512].astype(F32) + cr2[:, 0:512].astype(F32)
    t2[tensor] = cs2[:, 640:896].astype(F32) + cr2[:, 640:896].astype(F32)
    grads2_t = links.count
    for k in range(1, 4):
        links.copy(t2.at[tensor], t2.at[tensor], group[k])
    odt[...] = (cs2[:, 512:640].astype(F32) + cr2[:, 512:640].astype(F32))[:, 0:8]
    for k in range(1, 4):
        source = lax.rem(tensor + 4 - k, 4)
        arrival(None, sm_t.at[source], recv.at[small_t + k - 1], group[k]).wait_recv()
        arrival(None, nm_t.at[source], recv.at[norm_t + k - 1], group[k]).wait_recv()
        arrival(None, t2.at[source], recv.at[grads2_t + k - 1], group[k]).wait_recv()
    sums = (sm_t[0] + sm_t[1]) + (sm_t[2] + sm_t[3])
    for k in range(4):
        for p in range(2):
            bc_o[k : k + 1, p * 128 : p * 128 + 128] = sums[k * 2 + p : k * 2 + p + 1]
    for p in range(2):
        bcb_o[:, p * 128 : p * 128 + 128] = sums[8 + p : 9 + p]
    obc[...] = (t2[0] + t2[1]) + (t2[2] + t2[3])
    nm_s[...] = (nm_t[0] + nm_t[1]) + (nm_t[2] + nm_t[3])
    row = nm_s[pl.ds(chip, 1), :]
    onorm[...] = jnp.where(core == 0, row[:, 0:64], row[:, 64:128])
    wide.gather_wait(dtok_o)
    ring.gather_wait(out_o)
    links.finish()
    spread1.sent()
    spread2.sent()


def call(kernel, out_shapes, scratch, *args, specs=None, collective_id=None):
    return pl.pallas_call(
        kernel,
        out_shape=[jax.ShapeDtypeStruct(s, d) for s, d in out_shapes],
        in_specs=[pl.BlockSpec(memory_space=pl.ANY if n in (specs or ()) else pltpu.VMEM) for n in range(len(args))],
        out_specs=[pl.BlockSpec(memory_space=pltpu.VMEM)] * len(out_shapes),
        scratch_shapes=[pltpu.SemaphoreType.DMA(s) if d is None else pltpu.VMEM(s, d) for s, d in scratch],
        compiler_params=pltpu.CompilerParams(vmem_limit_bytes=VMEM_LIMIT, collective_id=collective_id, has_side_effects=collective_id is not None
        ),
    )(*args)


def local(
    tokens,
    segment,
    norm_gain,
    w_z,
    w_x,
    w_dt,
    w_bc,
    conv_x,
    conv_xb,
    conv_bc,
    conv_bcb,
    dt_bias,
    a_log,
    d_skip,
    gate_gain,
    w_out,
    cotangent,
):
    length = tokens.shape[0]
    head_count = dt_bias.shape[0]
    inner_width = head_count * HEADDIM
    bc_width = 2 * STATE
    seg = segment.reshape(8, 128)
    expand_np = np.kron(np.eye(8), np.ones((1, HEADDIM)))
    expand = jnp.asarray(expand_np, BF)
    expand_t = jnp.asarray(expand_np.T, BF)
    wide = (length, inner_width)
    state = (STATE, inner_width)
    grid = (8, 2, 64, 512)
    heads = (dt_bias[None], a_log[None], d_skip[None])
    own = (64, 512)
    half = ((2, 128, 1024), BF)
    rows = ((256, 1024), BF)

    def vector(shape, last):
        return [(s, F32) for s in (shape, shape, (8,) + shape, shape, shape, last)]

    (output, o_z, o_out, d_tokens, o_x, o_dt, o_bc, o_norm, conv_o, convb_o, cbc_o, cbcb_o, gate_o, dtb_o, alog_o, dsk_o) = call(
        main_kernel,
        [((length, 1024), BF), (own, F32), (own, F32), ((length, 1024), BF), (own, F32), ((64, 8), F32), ((64, 256), F32), ((1, 64), F32),
         ((4, 512), F32), ((1, 512), F32), ((4, 256), F32), ((1, 256), F32), ((1, 512), F32), ((1, 8), F32), ((1, 8), F32), ((1, 8), F32)],
        [((1024, 896), BF), ((1024, 1024), BF), ((length, 1024), BF), ((1, 1024), F32), (wide, BF), ((4, 128), F32),
         (wide, BF), ((length, 2 * STATE), BF), ((length, 128), BF), ((48, 128), F32),
         ((64, 896), BF), ((64, 1024), BF), ((EDGE, 1024), BF), ((8, 128), jnp.int32), ((length + EDGE, 768), F32), (state, F32), (state, BF), (state, BF),
         (wide, F32), ((length, 8), F32), ((length, STATE), BF), ((8, 8, 128), F32), ((3, 8, 8, 128), F32), (wide, BF),
         ((length + EDGE, 768), BF), ((length, 768), F32), ((length, 8), F32), ((length + 8, 8), F32), (state, F32), (wide, F32),
         ((length, 1024), BF), (state, BF), (grid, BF), (grid, BF),
         ((length, 768), F32), (state, F32), ((8, 8), F32),
         (state, BF), ((EDGE, 768), F32), ((8, 768), F32), ((8, 768), F32), half, half, rows, rows,
         ((8, 64, 512), BF), ((8, 64, 512), BF), ((8, 64, 1024), BF), ((7, 64, 1024), BF), ((64, 1024), BF), ((64, 1024), BF),
         ((8, 2, 64, 896), BF), half, half, rows, rows,
         ((8, 64, 896), BF), ((8, 64, 896), BF), ((7, 64, 896), BF), ((64, 896), BF), ((64, 896), BF), ((4, 64, 256), F32),
         *vector((48, 128), (4, 16, 128)), *vector((8, 128), (4, 8, 128)),
         ((120,), None), ((120,), None)],
        w_z, w_x, w_bc, w_dt, norm_gain[None], w_out, tokens, cotangent, seg,
        conv_x, conv_bc, conv_xb[None], conv_bcb[None], *heads, gate_gain[None], expand, expand_t,
        collective_id=1,
    )
    return (
        output, d_tokens, o_norm[0], o_z, o_x, o_dt, o_bc, conv_o, convb_o[0], cbc_o, cbcb_o[0],
        dtb_o[0], alog_o[0], dsk_o[0], gate_o[0], o_out,
    )


def solution(mesh):
    in_specs = (
        P(("shard", "context"), None),
        P(("shard", "context")),
        P("shard"),
        P("shard", "tensor"),
        P("shard", "tensor"),
        P("shard", "tensor"),
        P("shard", None),
        P(None, "tensor"),
        P("tensor"),
        P(),
        P(),
        P("tensor"),
        P("tensor"),
        P("tensor"),
        P("tensor"),
        P("shard", "tensor"),
        P(("shard", "context"), None),
    )
    out_specs = (
        P(("shard", "context"), None),
        P(("shard", "context"), None),
        P("shard"),
        P("shard", "tensor"),
        P("shard", "tensor"),
        P("shard", "tensor"),
        P("shard", None),
        P(None, "tensor"),
        P("tensor"),
        P(),
        P(),
        P("tensor"),
        P("tensor"),
        P("tensor"),
        P("tensor"),
        P("shard", "tensor"),
    )
    return jax.shard_map(local, mesh=mesh, in_specs=in_specs, out_specs=out_specs, check_vma=False)
```

```python
from functools import partial

import jax
import jax.numpy as jnp
import numpy as np
from jax import lax
from jax.experimental import pallas as pl
from jax.experimental.pallas import tpu as pltpu
from jax.sharding import PartitionSpec as P

HEADDIM = 64
STATE = 128
CONV = 4
INNER = 2048


EPSILON = 1e-05


F32 = jnp.float32
BF = jnp.bfloat16
Q = 128
EDGE = 16
VMEM_LIMIT = 60 * 1024 * 1024


def mm(a, b):
    return lax.dot_general(a, b, (((1,), (0,)), ((), ())), preferred_element_type=F32)


def mm_nt(a, b):
    return lax.dot_general(a, b, (((1,), (1,)), ((), ())), preferred_element_type=F32)


def mm_tn(a, b):
    return lax.dot_general(a, b, (((0,), (0,)), ((), ())), preferred_element_type=F32)


def split2(v):
    hi = v.astype(BF)
    return hi, (v - hi.astype(F32)).astype(BF)


def mm2(a, b):
    hi, lo = split2(a)
    return mm(hi, b) + mm(lo, b)


def mm3_left(a, b):
    hi, lo = split2(b)
    lo2 = (b - hi.astype(F32) - lo.astype(F32)).astype(BF)
    return mm(a, hi) + (mm(a, lo) + mm(a, lo2))


def softplus(v):
    return jnp.maximum(v, 0.0) + jnp.log1p(jnp.exp(-jnp.abs(v)))


def sigmoid(v):
    return 1.0 / (1.0 + jnp.exp(-v))


def triangles():
    rows = lax.broadcasted_iota(jnp.int32, (Q, Q), 0)
    cols = lax.broadcasted_iota(jnp.int32, (Q, Q), 1)
    return rows >= cols, rows <= cols


def as_low(mask):
    return jnp.where(mask, 1.0, 0.0).astype(BF)


def halves(slab):
    lane = lax.broadcasted_iota(jnp.int32, slab.shape, 1)
    zero = jnp.zeros_like(slab)
    first = jnp.where(lane < HEADDIM, slab, zero)
    second = jnp.where(lane >= HEADDIM, slab, zero)
    return jnp.concatenate([first, second], axis=0)


MESH = pl.DeviceIdType.MESH


class Links:
    def __init__(self, send, recv):
        self.send, self.recv, self.count, self.started = send, recv, 0, []

    def copy(self, src, dst, device):
        made = pltpu.make_async_remote_copy(
            src_ref=src,
            dst_ref=dst,
            send_sem=self.send.at[self.count],
            recv_sem=self.recv.at[self.count],
            device_id=device,
            device_id_type=MESH,
        )
        self.count += 1
        self.started.append(made)
        made.start()
        return made

    def finish(self):
        for made in self.started:
            made.wait_send()


def arrival(like, dst, links_recv, device):
    return pltpu.make_async_remote_copy(
        src_ref=dst, dst_ref=dst, send_sem=links_recv, recv_sem=links_recv, device_id=device, device_id_type=MESH
    )


def greet(devices):
    barrier = pltpu.get_barrier_semaphore()
    for device in devices:
        pl.semaphore_signal(barrier, inc=1, device_id=device, device_id_type=MESH)
    pl.semaphore_wait(barrier, len(devices))


def places():
    shard, context, tensor = (lax.axis_index(name) for name in ("shard", "context", "tensor"))
    core, chip = lax.rem(shard, 2), lax.div(shard, 2)

    def at(shard_to=None, context_to=None, tensor_to=None):
        return (
            shard if shard_to is None else shard_to,
            context if context_to is None else context_to,
            tensor if tensor_to is None else tensor_to,
        )

    chips = [None] + [lax.rem(chip + k, 8) for k in range(1, 8)]
    sibling = at(shard_to=chip * 2 + (1 - core))
    others = [None] + [at(shard_to=c * 2 + core) for c in chips[1:]]
    partner = at(context_to=1 - context)
    ranks = [None] + [lax.rem(tensor + k, 4) for k in range(1, 4)]
    group = [None] + [at(tensor_to=t) for t in ranks[1:]]
    return shard, context, tensor, core, chip, chips, sibling, others, partner, ranks, group, at


class Ring:
    def __init__(self, links, tensor, group):
        self.links, self.tensor = links, tensor
        self.up, self.down = group[1], group[3]
        self.t_up, self.t_down, self.t_far = (lax.rem(tensor + k, 4) for k in (1, 3, 2))

    def half(self, rank, which):
        return pl.ds(pl.multiple_of(rank * 256 + which * 128, 128), 128)

    def whole(self, rank):
        return pl.ds(pl.multiple_of(rank * 256, 256), 256)

    def reduce_first(self, src, near, from_down, from_up, make=None):
        def send(rank, which, dst, device):
            rows = self.half(rank, which)
            if make is not None:
                make(rows)
            return self.links.copy(src.at[rows], dst, device)

        self.first = (send(self.t_far, 0, near.at[0], self.up), send(self.t_far, 1, near.at[1], self.down))
        self.alone = (
            send(self.t_up, 1, from_down.at[pl.ds(128, 128)], self.up),
            send(self.t_down, 0, from_up.at[pl.ds(0, 128)], self.down),
        )

    def reduce_second(self, src, near, relay, from_down, from_up):
        copy = self.links.copy
        self.first[0].wait_recv()
        relay[0] = (near[0].astype(F32) + src[self.half(self.t_up, 0)].astype(F32)).astype(BF)
        up = copy(relay.at[0], from_down.at[pl.ds(0, 128)], self.up)
        self.first[1].wait_recv()
        relay[1] = (near[1].astype(F32) + src[self.half(self.t_down, 1)].astype(F32)).astype(BF)
        down = copy(relay.at[1], from_up.at[pl.ds(128, 128)], self.down)
        self.summed = (up, down)

    def reduce_wait(self):
        for made in self.alone + self.summed:
            made.wait_recv()

    def gather_first(self, ref):
        mine = ref.at[self.whole(self.tensor)]
        self.base = self.links.count
        self.links.copy(mine, mine, self.up)
        self.links.copy(mine, mine, self.down)

    def landed(self, slot, which, device):
        arrival(None, slot, self.links.recv.at[self.base + which], device).wait_recv()

    def gather_second(self, ref):
        self.landed(ref.at[self.whole(self.t_down)], 0, self.down)
        self.base2 = self.links.count
        up = ref.at[self.half(self.t_down, 0)]
        self.links.copy(up, up, self.up)
        self.landed(ref.at[self.whole(self.t_up)], 1, self.up)
        down = ref.at[self.half(self.t_up, 1)]
        self.links.copy(down, down, self.down)

    def gather_wait(self, ref):
        offset = self.base2 - self.base
        self.landed(ref.at[self.half(self.t_far, 0)], offset, self.down)
        self.landed(ref.at[self.half(self.t_far, 1)], offset + 1, self.up)


class Spread:
    def __init__(self, mine, out, base, send, recv, core, chip, at):
        self.mine, self.out, self.base, self.send, self.recv, self.core, self.chip = mine, out, base, send, recv, core, chip
        x = lax.rem(chip, 4)
        right, left, far = (chip - x + lax.rem(x + k, 4) for k in (1, 3, 2))
        over = lax.rem(chip + 4, 8)
        o_right, o_left, o_far = (lax.rem(c + 4, 8) for c in (right, left, far))
        there = [at(shard_to=c * 2 + core) for c in (over, right, left)]
        sibling = at(shard_to=chip * 2 + (1 - core))
        to_over, to_right, to_left = there
        self.copies = [
            (None, None, to_over), (None, None, to_right), (None, None, to_left), (None, None, sibling),
            (over, None, to_right), (over, None, to_left),
            (left, 0, to_right), (right, 1, to_left), (o_left, 0, to_right), (o_right, 1, to_left),
        ]
        owners = [over, left, right, o_left, o_right, far, o_far]
        self.copies += [(owner, None, sibling) for owner in owners]
        self.arrivals = [
            (over, None, core), (left, None, core), (right, None, core), (chip, None, 1 - core), (o_left, None, core), (o_right, None, core),
            (far, 0, core), (far, 1, core), (o_far, 0, core), (o_far, 1, core),
        ]
        self.arrivals += [(owner, None, 1 - core) for owner in owners]

    def slot(self, owner, core, half):
        start = (owner * 2 + core) * 64
        if half is None:
            return self.out.at[pl.ds(pl.multiple_of(start, 64), 64)]
        return self.out.at[pl.ds(pl.multiple_of(start + half * 32, 32), 32)]

    def copy(self, i):
        owner, half, device = self.copies[i]
        dst = self.slot(self.chip if owner is None else owner, self.core, half)
        src = self.mine if owner is None else dst
        return pltpu.make_async_remote_copy(
            src_ref=src, dst_ref=dst, send_sem=self.send.at[self.base + i], recv_sem=self.recv.at[self.base + i],
            device_id=device, device_id_type=MESH,
        )

    def wait(self, i):
        owner, half, core = self.arrivals[i]
        arrival(None, self.slot(owner, core, half), self.recv.at[self.base + i], self.copies[i][2]).wait_recv()

    def begin(self):
        for i in (0, 1, 2, 3):
            self.copy(i).start()
        self.out[pl.ds(pl.multiple_of((self.chip * 2 + self.core) * 64, 64), 64)] = self.mine[...]

    def event(self, n):
        waits, starts = (
            ((1,), (6, 11)), ((2,), (7, 12)), ((0,), (4, 5, 10)), ((6, 7), (15,)),
            ((4,), (8, 13)), ((5,), (9, 14)), ((8, 9), (16,)),
        )[n]
        for i in waits:
            self.wait(i)
        for i in starts:
            self.copy(i).start()

    def collect(self):
        for i in (3,) + tuple(range(10, 17)):
            self.wait(i)

    def sent(self):
        for i in range(17):
            self.copy(i).wait_send()


def add_slots(total, slots, lanes):
    for k in range(7):
        total = total + slots[k, :, lanes].astype(F32)
    return total


def main_kernel(
    wz, wx, wbc, wdt, norm, wo, tok, cot, seg, cwx, cwb, cbx, cbb, dtb, alog, dsk, gg, ex, ext,
    out_o, oz, oo, dtok_o, ox, odt, obc, onorm, conv_o, convb_o, bc_o, bcb_o, ggate_o, dtb_o, alog_o, dsk_o,
    in_o, zo_o, xn_o, gain_o, dz_o, gate_o, dx_o, dbc_o, ddt_o, small_o,
    mine1, mine2, etok_b, eseg, xs, st, st_low, st_in, y_s, er_s, c_s, row_s, row_r, yn_o,
    xbc_o, pre_o, dtr_o, colm_o, st_o, dy_o, branch_o, carry_o, gz_o, go_o,
    acts, grad, heads, g_in, tail_r, ret_s, ret_r, near, relay, from_d, from_u,
    sz, so, chunk, rg, cs, cr,
    gx, near2, relay2, from_d2, from_u2, sx, chunk2, rg2, cs2, cr2, t2,
    sm, sm_s, sm_c, sm_x, sm_r, sm_t, nm, nm_s, nm_c, nm_x, nm_r, nm_t, send, recv,
):
    shard, context, tensor, core, chip, chips, sibling, others, partner, ranks, group, at = places()
    mine1[:, 0:512] = wx[...]
    mine1[:, 512:768] = wbc[...]
    mine1[:, 768:896] = jnp.zeros((64, 128), BF)
    mine1[:, 768:776] = wdt[...]
    mine1[:, 776:777] = jnp.broadcast_to(norm[...].astype(F32), (8, 64)).T[:, 0:1].astype(BF)
    mine2[:, 0:512] = wz[...]
    mine2[:, 512:1024] = wo[...]
    greet([sibling, partner] + others[1:] + group[1:])
    links = Links(send, recv)

    links.count = 34
    seg_in = links.copy(seg, eseg, partner)
    tokens_in = links.copy(tok.at[pl.ds(1024 - EDGE, EDGE)], etok_b, partner)
    spread1 = Spread(mine1, in_o, 0, send, recv, core, chip, at)
    spread2 = Spread(mine2, zo_o, 17, send, recv, core, chip, at)
    spread1.begin()
    seg_in.wait_recv()
    seg_t = seg[...].astype(F32).T
    edge_t = jnp.where(context > 0, eseg[...].astype(F32).T, 0.0)
    edge_col = edge_t[120:128, 7:8]
    start = jnp.where(edge_col[7:8] == seg_t[0:1, 0:1], seg_t[0:1, 0:1], -1.0)
    colm_o[1024:1032] = jnp.zeros((8, 8), F32)
    for b in range(8):
        col = seg_t[:, b : b + 1]
        before = edge_col if b == 0 else seg_t[120:128, b - 1 : b]
        longer = jnp.concatenate([before, col], axis=0)
        entering = start if b == 0 else before[7:8]
        marks = [col]
        for d in range(1, 4):
            marks.append(jnp.where(longer[8 - d : 136 - d] == col, 1.0, 0.0))
        for value in (start, entering, col[127:128]):
            marks.append(jnp.where(col == value, 1.0, 0.0))
        marks.append(jnp.zeros_like(col))
        colm_o[b * Q : b * Q + Q] = jnp.concatenate(marks, axis=1)

    for n in range(7):
        spread1.event(n)
    spread2.begin()
    spread1.collect()
    tokens_in.wait_recv()

    a_neg = -jnp.exp(alog[...])
    causal, _ = triangles()
    lower = as_low(causal)
    gain_row = in_o[:, 768:896].astype(F32).T[8:9]
    gain_o[...] = gain_row

    def normed(block):
        plain = block.astype(F32)
        root = lax.rsqrt(jnp.mean(plain * plain, axis=1, keepdims=True) + EPSILON)
        return (plain * root * gain_row).astype(BF)

    edge_tokens = jnp.where(context > 0, etok_b[...].astype(F32), 0.0)
    edge = mm(normed(edge_tokens), in_o[:, 0:768]).astype(BF)
    xbc_o[0:EDGE] = edge
    xs[0:EDGE] = edge.astype(F32)
    st[...] = jnp.zeros_like(st)
    expand = ex[...]
    dsk_e = mm2(dsk[...], expand)

    def body(b, run):
        r = pl.ds(pl.multiple_of(b * Q, Q), Q)
        rn = pl.ds(pl.multiple_of(b * Q + EDGE, EDGE), Q)
        xn = normed(tok[r])
        xn_o[r] = xn
        both = mm(xn, in_o[...])
        xb = both[:, 0:768].astype(BF)
        xbc_o[rn] = xb
        xs[rn] = xb.astype(F32)
        raw = both[:, 768:776]
        dtr_o[r] = raw
        marks = colm_o[r]
        acts = []
        for c in range(6):
            lanes = slice(c * 128, c * 128 + 128)
            cw, cb, at = (cwx, cbx, lanes) if c < 4 else (cwb, cbb, slice(c * 128 - 512, c * 128 - 384))
            slab = xs[pl.ds(pl.multiple_of(b * Q, Q), Q + EDGE), lanes]
            pre = cb[:, at] + cw[3:4, at] * slab[EDGE:]
            for d in range(1, 4):
                pre = pre + (cw[3 - d : 4 - d, at] * slab[EDGE - d : Q + EDGE - d]) * marks[:, d : d + 1]
            pre_o[r, lanes] = pre
            acts.append(pre * sigmoid(pre))
        b_low = acts[4].astype(BF)
        c_low = acts[5].astype(BF)
        c_s[r] = c_low
        dt = softplus(raw + dtb[...])
        cum = mm3_left(lower, dt * a_neg)
        er_s[r] = jnp.exp(run + cum) * marks[:, 4:5]
        cum_t = cum.T
        last = cum[Q - 1 : Q]
        enter = jnp.exp(cum) * marks[:, 5:6]
        tail = jnp.exp(last - cum) * marks[:, 6:7]
        dt_e = mm2(dt, expand)
        enter_e = mm2(enter, expand)
        tail_e = mm2(tail, expand)
        mask = causal & (marks[:, 0:1] == seg[pl.ds(b, 1), :].astype(F32))
        scores = jnp.where(mask, mm_nt(c_low, b_low), 0.0)
        state = st[...]
        inter = mm(c_low, state.astype(BF))
        pieces = []
        for p in range(4):
            lanes = slice(p * 128, p * 128 + 128)
            xdt = acts[p] * dt_e[:, lanes]
            pieces.append((xdt * tail_e[:, lanes]).astype(BF))
            ws = []
            for h in (2 * p, 2 * p + 1):
                decay = jnp.exp(jnp.minimum(cum[:, h : h + 1] - cum_t[h : h + 1, :], 0.0))
                ws.append((decay * scores).astype(BF))
            intra = mm(jnp.concatenate(ws, axis=1), halves(xdt.astype(BF)))
            y_s[r, lanes] = intra + enter_e[:, lanes] * inter[:, lanes] + dsk_e[:, lanes] * acts[p]
        fresh = mm_tn(b_low, jnp.concatenate(pieces, axis=1))
        st[...] = enter_e[Q - 1 : Q] * state + fresh

        for n in range(7):
            pl.when(b == n)(partial(spread2.event, n))

        return run + last

    lax.fori_loop(0, 8, body, jnp.zeros((1, 8), F32))
    st_low[...] = st[...].astype(BF)
    state_in = links.copy(st_low, st_in, partner)
    spread2.collect()

    def project(b, carry):
        r = pl.ds(pl.multiple_of(b * 256, 256), 256)
        acts[r, 0:512] = mm(xn_o[r], zo_o[:, 0:512])
        dy_o[r] = mm(cot[r], zo_o[:, 512:1024])
        return carry

    lax.fori_loop(0, 4, project, 0)
    state_in.wait_recv()
    st_o[...] = jnp.where(context > 0, st_in[...].astype(F32), 0.0)

    def sums(b, carry):
        r = pl.ds(pl.multiple_of(b * Q, Q), Q)
        y = y_s[r] + mm2(er_s[r], expand) * mm(c_s[r], st_o[...].astype(BF))
        y_s[r] = y
        z = acts[r, 0:512]
        gated = y * (z * sigmoid(z))
        first_sum = jnp.sum(gated * gated, axis=1, keepdims=True)
        second_sum = jnp.sum(dy_o[r] * gg[...] * gated, axis=1, keepdims=True)
        row_s[b] = jnp.concatenate([first_sum, second_sum, jnp.zeros((Q, 6), F32)], axis=1).T
        return carry

    lax.fori_loop(0, 8, sums, 0)
    rows_in = [links.copy(row_s, row_r.at[k - 1], group[k]) for k in range(1, 4)]
    for copy in rows_in:
        copy.wait_recv()
    gate_o[...] = jnp.zeros_like(gate_o)
    st[...] = jnp.zeros_like(st)

    def finish(b, carry):
        r = pl.ds(pl.multiple_of(b * Q, Q), Q)
        total = (row_s[b] + row_r[0, b] + row_r[1, b] + row_r[2, b]).T
        root = lax.rsqrt(total[:, 0:1] * (1.0 / INNER) + EPSILON)
        cross = (root * root * root) * (total[:, 1:2] * (1.0 / INNER))
        er_e = mm2(er_s[r], expand)
        normals, carries = [], []
        for p in range(4):
            lanes = slice(p * 128, p * 128 + 128)
            y = y_s[r, lanes]
            z = acts[r, lanes]
            dn = dy_o[r, lanes]
            sig = sigmoid(z)
            gate = z * sig
            gated = y * gate
            scaled = gated * root
            normals.append((scaled * gg[:, lanes]).astype(BF))
            gate_o[p : p + 1] += jnp.sum(dn * scaled, axis=0, keepdims=True)
            d_gated = root * (dn * gg[:, lanes]) - gated * cross
            d_y = d_gated * gate
            dy_o[r, lanes] = d_y
            dz_o[r, lanes] = (d_gated * y * (sig * (1.0 + z * (1.0 - sig)))).astype(BF)
            carries.append((d_y * er_e[:, lanes]).astype(BF))
        low = jnp.concatenate(normals, axis=1)
        yn_o[r] = low
        branch_o[r] = mm_nt(low, zo_o[:, 512:1024]).astype(BF)
        st[...] += mm_tn(c_s[r], jnp.concatenate(carries, axis=1))
        return carry

    lax.fori_loop(0, 8, finish, 0)
    carry_o[...] = st[...].astype(BF)
    carry_in = links.copy(carry_o, g_in, partner)
    ring = Ring(links, tensor, group)
    ring.reduce_first(branch_o, near, from_d, from_u)
    for m in range(8):
        lanes = slice(m * 128, m * 128 + 128)
        gz_o[m] = mm_tn(xn_o[:, lanes], dz_o[...]).astype(BF).reshape(2, 64, 512)
        go_o[m] = mm_tn(cot[:, lanes], yn_o[...]).astype(BF).reshape(2, 64, 512)
    sib_in = (links.copy(gz_o.at[:, 1 - core], sz, sibling), links.copy(go_o.at[:, 1 - core], so, sibling))
    a_neg = -jnp.exp(alog[...])
    causal, anti = triangles()
    lower = as_low(causal)
    upper = as_low(anti)
    expand = ex[...]
    expand_t = ext[...]
    dsk_e = mm2(dsk[...], expand)

    def head_sum(v):
        return mm2(v, expand_t)

    y_s[0:Q] = st_o[...]

    def forward(b, carry):
        r = pl.ds(pl.multiple_of(b * Q, Q), Q)
        marks = colm_o[r]
        dt = softplus(dtr_o[r] + dtb[...])
        cum = mm3_left(lower, dt * a_neg)
        last = cum[Q - 1 : Q]
        tail = jnp.exp(last - cum) * marks[:, 6:7] * dt
        keep_e = mm2(jnp.exp(last) * marks[Q - 1 : Q, 5:6], expand)
        tail_e = mm2(tail, expand)
        pieces = []
        for c in range(6):
            lanes = slice(c * 128, c * 128 + 128)
            pre = pre_o[r, lanes]
            act = pre * sigmoid(pre)
            acts[r, lanes] = act
            if c < 4:
                pieces.append((act * tail_e[:, lanes]).astype(BF))
            if c == 4:
                b_low = act.astype(BF)
        fresh = mm_tn(b_low, jnp.concatenate(pieces, axis=1))
        y_s[pl.ds(pl.multiple_of(b * Q + Q, Q), Q)] = keep_e * y_s[r] + fresh
        return carry

    lax.fori_loop(0, 7, forward, 0)
    r7 = slice(7 * Q, 8 * Q)
    for c in range(6):
        lanes = slice(c * 128, c * 128 + 128)
        pre = pre_o[r7, lanes]
        acts[r7, lanes] = pre * sigmoid(pre)
    for copy in sib_in:
        copy.wait_recv()

    def merge(c, carry):
        for mine, theirs, at in ((gz_o, sz, 0), (go_o, so, 512)):
            chunk[c, :, at : at + 512] = (mine[c, core].astype(F32) + theirs[c].astype(F32)).astype(BF)
        return carry

    lax.fori_loop(0, 8, merge, 0)
    grads_in = [links.copy(chunk.at[chips[k]], rg.at[k - 1], others[k]) for k in range(1, 8)]
    carry_in.wait_recv()
    grad[...] = jnp.where(context == 0, g_in[...].astype(F32), 0.0)
    heads[...] = jnp.zeros_like(heads)
    xs[0:8] = jnp.zeros((8, 768), F32)
    xs[1032:1040] = jnp.zeros((8, 768), F32)

    def backward(i, carry):
        b = 7 - i
        r = pl.ds(pl.multiple_of(b * Q, Q), Q)
        rp = pl.ds(pl.multiple_of(b * Q + 8, 8), Q)
        marks = colm_o[r]
        raw = dtr_o[r] + dtb[...]
        dt = softplus(raw)
        cum = mm3_left(lower, dt * a_neg)
        cum_t = cum.T
        last = cum[Q - 1 : Q]
        enter = jnp.exp(cum) * marks[:, 5:6]
        tail = jnp.exp(last - cum) * marks[:, 6:7]
        dt_e = mm2(dt, expand)
        enter_e = mm2(enter, expand)
        tail_e = mm2(tail, expand)
        keep_e = enter_e[Q - 1 : Q]
        b_low = acts[r, 512:640].astype(BF)
        c_low = acts[r, 640:768].astype(BF)
        state = y_s[r]
        state_low = state.astype(BF)
        g_now = grad[...]
        g_low = g_now.astype(BF)
        inter = mm(c_low, state_low)
        back = mm(b_low, g_low)
        mask = causal & (marks[:, 0:1] == seg[pl.ds(b, 1), :].astype(F32))
        scores = jnp.where(mask, mm_nt(c_low, b_low), 0.0)
        kept = jnp.sum(state * g_now, axis=0, keepdims=True) * keep_e
        entered, tailed, e_terms, q_terms, x_terms, k_terms = [], [], [], [], [], []
        rows, cols = [], []
        d_scores = jnp.zeros((Q, Q), F32)
        for p in range(4):
            lanes = slice(p * 128, p * 128 + 128)
            x = acts[r, lanes]
            dys = dy_o[r, lanes]
            xdt = x * dt_e[:, lanes]
            xdt_low = xdt.astype(BF)
            ed = enter_e[:, lanes] * dys
            tx = tail_e[:, lanes] * xdt
            entered.append(ed.astype(BF))
            tailed.append(tx.astype(BF))
            dy_two = halves(dys.astype(BF))
            dw_two = mm_nt(dy_two, xdt_low)
            ws = []
            for k in range(2):
                h = 2 * p + k
                decay = jnp.exp(jnp.minimum(cum[:, h : h + 1] - cum_t[h : h + 1, :], 0.0))
                weight = decay * scores
                dw = dw_two[k * Q : k * Q + Q]
                d_scores = d_scores + decay * dw
                both = weight * dw
                rows.append(jnp.sum(both, axis=1, keepdims=True))
                cols.append(jnp.sum(both, axis=0, keepdims=True))
                ws.append(weight.astype(BF))
            dxdt = mm_tn(jnp.concatenate(ws, axis=0), dy_two) + tail_e[:, lanes] * back[:, lanes]
            e_terms.append(ed * inter[:, lanes] - tx * back[:, lanes])
            q_terms.append(jnp.sum(tx * back[:, lanes], axis=0, keepdims=True) + kept[:, lanes])
            x_terms.append(dxdt * x)
            k_terms.append(jnp.sum(dys * x, axis=0, keepdims=True))
            pre = pre_o[r, lanes]
            sig = sigmoid(pre)
            xs[rp, lanes] = (dxdt * dt_e[:, lanes] + dsk_e[:, lanes] * dys) * (sig * (1.0 + pre * (1.0 - sig)))
        entered = jnp.concatenate(entered, axis=1)
        tailed = jnp.concatenate(tailed, axis=1)
        ds_low = jnp.where(mask, d_scores, 0.0).astype(BF)
        d_c = mm_nt(entered, state_low) + mm(ds_low, b_low)
        d_b = mm_nt(tailed, g_low) + mm_tn(ds_low, c_low)
        grad[...] = keep_e * g_now + mm_tn(c_low, entered)
        for c, value in ((4, d_b), (5, d_c)):
            lanes = slice(c * 128, c * 128 + 128)
            pre = pre_o[r, lanes]
            sig = sigmoid(pre)
            xs[rp, lanes] = value * (sig * (1.0 + pre * (1.0 - sig)))
        d_cum = jnp.concatenate(rows, axis=1) - jnp.concatenate(cols, axis=0).T
        d_cum = d_cum + head_sum(jnp.concatenate(e_terms, axis=1))
        d_log = mm3_left(upper, d_cum) + head_sum(jnp.concatenate(q_terms, axis=1))
        d_dt = d_log * a_neg + head_sum(jnp.concatenate(x_terms, axis=1))
        d_raw = d_dt * sigmoid(raw)
        ddt_o[r] = jnp.concatenate([d_raw, jnp.zeros((Q, 120), F32)], axis=1).astype(BF)
        heads[0:1] += jnp.sum(d_raw, axis=0, keepdims=True)
        heads[1:2] += jnp.sum(d_log * dt, axis=0, keepdims=True) * a_neg
        heads[2:3] += head_sum(jnp.concatenate(k_terms, axis=1))
        return carry

    lax.fori_loop(0, 1, backward, 0)
    ring.reduce_second(branch_o, near, relay, from_d, from_u)
    lax.fori_loop(1, 4, backward, 0)
    ring.reduce_wait()

    def finish_out(i, carry):
        r = pl.ds(pl.multiple_of(i * 64, 64), 64)
        rt = pl.ds(pl.multiple_of(tensor * 256 + i * 64, 64), 64)
        total = branch_o[rt].astype(F32) + from_d[r].astype(F32) + from_u[r].astype(F32)
        out_o[rt] = (tok[rt].astype(F32) + total).astype(BF)
        return carry

    lax.fori_loop(0, 4, finish_out, 0)
    ring.gather_first(out_o)
    lax.fori_loop(4, 8, backward, 0)
    small_o[...] = jnp.zeros_like(small_o)
    small_o[24:32, 0:8] = heads[...]

    for c in range(6):
        lanes = slice(c * 128, c * 128 + 128)
        first = xs[0:16, lanes]
        cw, wl = (cwx, lanes) if c < 4 else (cwb, slice(c * 128 - 512, c * 128 - 384))
        flags = jnp.concatenate([jnp.zeros((8, 8), F32), colm_o[0:8]], axis=0)
        total = jnp.zeros((8, 128), F32)
        for d in range(1, 4):
            total = total + cw[3 - d : 4 - d, wl] * (first * flags[:, d : d + 1])[d : d + 8]
        ret_s[:, lanes] = total
    ret_in = links.copy(ret_s, ret_r, partner)
    ring.gather_second(out_o)
    for copy in grads_in:
        copy.wait_recv()
    for at in range(0, 1024, 128):
        lanes = slice(at, at + 128)
        cs[:, lanes] = add_slots(chunk[chip, :, lanes].astype(F32), rg, lanes).astype(BF)
    grads_ctx = links.copy(cs, cr, partner)
    for c in range(6):
        lanes = slice(c * 128, c * 128 + 128)
        cw, wl = (cwx, lanes) if c < 4 else (cwb, slice(c * 128 - 512, c * 128 - 384))

        def conv(b, sums, lanes=lanes, c=c, cw=cw, wl=wl):
            r = pl.ds(pl.multiple_of(b * Q, Q), Q)
            slab = xs[pl.ds(pl.multiple_of(b * Q + 8, 8), Q + 8), lanes]
            marks = colm_o[pl.ds(pl.multiple_of(b * Q, Q), Q + 8)]
            xin = xbc_o[pl.ds(pl.multiple_of(b * Q, Q), Q + EDGE), lanes].astype(F32)
            main = slab[0:Q]
            out = cw[3:4, wl] * main
            new = [sums[0] + jnp.sum(main, axis=0, keepdims=True),
                   sums[1] + jnp.sum(main * xin[EDGE:], axis=0, keepdims=True)]
            for d in range(1, 4):
                masked = slab * marks[:, d : d + 1]
                out = out + cw[3 - d : 4 - d, wl] * masked[d : d + Q]
                new.append(sums[d + 1] + jnp.sum(masked[0:Q] * xin[EDGE - d : Q + EDGE - d], axis=0, keepdims=True))
            if c < 4:
                dx_o[r, lanes] = out.astype(BF)
            else:
                dbc_o[r, slice(c * 128 - 512, c * 128 - 384)] = out.astype(BF)

            @pl.when(b == 7)
            def _():
                tail_r[:, lanes] = out[Q - EDGE :]

            return tuple(new)

        zero = jnp.zeros((1, 128), F32)
        sums = lax.fori_loop(0, 8, conv, (zero,) * 5)
        at = 16 + c if c < 4 else 36 + c
        small_o[at : at + 1] = sums[0]
        for d in range(4):
            at = (3 - d) * 4 + c if c < 4 else 28 + (3 - d) * 2 + c
            small_o[at : at + 1] = sums[d + 1]
    ret_in.wait_recv()
    returned = jnp.where(context == 0, ret_r[...], 0.0)
    last = tail_r[...] + jnp.concatenate([jnp.zeros((EDGE - 8, 768), F32), returned], axis=0)
    dx_o[1024 - EDGE : 1024] = last[:, 0:512].astype(BF)
    dbc_o[1024 - EDGE : 1024] = last[:, 512:768].astype(BF)
    grads_ctx.wait_recv()
    oz[...] = cs[:, 0:512].astype(F32) + cr[:, 0:512].astype(F32)
    oo[...] = cs[:, 512:1024].astype(F32) + cr[:, 512:1024].astype(F32)
    for made in ring.first + ring.alone:
        made.wait_send()
        links.started = [other for other in links.started if other is not made]
    sm[...] = small_o[...]
    sm[20:24] = gate_o[...]
    wide = Ring(links, tensor, group)

    def make(r):
        total = mm_nt(dz_o[r], zo_o[:, 0:512]) + mm_nt(dx_o[r], in_o[:, 0:512]) + mm_nt(ddt_o[r], in_o[:, 768:896]) + mm_nt(dbc_o[r], in_o[:, 512:768])
        branch_o[r] = total.astype(BF)

    wide.reduce_first(branch_o, near2, from_d2, from_u2, make)
    small_in = links.copy(sm, sm_s, sibling)

    def outer(m):
        block = xn_o[:, m * 128 : m * 128 + 128]
        gx[m, :, :, 0:512] = mm_tn(block, dx_o[...]).astype(BF).reshape(2, 64, 512)
        gx[m, :, :, 512:640] = mm_tn(block, ddt_o[...]).astype(BF).reshape(2, 64, 128)
        gx[m, :, :, 640:896] = mm_tn(block, dbc_o[...]).astype(BF).reshape(2, 64, 256)

    make(wide.half(wide.t_up, 0))
    make(wide.half(wide.t_down, 1))
    for m in range(4):
        outer(m)
    wide.reduce_second(branch_o, near2, relay2, from_d2, from_u2)
    for m in range(4, 8):
        outer(m)
    sib_in = links.copy(gx.at[:, 1 - core], sx, sibling)
    small_in.wait_recv()
    sm_c[chip] = sm[...] + sm_s[...]
    small_base = links.count - 1
    for k in range(1, 8):
        links.copy(sm_c.at[chip], sm_c.at[chip], others[k])
    make(wide.half(tensor, 0))
    make(wide.half(tensor, 1))
    sib_in.wait_recv()

    def merge(c, carry):
        chunk2[c] = (gx[c, core].astype(F32) + sx[c].astype(F32)).astype(BF)
        return carry

    lax.fori_loop(0, 8, merge, 0)
    grads_in = [links.copy(chunk2.at[chips[k]], rg2.at[k - 1], others[k]) for k in range(1, 8)]

    wide.reduce_wait()

    def inner(i, g_norm):
        r = pl.ds(pl.multiple_of(i * 64, 64), 64)
        rt = pl.ds(pl.multiple_of(tensor * 256 + i * 64, 64), 64)
        total = branch_o[rt].astype(F32) + from_d2[r].astype(F32) + from_u2[r].astype(F32)
        plain = tok[rt].astype(F32)
        root = lax.rsqrt(jnp.mean(plain * plain, axis=1, keepdims=True) + EPSILON)
        stat = plain * root
        d_plain = total * gain_o[...]
        mean = jnp.mean(d_plain * plain, axis=1, keepdims=True)
        dtok_o[rt] = (cot[rt].astype(F32) + root * d_plain - stat * (root * root) * mean).astype(BF)
        return g_norm + jnp.sum(total * stat, axis=0, keepdims=True)

    g_norm = lax.fori_loop(0, 4, inner, jnp.zeros((1, 1024), F32))
    wide.gather_first(dtok_o)
    for c in range(8):
        nm[c : c + 1] = g_norm[:, c * 128 : c * 128 + 128]
    norm_sib = links.copy(nm, nm_s, sibling)

    for k in range(1, 8):
        source = lax.rem(chip + 8 - k, 8)
        arrival(None, sm_c.at[source], recv.at[small_base + k], others[k]).wait_recv()
    total = sm_c[0]
    for c in range(1, 8):
        total = total + sm_c[c]
    sm_x[...] = total
    small_ctx = links.copy(sm_x, sm_r, partner)
    norm_sib.wait_recv()
    nm_c[chip] = nm[...] + nm_s[...]
    norm_base = links.count - 1
    for k in range(1, 8):
        links.copy(nm_c.at[chip], nm_c.at[chip], others[k])
    for copy in grads_in:
        copy.wait_recv()
    for col in range(0, 896, 128):
        lanes = slice(col, col + 128)
        cs2[:, lanes] = add_slots(chunk2[chip, :, lanes].astype(F32), rg2, lanes).astype(BF)
    grads_ctx = links.copy(cs2, cr2, partner)
    wide.gather_second(dtok_o)
    for k in range(1, 8):
        source = lax.rem(chip + 8 - k, 8)
        arrival(None, nm_c.at[source], recv.at[norm_base + k], others[k]).wait_recv()
    total = nm_c[0]
    for c in range(1, 8):
        total = total + nm_c[c]
    nm_x[...] = total
    norm_ctx = links.copy(nm_x, nm_r, partner)
    small_ctx.wait_recv()
    sums = sm_x[...] + sm_r[...]
    for k in range(4):
        for p in range(4):
            conv_o[k : k + 1, p * 128 : p * 128 + 128] = sums[k * 4 + p : k * 4 + p + 1]
    for p in range(4):
        convb_o[:, p * 128 : p * 128 + 128] = sums[16 + p : 17 + p]
        ggate_o[:, p * 128 : p * 128 + 128] = sums[20 + p : 21 + p]
    dtb_o[...] = sums[24:25, 0:8]
    alog_o[...] = sums[25:26, 0:8]
    dsk_o[...] = sums[26:27, 0:8]
    sm_t[tensor] = sums[32:48]
    small_t = links.count
    for k in range(1, 4):
        links.copy(sm_t.at[tensor], sm_t.at[tensor], group[k])
    norm_ctx.wait_recv()
    nm_t[tensor] = nm_x[...] + nm_r[...]
    norm_t = links.count
    for k in range(1, 4):
        links.copy(nm_t.at[tensor], nm_t.at[tensor], group[k])
    grads_ctx.wait_recv()
    ox[...] = cs2[:, 0:512].astype(F32) + cr2[:, 0:512].astype(F32)
    t2[tensor] = cs2[:, 640:896].astype(F32) + cr2[:, 640:896].astype(F32)
    grads2_t = links.count
    for k in range(1, 4):
        links.copy(t2.at[tensor], t2.at[tensor], group[k])
    odt[...] = (cs2[:, 512:640].astype(F32) + cr2[:, 512:640].astype(F32))[:, 0:8]
    for k in range(1, 4):
        source = lax.rem(tensor + 4 - k, 4)
        arrival(None, sm_t.at[source], recv.at[small_t + k - 1], group[k]).wait_recv()
        arrival(None, nm_t.at[source], recv.at[norm_t + k - 1], group[k]).wait_recv()
        arrival(None, t2.at[source], recv.at[grads2_t + k - 1], group[k]).wait_recv()
    sums = (sm_t[0] + sm_t[1]) + (sm_t[2] + sm_t[3])
    for k in range(4):
        for p in range(2):
            bc_o[k : k + 1, p * 128 : p * 128 + 128] = sums[k * 2 + p : k * 2 + p + 1]
    for p in range(2):
        bcb_o[:, p * 128 : p * 128 + 128] = sums[8 + p : 9 + p]
    obc[...] = (t2[0] + t2[1]) + (t2[2] + t2[3])
    nm_s[...] = (nm_t[0] + nm_t[1]) + (nm_t[2] + nm_t[3])
    row = nm_s[pl.ds(chip, 1), :]
    onorm[...] = jnp.where(core == 0, row[:, 0:64], row[:, 64:128])
    wide.gather_wait(dtok_o)
    ring.gather_wait(out_o)
    links.finish()
    spread1.sent()
    spread2.sent()


def call(kernel, out_shapes, scratch, *args, specs=None, collective_id=None):
    return pl.pallas_call(
        kernel,
        out_shape=[jax.ShapeDtypeStruct(s, d) for s, d in out_shapes],
        in_specs=[pl.BlockSpec(memory_space=pl.ANY if n in (specs or ()) else pltpu.VMEM) for n in range(len(args))],
        out_specs=[pl.BlockSpec(memory_space=pltpu.VMEM)] * len(out_shapes),
        scratch_shapes=[pltpu.SemaphoreType.DMA(s) if d is None else pltpu.VMEM(s, d) for s, d in scratch],
        compiler_params=pltpu.CompilerParams(vmem_limit_bytes=VMEM_LIMIT, collective_id=collective_id, has_side_effects=collective_id is not None
        ),
    )(*args)


def local(
    tokens,
    segment,
    norm_gain,
    w_z,
    w_x,
    w_dt,
    w_bc,
    conv_x,
    conv_xb,
    conv_bc,
    conv_bcb,
    dt_bias,
    a_log,
    d_skip,
    gate_gain,
    w_out,
    cotangent,
):
    length = tokens.shape[0]
    head_count = dt_bias.shape[0]
    inner_width = head_count * HEADDIM
    bc_width = 2 * STATE
    seg = segment.reshape(8, 128)
    expand_np = np.kron(np.eye(8), np.ones((1, HEADDIM)))
    expand = jnp.asarray(expand_np, BF)
    expand_t = jnp.asarray(expand_np.T, BF)
    wide = (length, inner_width)
    state = (STATE, inner_width)
    grid = (8, 2, 64, 512)
    heads = (dt_bias[None], a_log[None], d_skip[None])
    own = (64, 512)
    half = ((2, 128, 1024), BF)
    rows = ((256, 1024), BF)

    def vector(shape, last):
        return [(s, F32) for s in (shape, shape, (8,) + shape, shape, shape, last)]

    (output, o_z, o_out, d_tokens, o_x, o_dt, o_bc, o_norm, conv_o, convb_o, cbc_o, cbcb_o, gate_o, dtb_o, alog_o, dsk_o) = call(
        main_kernel,
        [((length, 1024), BF), (own, F32), (own, F32), ((length, 1024), BF), (own, F32), ((64, 8), F32), ((64, 256), F32), ((1, 64), F32),
         ((4, 512), F32), ((1, 512), F32), ((4, 256), F32), ((1, 256), F32), ((1, 512), F32), ((1, 8), F32), ((1, 8), F32), ((1, 8), F32)],
        [((1024, 896), BF), ((1024, 1024), BF), ((length, 1024), BF), ((1, 1024), F32), (wide, BF), ((4, 128), F32),
         (wide, BF), ((length, 2 * STATE), BF), ((length, 128), BF), ((48, 128), F32),
         ((64, 896), BF), ((64, 1024), BF), ((EDGE, 1024), BF), ((8, 128), jnp.int32), ((length + EDGE, 768), F32), (state, F32), (state, BF), (state, BF),
         (wide, F32), ((length, 8), F32), ((length, STATE), BF), ((8, 8, 128), F32), ((3, 8, 8, 128), F32), (wide, BF),
         ((length + EDGE, 768), BF), ((length, 768), F32), ((length, 8), F32), ((length + 8, 8), F32), (state, F32), (wide, F32),
         ((length, 1024), BF), (state, BF), (grid, BF), (grid, BF),
         ((length, 768), F32), (state, F32), ((8, 8), F32),
         (state, BF), ((EDGE, 768), F32), ((8, 768), F32), ((8, 768), F32), half, half, rows, rows,
         ((8, 64, 512), BF), ((8, 64, 512), BF), ((8, 64, 1024), BF), ((7, 64, 1024), BF), ((64, 1024), BF), ((64, 1024), BF),
         ((8, 2, 64, 896), BF), half, half, rows, rows,
         ((8, 64, 896), BF), ((8, 64, 896), BF), ((7, 64, 896), BF), ((64, 896), BF), ((64, 896), BF), ((4, 64, 256), F32),
         *vector((48, 128), (4, 16, 128)), *vector((8, 128), (4, 8, 128)),
         ((120,), None), ((120,), None)],
        w_z, w_x, w_bc, w_dt, norm_gain[None], w_out, tokens, cotangent, seg,
        conv_x, conv_bc, conv_xb[None], conv_bcb[None], *heads, gate_gain[None], expand, expand_t,
        collective_id=1,
    )
    return (
        output, d_tokens, o_norm[0], o_z, o_x, o_dt, o_bc, conv_o, convb_o[0], cbc_o, cbcb_o[0],
        dtb_o[0], alog_o[0], dsk_o[0], gate_o[0], o_out,
    )


def solution(mesh):
    in_specs = (
        P(("shard", "context"), None),
        P(("shard", "context")),
        P("shard"),
        P("shard", "tensor"),
        P("shard", "tensor"),
        P("shard", "tensor"),
        P("shard", None),
        P(None, "tensor"),
        P("tensor"),
        P(),
        P(),
        P("tensor"),
        P("tensor"),
        P("tensor"),
        P("tensor"),
        P("shard", "tensor"),
        P(("shard", "context"), None),
    )
    out_specs = (
        P(("shard", "context"), None),
        P(("shard", "context"), None),
        P("shard"),
        P("shard", "tensor"),
        P("shard", "tensor"),
        P("shard", "tensor"),
        P("shard", None),
        P(None, "tensor"),
        P("tensor"),
        P(),
        P(),
        P("tensor"),
        P("tensor"),
        P("tensor"),
        P("tensor"),
        P("shard", "tensor"),
    )
    return jax.shard_map(local, mesh=mesh, in_specs=in_specs, out_specs=out_specs, check_vma=False)
```
